128 devices in a mesh: batch: 16 (over x, y_lo, core), aug: 8 (over y_hi, z).
Axes of the slice: x: 4, y: 4 (y_hi: 2, y_lo: 2; y = y_hi * 2 + y_lo), z: 4, core: 2. Of those that a mesh axis runs over, the one named last changes fastest.
Arguments:
- student_image: bfloat16 [8, 4608, 512], P('aug', 'batch'), may hold values from -8 to 8
- student_text: bfloat16 [4608, 512], P('batch'), may hold values from -8 to 8
- teacher_image: bfloat16 [8, 4608, 1280], P('aug', 'batch'), may hold values from -8 to 8
- teacher_text: bfloat16 [4608, 1280], P('batch'), may hold values from -8 to 8
Outputs:
- loss: float32 [], replicated
- grad_image: float32 [8, 4608, 512], P('aug', 'batch')
- grad_text: float32 [4608, 512], P('batch')
The draws below stay inside these ranges and needn't reach their ends.
All inputs are finite; a program needn't handle non-finite values.
Results may differ from the reference program's by a relative error of at most 0.0011.
The reference program's roundings to bfloat16 on the way (of `target_weights` and `weights`) count: a program that leaves them out, or rounds other values in their place, can miss the bound.
Values may be sent and summed in bfloat16 or wider, within the bound.
A program may use at most 128 MiB of HBM per device.

```python
import math
import jax
import jax.numpy as jnp

SW = 512
TW = 1280
PAIRS = 4608
VIEWS = 8


def draw_student_image(key, part):
    key = jax.random.fold_in(key, 1)
    values = jnp.clip(jax.random.normal(key, (VIEWS, PAIRS, SW), jnp.float32), -4.0, 4.0)
    return values.astype(jnp.bfloat16)


def draw_student_text(key, part):
    key = jax.random.fold_in(key, 2)
    values = jnp.clip(jax.random.normal(key, (PAIRS, SW), jnp.float32), -4.0, 4.0)
    return values.astype(jnp.bfloat16)


def draw_teacher_image(key, part):
    key = jax.random.fold_in(key, 3)
    values = jnp.clip(jax.random.normal(key, (VIEWS, PAIRS, TW), jnp.float32), -4.0, 4.0)
    return values.astype(jnp.bfloat16)


def draw_teacher_text(key, part):
    key = jax.random.fold_in(key, 4)
    values = jnp.clip(jax.random.normal(key, (PAIRS, TW), jnp.float32), -4.0, 4.0)
    return values.astype(jnp.bfloat16)


def setup_inputs(seed: int = 0) -> dict:
    key_list = jax.random.split(jax.random.key(seed), 5)
    student_image = draw_student_image(jax.random.fold_in(key_list[4], 71), 0)
    student_text = draw_student_text(jax.random.fold_in(key_list[4], 71), 0)
    teacher_image = draw_teacher_image(jax.random.fold_in(key_list[4], 71), 0)
    teacher_text = draw_teacher_text(jax.random.fold_in(key_list[4], 71), 0)
    return {"student_image": student_image, "student_text": student_text, "teacher_image": teacher_image, "teacher_text": teacher_text}


def reference(student_image, student_text, teacher_image, teacher_text):
    views = student_image.shape[0]
    pairs = student_text.shape[0]
    student_scale = 3.0 / math.sqrt(student_text.shape[1])
    teacher_scale = 3.0 / math.sqrt(teacher_text.shape[1])
    targets = jnp.zeros((pairs, pairs), jnp.float32)
    for view in range(views):
        teacher_logits = jnp.dot(teacher_image[view], teacher_text.T, preferred_element_type=jnp.float32) * teacher_scale
        row_part = jnp.exp(teacher_logits - jax.nn.logsumexp(teacher_logits, axis=1, keepdims=True))
        col_part = jnp.exp(teacher_logits - jax.nn.logsumexp(teacher_logits, axis=0, keepdims=True))
        targets = targets + row_part + col_part
    target_weights = (targets / views).astype(jnp.bfloat16)
    target_text = jnp.dot(target_weights, student_text, preferred_element_type=jnp.float32)
    loss_sum = jnp.zeros((), jnp.float32)
    grad_text = jnp.zeros(student_text.shape, jnp.float32)
    image_grads = []
    for view in range(views):
        student_logits = jnp.dot(student_image[view], student_text.T, preferred_element_type=jnp.float32) * student_scale
        row_lse = jax.nn.logsumexp(student_logits, axis=1, keepdims=True)
        col_lse = jax.nn.logsumexp(student_logits, axis=0, keepdims=True)
        loss_sum = loss_sum - jnp.sum(target_weights.astype(jnp.float32) * student_logits) + jnp.sum(row_lse) + jnp.sum(col_lse)
        weights = (jnp.exp(student_logits - row_lse) + jnp.exp(student_logits - col_lse)).astype(jnp.bfloat16)
        image_grads.append((jnp.dot(weights, student_text, preferred_element_type=jnp.float32) - target_text) * student_scale)
        grad_text = grad_text + jnp.dot(weights.T, student_image[view], preferred_element_type=jnp.float32)
        grad_text = grad_text - jnp.dot(target_weights.T, student_image[view], preferred_element_type=jnp.float32)
    grad_text = grad_text * student_scale
    loss = loss_sum / (2.0 * views * pairs)
    return (loss, jnp.stack(image_grads, axis=0), grad_text)
```

```python
import functools
import math

import jax
import jax.numpy as jnp
from jax import lax
from jax.experimental import pallas as pl
from jax.experimental.pallas import tpu as pltpu
from jax.sharding import PartitionSpec as P

MESH = pl.DeviceIdType.MESH
F32 = jnp.float32
BF16 = jnp.bfloat16
ROWS = 288
HALF = ROWS // 2
CH = 384
NCH = 3
NT = (((1,), (1,)), ((), ()))
NN = (((1,), (0,)), ((), ()))
TN = (((0,), (0,)), ((), ()))


def dot(a, b, dims):
    return lax.dot_general(a, b, dims, preferred_element_type=F32)


def kernel(
    simg, stext, timg, ttext,
    loss_out, gi_out, gt_out,
    it, is_, tt, ts, pt, qt, ps, qs, w, tgt, tgt_in, tw,
    gsend, grecv, gtp, gt_sib, rs_buf, fb_src, fb_buf, gtc,
    rowst, rowsend, rowrecv, rowfac, rowtmp, colst, colrecv, colfac, collse,
    loss_src, loss_b, loss_src2, loss_a,
    zi_s, zi_r, t1_s, t1_r, t2_s, t2_r, t3_s, t3_r,
    row_s, row_r, col_s, col_r, tgt_s, tgt_r, g_s, g_r, gc_s, gc_r,
    rs_s, rs_r, fb_s, fb_r, lb_s, lb_r, la_s, la_r,
):
    b = lax.axis_index("batch")
    a = lax.axis_index("aug")
    x, j = b // 4, b % 4
    yl, k = j // 2, j % 2
    yh, z = a // 4, a % 4
    sib = (b + 1 - 2 * k, a)
    teacher_scale = 3.0 / math.sqrt(timg.shape[1])
    student_scale = 3.0 / math.sqrt(simg.shape[1])

    def dev(x_, j_, yh_, z_):
        return (x_ * 4 + j_, yh_ * 4 + z_)

    def znext(d):
        return (b, yh * 4 + lax.rem(z + d, 4))

    def copy(src, dst, ss, rs, to):
        return pltpu.make_async_remote_copy(
            src_ref=src, dst_ref=dst, send_sem=ss, recv_sem=rs, device_id=to, device_id_type=MESH
        )

    barrier = pltpu.get_barrier_semaphore()

    def greet_plane(d, _):
        i = lax.rem(b * 2 + yh + d, 32)
        pl.semaphore_signal(barrier, 1, device_id=(i // 2, (i % 2) * 4 + z), device_id_type=MESH)
        return 0

    lax.fori_loop(1, 32, greet_plane, 0)

    def greet_line(d, _):
        dz, i = d // 8 + 1, d % 8
        pl.semaphore_signal(
            barrier, 1, device_id=dev(x, i // 2, i % 2, lax.rem(z + dz, 4)), device_id_type=MESH
        )
        return 0

    lax.fori_loop(0, 24, greet_line, 0)
    pl.semaphore_wait(barrier, 55)

    zm1, zp1, zp2 = lax.rem(z + 3, 4), lax.rem(z + 1, 4), lax.rem(z + 2, 4)
    own = (timg, simg)
    imgs = (it, is_)
    texts = (tt, ts)
    own_text = (ttext, stext)

    def half(h):
        return pl.ds(h * HALF, HALF)

    def img_send(m, d, h):
        return copy(
            own[m].at[half(h)], imgs[m].at[z, half(h)], zi_s.at[m, d, h], zi_r.at[m, d, h],
            znext(1 if d == 0 else 3),
        )

    def img_relay(m, d):
        slot = zm1 if d == 0 else zp1
        ref = imgs[m].at[slot, half(d)]
        return copy(ref, ref, zi_s.at[m, 2, d], zi_r.at[m, 2, d], znext(1 if d == 0 else 3))

    def img_recv(m, d, h):
        slot = zm1 if d == 0 else zp1
        ref = imgs[m].at[slot, half(h)]
        copy(ref, ref, zi_s.at[m, d, h], zi_r.at[m, d, h], znext(1)).wait_recv()

    def img_recv_far(m, d):
        ref = imgs[m].at[zp2, half(d)]
        copy(ref, ref, zi_s.at[m, 2, d], zi_r.at[m, 2, d], znext(1)).wait_recv()

    def img_start(m):
        img_send(m, 0, 0).start()
        img_send(m, 1, 1).start()
        img_send(m, 0, 1).start()
        img_send(m, 1, 0).start()

    def img_pass_on(m):
        img_recv(m, 0, 0)
        img_relay(m, 0).start()
        img_recv(m, 1, 1)
        img_relay(m, 1).start()

    syl, sk = z // 2, z % 2
    is_source = j == z

    def tslab(m, blk, h):
        return texts[m].at[pl.ds(blk * ROWS + h * HALF, HALF)]

    def text_first(m):
        return (
            copy(own_text[m].at[pl.ds((1 - sk) * HALF, HALF)], tslab(m, x, 1 - sk),
                 t1_s.at[m, 0], t1_r.at[m], dev(x, syl * 2 + 1 - sk, yh, z)),
            copy(own_text[m].at[half(0)], tslab(m, x, 0),
                 t1_s.at[m, 1], t1_r.at[m], dev(x, (1 - syl) * 2, yh, z)),
            copy(own_text[m].at[half(1)], tslab(m, x, 1),
                 t1_s.at[m, 2], t1_r.at[m], dev(x, (1 - syl) * 2 + 1, yh, z)),
        )

    def text_start(m):
        @pl.when(is_source)
        def _():
            for c in text_first(m):
                c.start()
            tslab(m, x, k)[...] = own_text[m][pl.ds(k * HALF, HALF)]

    def text_x(m, d):
        return copy(tslab(m, x, k), tslab(m, x, k), t2_s.at[m, d - 1], t2_r.at[m, d - 1],
                    (lax.rem(x + d, 4) * 4 + j, a))

    def text_sib(m, d):
        blk = lax.rem(x + 4 - d, 4)
        return copy(tslab(m, blk, k), tslab(m, blk, k), t3_s.at[m, d], t3_r.at[m, d], sib)

    def text_spread(m):
        @pl.when(jnp.logical_not(is_source))
        def _():
            copy(tslab(m, x, k), tslab(m, x, k), t1_s.at[m, 0], t1_r.at[m], sib).wait_recv()

        for d in (1, 3, 2):
            text_x(m, d).start()
        text_sib(m, 0).start()

    def text_share(m):
        for d in (1, 3, 2):
            blk = lax.rem(x + 4 - d, 4)
            copy(tslab(m, blk, k), tslab(m, blk, k), t2_s.at[m, d - 1], t2_r.at[m, d - 1],
                 sib).wait_recv()
            text_sib(m, d).start()

    def text_wait(m):
        for d in range(4):
            blk = lax.rem(x + 4 - d, 4)
            copy(tslab(m, blk, 1 - k), tslab(m, blk, 1 - k), t3_s.at[m, d], t3_r.at[m, d],
                 sib).wait_recv()

    lane = lax.broadcasted_iota(jnp.int32, (ROWS, 128), 1)

    def scores(m, v, pr, qr, scale):
        def first(n, top):
            t = dot(imgs[m][v], texts[m][pl.ds(n * CH, CH), :], NT) * scale
            cm = jnp.max(t, axis=0, keepdims=True)
            q = jnp.exp(t - cm)
            pr[v, n] = t
            qr[v, n] = q
            colst[m, n, pl.ds(v, 1), :] = cm
            colst[m, n, pl.ds(v + 4, 1), :] = jnp.sum(q, axis=0, keepdims=True)
            return jnp.maximum(
                top, jnp.maximum(jnp.maximum(t[:, :128], t[:, 128:256]), t[:, 256:])
            )

        top = lax.fori_loop(0, NCH, first, jnp.full((ROWS, 128), -jnp.inf, F32))
        top = jnp.max(top, axis=1, keepdims=True)

        def second(n, total):
            p = jnp.exp(pr[v, n] - top)
            pr[v, n] = p
            return total + (p[:, :128] + p[:, 128:256] + p[:, 256:])

        total = lax.fori_loop(0, NCH, second, jnp.zeros((ROWS, 128), F32))
        total = jnp.sum(total, axis=1, keepdims=True)
        rowst[:ROWS, :] = jnp.where(
            lane == v, top, jnp.where(lane == v + 4, total, rowst[:ROWS, :])
        )

    def row_copy(m, d):
        return copy(rowsend.at[m], rowrecv.at[m, d - 1], row_s.at[m, d - 1], row_r.at[m, d - 1],
                    znext(d))

    def col_copy(m, d):
        return copy(colst.at[m], colrecv.at[m, d - 1], col_s.at[m, d - 1], col_r.at[m, d - 1],
                    (lax.rem(b + d, 16), a))

    def stats_start(m):
        def go(d, _):
            col_copy(m, d).start()
            return 0

        lax.fori_loop(1, 16, go, 0)
        rowsend[m] = jnp.transpose(rowst[...])[:8]
        for d in (1, 3, 2):
            row_copy(m, d).start()

    def stats_finish(m):
        for d in (1, 3, 2):
            row_copy(m, d).wait_recv()
        mine = rowsend[m]
        top = mine[:4]
        for d in range(3):
            top = jnp.maximum(top, rowrecv[m, d, :4])
        total = mine[4:] * jnp.exp(mine[:4] - top)
        for d in range(3):
            got = rowrecv[m, d]
            total = total + got[4:] * jnp.exp(got[:4] - top)
        row_lse = top + jnp.log(total)
        rowtmp[0:4, :] = jnp.exp(mine[:4] - row_lse)
        rowfac[...] = jnp.transpose(rowtmp[...])

        def arrived(d, _):
            col_copy(m, d).wait_recv()
            return 0

        lax.fori_loop(1, 16, arrived, 0)
        cmine = colst[m]

        def highest(d, t):
            return jnp.maximum(t, colrecv[m, d, :, :4, :])

        ctop = lax.fori_loop(0, 15, highest, cmine[:, :4, :])

        def add(d, t):
            got = colrecv[m, d]
            return t + got[:, 4:, :] * jnp.exp(got[:, :4, :] - ctop)

        ctotal = lax.fori_loop(
            0, 15, add, cmine[:, 4:, :] * jnp.exp(cmine[:, :4, :] - ctop)
        )
        col_lse = ctop + jnp.log(ctotal)
        colfac[:, 0:4, :] = jnp.exp(cmine[:, :4, :] - col_lse)
        return row_lse, col_lse

    rowst[...] = jnp.ones_like(rowst)
    rowtmp[...] = jnp.zeros_like(rowtmp)
    img_start(0)
    text_start(0)
    it[z] = timg[...]
    is_[z] = simg[...]
    text_spread(0)
    img_pass_on(0)
    text_start(1)
    img_start(1)
    text_share(0)
    text_spread(1)
    text_wait(0)

    def view_at(i):
        return lax.rem(z + i, 4)

    scores(0, z, pt, qt, teacher_scale)
    img_pass_on(1)
    img_recv(0, 0, 1)
    scores(0, zm1, pt, qt, teacher_scale)
    img_recv(0, 1, 0)
    scores(0, zp1, pt, qt, teacher_scale)
    text_share(1)
    img_recv_far(0, 0)
    img_recv_far(0, 1)
    scores(0, zp2, pt, qt, teacher_scale)
    stats_start(0)
    stats_finish(0)

    partner = (b, (1 - yh) * 4 + z)

    def tgt_copy(n):
        return copy(tgt.at[n], tgt_in.at[n], tgt_s.at[n], tgt_r.at[n], partner)

    for n in range(NCH):
        acc = None
        for v in range(4):
            term = pt[v, n] * rowfac[:ROWS, v : v + 1] + qt[v, n] * colfac[n, v : v + 1, :]
            acc = term if acc is None else acc + term
        tgt[n] = acc
        tgt_copy(n).start()

    text_wait(1)
    scores(1, z, ps, qs, student_scale)
    img_recv(1, 0, 1)
    scores(1, zm1, ps, qs, student_scale)
    img_recv(1, 1, 0)
    scores(1, zp1, ps, qs, student_scale)
    img_recv_far(1, 0)
    img_recv_far(1, 1)
    scores(1, zp2, ps, qs, student_scale)
    stats_start(1)
    row_lse, col_lse = stats_finish(1)
    rl = lax.broadcasted_iota(jnp.int32, (4, CH), 0)
    cl = lax.broadcasted_iota(jnp.int32, (4, CH), 1)
    lse_part = jnp.sum(
        jnp.where((rl == z) & (cl < ROWS), row_lse, 0.0)
        + jnp.sum(col_lse, axis=0) * (1.0 / 16.0),
        axis=0, keepdims=True,
    )
    collse[0:1, :] = lse_part

    for v in range(4):
        for n in range(NCH):
            w[v, n] = (
                ps[v, n] * rowfac[:ROWS, v : v + 1] + qs[v, n] * colfac[n, v : v + 1, :]
            ).astype(BF16)

    def image_term(i, _):
        v = view_at(i)
        acc = dot(w[v, 0], ts[0:CH, :], NN)
        for n in range(1, NCH):
            acc = acc + dot(w[v, n], ts[n * CH : (n + 1) * CH, :], NN)
        gsend[i] = acc
        return 0

    lax.fori_loop(0, 4, image_term, 0)

    def text_term(n, _):
        acc = dot(w[0, n], is_[0], TN)
        for v in range(1, 4):
            acc = acc + dot(w[v, n], is_[v], TN)
        gtp[n] = acc
        return 0

    lax.fori_loop(0, NCH, text_term, 0)
    total_img = (
        is_[0].astype(F32) + is_[1].astype(F32) + is_[2].astype(F32) + is_[3].astype(F32)
    )
    hi = total_img.astype(BF16)
    lo = (total_img - hi.astype(F32)).astype(BF16)

    for n in range(NCH):
        tgt_copy(n).wait_recv()
        tw[n] = ((tgt[n] + tgt_in[n]) * 0.125).astype(BF16)
    target_text = dot(tw[0], ts[0:CH, :], NN)
    for n in range(1, NCH):
        target_text = target_text + dot(tw[n], ts[n * CH : (n + 1) * CH, :], NN)

    def g_copy(d):
        return copy(gsend.at[d], grecv.at[d - 1], g_s.at[d - 1], g_r.at[d - 1], znext(d))

    for d in (2, 1, 3):
        gsend[d] = gsend[d] - target_text
        g_copy(d).start()
    gsend[0] = gsend[0] - target_text

    for n in range(NCH):
        res = gtp[n] - dot(tw[n], hi, TN) - dot(tw[n], lo, TN)
        for s in range(8):
            row = n * CH + s * 48
            blk, inner = row // ROWS, row % ROWS
            kk, off = inner // HALF, inner % HALF
            for g in range(4):
                gtc[kk, blk, g, off : off + 48, :] = res[
                    s * 48 : (s + 1) * 48, g * 128 : (g + 1) * 128
                ]
    gc = copy(gtc.at[1 - k], gt_sib, gc_s.at[0], gc_r.at[0], sib)
    gc.start()

    target_loss = jnp.sum(
        jnp.sum(total_img * target_text, axis=0, keepdims=True), axis=1, keepdims=True
    )
    part = jnp.sum(collse[0:1, :], axis=1, keepdims=True) - target_loss * student_scale
    loss_src[...] = jnp.broadcast_to(part, (8, 128))

    def lb_copy(d):
        return copy(loss_src, loss_b.at[d - 1], lb_s.at[d - 1], lb_r.at[d - 1],
                    (lax.rem(b + d, 16), a))

    def lb_go(d, _):
        lb_copy(d).start()
        return 0

    lax.fori_loop(1, 16, lb_go, 0)

    gc.wait_recv()
    for blk in range(4):
        for g in range(4):
            gtc[k, blk, g] = gtc[k, blk, g] + gt_sib[blk, g]
    chip = x * 4 + yl * 2 + yh

    def rs_copy(d):
        i = lax.rem(chip + d, 16)
        xi, yli, yhi = i // 4, (i // 2) % 2, i % 2
        return copy(gtc.at[k, xi, yhi * 2 + yli], rs_buf.at[d - 1], rs_s.at[d - 1],
                    rs_r.at[d - 1], dev(xi, yli * 2 + k, yhi, z))

    def rs_go(d, _):
        rs_copy(d).start()
        return 0

    lax.fori_loop(1, 16, rs_go, 0)

    def lb_wait(d, acc):
        lb_copy(d).wait_recv()
        return acc + loss_b[d - 1]

    loss_src2[...] = lax.fori_loop(1, 16, lb_wait, loss_src[...])

    def la_copy(d):
        return copy(loss_src2, loss_a.at[d - 1], la_s.at[d - 1], la_r.at[d - 1],
                    (b, lax.rem(a + d, 8)))

    def la_go(d, _):
        la_copy(d).start()
        return 0

    lax.fori_loop(1, 8, la_go, 0)

    def rs_wait(d, _):
        rs_copy(d).wait_recv()
        fb_src[...] = fb_src[...] + rs_buf[d - 1]
        return 0

    fb_src[...] = gtc[k, x, yh * 2 + yl]
    lax.fori_loop(1, 16, rs_wait, 0)
    fb_src[...] = fb_src[...] * student_scale

    def fb_to(i):
        return (x * 4 + z, i)

    def fb_copy(i):
        return copy(fb_src, fb_buf.at[j * 2 + yh], fb_s.at[i], fb_r.at[j * 2 + yh], fb_to(i))

    def is_self(i):
        return (j == z) & (i == a)

    def fb_go(i, _):
        @pl.when(jnp.logical_not(is_self(i)))
        def _():
            fb_copy(i).start()

        return 0

    lax.fori_loop(0, 8, fb_go, 0)

    @pl.when(j == z)
    def _():
        fb_buf[j * 2 + yh] = fb_src[...]

    acc = gsend[0]
    for d in (1, 3, 2):
        g_copy(d).wait_recv()
        acc = acc + grecv[d - 1]
    gi_out[...] = acc * student_scale

    def la_wait(d, acc):
        la_copy(d).wait_recv()
        return acc + loss_a[d - 1]

    loss_out[...] = lax.fori_loop(1, 8, la_wait, loss_src2[...]) * (1.0 / (2.0 * 8 * 4608))

    def fb_wait(s, _):
        mine = (z == j) & (s == j * 2 + yh)

        @pl.when(jnp.logical_not(mine))
        def _():
            copy(fb_src, fb_buf.at[s], fb_s.at[s], fb_r.at[s], sib).wait_recv()

        return 0

    lax.fori_loop(0, 8, fb_wait, 0)
    for s in range(8):
        syl_, sk_, syh_ = s // 4, (s // 2) % 2, s % 2
        g = syh_ * 2 + syl_
        gt_out[sk_ * HALF : (sk_ + 1) * HALF, g * 128 : (g + 1) * 128] = fb_buf[s]

    for m in range(2):
        for d in range(2):
            for h in range(2):
                img_send(m, d, h).wait_send()
            img_relay(m, d).wait_send()

        @pl.when(is_source)
        def _():
            for c in text_first(m):
                c.wait_send()

        for d in (1, 2, 3):
            text_x(m, d).wait_send()
            row_copy(m, d).wait_send()
        for d in range(4):
            text_sib(m, d).wait_send()

        def col_sent(d, _):
            col_copy(m, d).wait_send()
            return 0

        lax.fori_loop(1, 16, col_sent, 0)
    for n in range(NCH):
        tgt_copy(n).wait_send()
    for d in (1, 2, 3):
        g_copy(d).wait_send()
    gc.wait_send()

    def sent16(d, _):
        rs_copy(d).wait_send()
        lb_copy(d).wait_send()
        return 0

    lax.fori_loop(1, 16, sent16, 0)

    def sent8(d, _):
        la_copy(d).wait_send()
        return 0

    lax.fori_loop(1, 8, sent8, 0)

    def fb_sent(i, _):
        @pl.when(jnp.logical_not(is_self(i)))
        def _():
            fb_copy(i).wait_send()

        return 0

    lax.fori_loop(0, 8, fb_sent, 0)


def per_device(student_image, student_text, teacher_image, teacher_text):
    vm = pl.BlockSpec(memory_space=pltpu.VMEM)
    dma = pltpu.SemaphoreType.DMA
    V = pltpu.VMEM
    sw, twd = student_image.shape[2], teacher_image.shape[2]
    loss, gi, gt = pl.pallas_call(
        kernel,
        name="distill",
        out_shape=(
            jax.ShapeDtypeStruct((8, 128), F32),
            jax.ShapeDtypeStruct((ROWS, sw), F32),
            jax.ShapeDtypeStruct((ROWS, sw), F32),
        ),
        in_specs=[vm] * 4,
        out_specs=(vm, vm, vm),
        scratch_shapes=[
            V((4, ROWS, twd), BF16), V((4, ROWS, sw), BF16),
            V((4 * ROWS, twd), BF16), V((4 * ROWS, sw), BF16),
            V((4, NCH, ROWS, CH), F32), V((4, NCH, ROWS, CH), F32),
            V((4, NCH, ROWS, CH), F32), V((4, NCH, ROWS, CH), F32),
            V((4, NCH, ROWS, CH), BF16),
            V((NCH, ROWS, CH), F32), V((NCH, ROWS, CH), F32), V((NCH, ROWS, CH), BF16),
            V((4, ROWS, sw), F32), V((3, ROWS, sw), F32),
            V((NCH, CH, sw), F32), V((4, 4, HALF, 128), F32),
            V((15, HALF, 128), F32), V((HALF, 128), F32), V((8, HALF, 128), F32),
            V((2, 4, 4, HALF, 128), F32),
            V((384, 128), F32), V((2, 8, 384), F32), V((2, 3, 8, 384), F32),
            V((384, 128), F32), V((128, 384), F32),
            V((2, NCH, 8, CH), F32), V((2, 15, NCH, 8, CH), F32),
            V((NCH, 8, CH), F32), V((8, CH), F32),
            V((8, 128), F32), V((15, 8, 128), F32), V((8, 128), F32), V((7, 8, 128), F32),
            dma((2, 3, 2)), dma((2, 3, 2)),
            dma((2, 3)), dma((2,)), dma((2, 3)), dma((2, 3)), dma((2, 4)), dma((2, 4)),
            dma((2, 3)), dma((2, 3)), dma((2, 15)), dma((2, 15)),
            dma((3,)), dma((3,)), dma((3,)), dma((3,)), dma((1,)), dma((1,)),
            dma((15,)), dma((15,)), dma((8,)), dma((8,)),
            dma((15,)), dma((15,)), dma((7,)), dma((7,)),
        ],
        compiler_params=pltpu.CompilerParams(
            collective_id=0, has_side_effects=True, vmem_limit_bytes=60 * 1024 * 1024
        ),
        cost_estimate=pl.CostEstimate(
            flops=8 * 10**9, bytes_accessed=4 * 2**20, transcendentals=6 * 10**6
        ),
    )(student_image[0], student_text, teacher_image[0], teacher_text)
    return loss[0, 0], gi[None], gt


def solution(mesh):
    return jax.shard_map(
        per_device,
        mesh=mesh,
        in_specs=(
            P("aug", "batch", None),
            P("batch", None),
            P("aug", "batch", None),
            P("batch", None),
        ),
        out_specs=(P(), P("aug", "batch", None), P("batch", None)),
        check_vma=False,
    )
```

```python
import functools
import math

import jax
import jax.numpy as jnp
from jax import lax
from jax.experimental import pallas as pl
from jax.experimental.pallas import tpu as pltpu
from jax.sharding import PartitionSpec as P

MESH = pl.DeviceIdType.MESH
F32 = jnp.float32
BF16 = jnp.bfloat16
ROWS = 288
HALF = ROWS // 2
COLS = 4 * ROWS
NCH = 3
NT = (((1,), (1,)), ((), ()))
NN = (((1,), (0,)), ((), ()))
TN = (((0,), (0,)), ((), ()))


def dot(a, b, dims):
    return lax.dot_general(a, b, dims, preferred_element_type=F32)


def kernel(
    simg, stext, timg, ttext,
    loss_out, gi_out, gt_out,
    it, is_, tt, ts, pt, qt, ps, qs, w, tgt, tgt_in, tw,
    gsend, grecv, gtp, gt_sib, rs_buf, fb_src, fb_buf, gtc,
    rowst, rowsend, rowrecv, rowfac, rowtmp, colst, colrecv, colfac,
    loss_src, loss_b, loss_src2, loss_a,
    zi_s, zi_r, t1_s, t1_r, t2_s, t2_r, t3_s, t3_r,
    row_s, row_r, col_s, col_r, tgt_s, tgt_r, g_s, g_r, gc_s, gc_r,
    rs_s, rs_r, fb_s, fb_r, lb_s, lb_r, la_s, la_r,
):
    b = lax.axis_index("batch")
    a = lax.axis_index("aug")
    x, j = b // 4, b % 4
    yl, k = j // 2, j % 2
    yh, z = a // 4, a % 4
    sib = (b + 1 - 2 * k, a)
    teacher_scale = 3.0 / math.sqrt(timg.shape[1])
    student_scale = 3.0 / math.sqrt(simg.shape[1])

    def dev(x_, j_, yh_, z_):
        return (x_ * 4 + j_, yh_ * 4 + z_)

    def znext(d):
        return (b, yh * 4 + lax.rem(z + d, 4))

    def copy(src, dst, ss, rs, to):
        return pltpu.make_async_remote_copy(
            src_ref=src, dst_ref=dst, send_sem=ss, recv_sem=rs, device_id=to, device_id_type=MESH
        )

    sent = []

    def start(c):
        c.start()
        sent.append(c.wait_send)

    def start_all(lo, hi, make):
        def go(i, _):
            make(i).start()
            return 0

        def gone(i, _):
            make(i).wait_send()
            return 0

        lax.fori_loop(lo, hi, go, 0)
        sent.append(lambda: lax.fori_loop(lo, hi, gone, 0))

    barrier = pltpu.get_barrier_semaphore()

    near = [(b, yh * 4 + lax.rem(z + d, 4)) for d in (1, 2, 3)]
    near += [(lax.rem(x + d, 4) * 4 + j, a) for d in (1, 2, 3)]
    near += [(x * 4 + lax.rem(j + d, 4), a) for d in (1, 2, 3)]
    near += [(b, (1 - yh) * 4 + z)]
    for peer in near:
        pl.semaphore_signal(barrier, 1, device_id=peer, device_id_type=MESH)
    pl.semaphore_wait(barrier, len(near))

    zm1, zp1, zp2 = lax.rem(z + 3, 4), lax.rem(z + 1, 4), lax.rem(z + 2, 4)
    own = (timg, simg)
    imgs = (it, is_)
    texts = (tt, ts)
    own_text = (ttext, stext)

    def half(h):
        return pl.ds(h * HALF, HALF)

    def img_send(m, d, h):
        return copy(
            own[m].at[half(h)], imgs[m].at[z, half(h)], zi_s.at[m, d, h], zi_r.at[m, d, h],
            znext(1 if d == 0 else 3),
        )

    def img_relay(m, d):
        slot = zm1 if d == 0 else zp1
        ref = imgs[m].at[slot, half(d)]
        return copy(ref, ref, zi_s.at[m, 2, d], zi_r.at[m, 2, d], znext(1 if d == 0 else 3))

    def img_recv(m, d, h):
        slot = zm1 if d == 0 else zp1
        ref = imgs[m].at[slot, half(h)]
        copy(ref, ref, zi_s.at[m, d, h], zi_r.at[m, d, h], znext(1)).wait_recv()

    def img_recv_far(m, d):
        ref = imgs[m].at[zp2, half(d)]
        copy(ref, ref, zi_s.at[m, 2, d], zi_r.at[m, 2, d], znext(1)).wait_recv()

    def img_start(m):
        for d, h in ((0, 0), (1, 1), (0, 1), (1, 0)):
            start(img_send(m, d, h))

    def img_pass_on(m):
        img_recv(m, 0, 0)
        start(img_relay(m, 0))
        img_recv(m, 1, 1)
        start(img_relay(m, 1))

    syl, sk = z // 2, z % 2
    is_source = j == z

    def tslab(m, blk, h):
        return texts[m].at[pl.ds(blk * ROWS + h * HALF, HALF)]

    def text_first(m):
        return (
            copy(own_text[m].at[pl.ds((1 - sk) * HALF, HALF)], tslab(m, x, 1 - sk),
                 t1_s.at[m, 0], t1_r.at[m], dev(x, syl * 2 + 1 - sk, yh, z)),
            copy(own_text[m].at[half(0)], tslab(m, x, 0),
                 t1_s.at[m, 1], t1_r.at[m], dev(x, (1 - syl) * 2, yh, z)),
            copy(own_text[m].at[half(1)], tslab(m, x, 1),
                 t1_s.at[m, 2], t1_r.at[m], dev(x, (1 - syl) * 2 + 1, yh, z)),
        )

    def text_start(m):
        @pl.when(is_source)
        def _():
            for c in text_first(m):
                c.start()
            tslab(m, x, k)[...] = own_text[m][pl.ds(k * HALF, HALF)]

        def gone():
            @pl.when(is_source)
            def _():
                for c in text_first(m):
                    c.wait_send()

        sent.append(gone)

    def text_x(m, d):
        return copy(tslab(m, x, k), tslab(m, x, k), t2_s.at[m, d - 1], t2_r.at[m, d - 1],
                    (lax.rem(x + d, 4) * 4 + j, a))

    def text_sib(m, d):
        blk = lax.rem(x + 4 - d, 4)
        return copy(tslab(m, blk, k), tslab(m, blk, k), t3_s.at[m, d], t3_r.at[m, d], sib)

    def text_spread(m):
        @pl.when(jnp.logical_not(is_source))
        def _():
            copy(tslab(m, x, k), tslab(m, x, k), t1_s.at[m, 0], t1_r.at[m], sib).wait_recv()

        for d in (1, 3, 2):
            start(text_x(m, d))
        start(text_sib(m, 0))

    def text_share(m):
        for d in (1, 3, 2):
            blk = lax.rem(x + 4 - d, 4)
            copy(tslab(m, blk, k), tslab(m, blk, k), t2_s.at[m, d - 1], t2_r.at[m, d - 1],
                 sib).wait_recv()
            start(text_sib(m, d))

    def text_wait(m):
        for d in range(4):
            blk = lax.rem(x + 4 - d, 4)
            copy(tslab(m, blk, 1 - k), tslab(m, blk, 1 - k), t3_s.at[m, d], t3_r.at[m, d],
                 sib).wait_recv()

    lane = lax.broadcasted_iota(jnp.int32, (ROWS, 128), 1)

    def fold(op, t):
        return functools.reduce(op, [t[:, i * 128 : (i + 1) * 128] for i in range(COLS // 128)])

    def scores(m, v, pr, qr, scale):
        t = dot(imgs[m][v], texts[m][...], NT) * scale
        cm = jnp.max(t, axis=0, keepdims=True)
        top = jnp.max(fold(jnp.maximum, t), axis=1, keepdims=True)
        q = jnp.exp(t - cm)
        qr[v] = q
        p = jnp.exp(t - top)
        pr[v] = p
        colst[m, pl.ds(v, 1), :] = cm
        colst[m, pl.ds(v + 4, 1), :] = jnp.sum(q, axis=0, keepdims=True)
        total = jnp.sum(fold(jnp.add, p), axis=1, keepdims=True)
        rowst[:ROWS, :] = jnp.where(
            lane == v, top, jnp.where(lane == v + 4, total, rowst[:ROWS, :])
        )

    def row_copy(m, d):
        return copy(rowsend.at[m], rowrecv.at[m, d - 1], row_s.at[m, d - 1], row_r.at[m, d - 1],
                    znext(d))

    def col_copy(m, d):
        return copy(colst.at[m], colrecv.at[m, d - 1], col_s.at[m, d - 1], col_r.at[m, d - 1],
                    (lax.rem(b + d, 16), a))

    def stats_start(m):
        start_all(1, 16, lambda d: col_copy(m, d))
        rowsend[m] = jnp.transpose(rowst[...])[:8]
        for d in (1, 3, 2):
            start(row_copy(m, d))

    def stats_finish(m):
        for d in (1, 3, 2):
            row_copy(m, d).wait_recv()
        mine = rowsend[m]
        top = mine[:4]
        for d in range(3):
            top = jnp.maximum(top, rowrecv[m, d, :4])
        total = mine[4:] * jnp.exp(mine[:4] - top)
        for d in range(3):
            got = rowrecv[m, d]
            total = total + got[4:] * jnp.exp(got[:4] - top)
        row_lse = top + jnp.log(total)
        rowtmp[0:4, :] = jnp.exp(mine[:4] - row_lse)
        rowfac[...] = jnp.transpose(rowtmp[...])

        def arrived(d, _):
            col_copy(m, d).wait_recv()
            return 0

        lax.fori_loop(1, 16, arrived, 0)
        cmine = colst[m]

        def highest(d, t):
            return jnp.maximum(t, colrecv[m, d, :4, :])

        ctop = lax.fori_loop(0, 15, highest, cmine[:4])

        def add(d, t):
            got = colrecv[m, d]
            return t + got[4:] * jnp.exp(got[:4] - ctop)

        ctotal = lax.fori_loop(
            0, 15, add, cmine[4:] * jnp.exp(cmine[:4] - ctop)
        )
        col_lse = ctop + jnp.log(ctotal)
        colfac[0:4, :] = jnp.exp(cmine[:4] - col_lse)
        return row_lse, col_lse

    rowst[...] = jnp.ones_like(rowst)
    rowtmp[...] = jnp.zeros_like(rowtmp)
    img_start(0)
    text_start(0)
    it[z] = timg[...]
    is_[z] = simg[...]
    text_spread(0)
    img_pass_on(0)
    text_start(1)
    img_start(1)
    text_share(0)
    text_spread(1)
    text_wait(0)

    def view_at(i):
        return lax.rem(z + i, 4)

    scores(0, z, pt, qt, teacher_scale)
    img_pass_on(1)
    img_recv(0, 0, 1)
    scores(0, zm1, pt, qt, teacher_scale)
    img_recv(0, 1, 0)
    scores(0, zp1, pt, qt, teacher_scale)
    text_share(1)
    img_recv_far(0, 0)
    img_recv_far(0, 1)
    scores(0, zp2, pt, qt, teacher_scale)
    stats_start(0)
    stats_finish(0)

    partner = (b, (1 - yh) * 4 + z)

    def tgt_copy(n):
        return copy(tgt.at[n], tgt_in.at[n], tgt_s.at[n], tgt_r.at[n], partner)

    for n in range(NCH):
        rows = slice(n * 96, (n + 1) * 96)
        acc = None
        for v in range(4):
            term = pt[v, rows] * rowfac[rows, v : v + 1] + qt[v, rows] * colfac[v : v + 1, :]
            acc = term if acc is None else acc + term
        tgt[n] = acc
        start(tgt_copy(n))

    text_wait(1)
    scores(1, z, ps, qs, student_scale)
    img_recv(1, 0, 1)
    scores(1, zm1, ps, qs, student_scale)
    img_recv(1, 1, 0)
    scores(1, zp1, ps, qs, student_scale)
    img_recv_far(1, 0)
    img_recv_far(1, 1)
    scores(1, zp2, ps, qs, student_scale)
    stats_start(1)
    row_lse, col_lse = stats_finish(1)
    rl = lax.broadcasted_iota(jnp.int32, (4, 384), 0)
    cl = lax.broadcasted_iota(jnp.int32, (4, 384), 1)
    row_part = jnp.sum(jnp.where((rl == z) & (cl < ROWS), row_lse, 0.0), axis=0, keepdims=True)
    lse_part = (
        jnp.sum(row_part, axis=1, keepdims=True)
        + jnp.sum(jnp.sum(col_lse, axis=0, keepdims=True), axis=1, keepdims=True) * (1.0 / 16.0)
    )

    for v in range(4):
        for n in range(NCH):
            rows = slice(n * 96, (n + 1) * 96)
            w[v, rows] = (
                ps[v, rows] * rowfac[rows, v : v + 1] + qs[v, rows] * colfac[v : v + 1, :]
            ).astype(BF16)

    def image_term(i, _):
        v = view_at(i)
        gsend[i] = dot(w[v], ts[...], NN)
        return 0

    lax.fori_loop(0, 4, image_term, 0)

    acc = dot(w[0], is_[0], TN)
    for v in range(1, 4):
        acc = acc + dot(w[v], is_[v], TN)
    gtp[...] = acc
    total_img = (
        is_[0].astype(F32) + is_[1].astype(F32) + is_[2].astype(F32) + is_[3].astype(F32)
    )
    hi = total_img.astype(BF16)
    lo = (total_img - hi.astype(F32)).astype(BF16)

    for n in range(NCH):
        tgt_copy(n).wait_recv()
        tw[n * 96 : (n + 1) * 96] = ((tgt[n] + tgt_in[n]) * 0.125).astype(BF16)
    target_text = dot(tw[...], ts[...], NN)

    def g_copy(d):
        return copy(gsend.at[d], grecv.at[d - 1], g_s.at[d - 1], g_r.at[d - 1], znext(d))

    for d in (2, 1, 3):
        gsend[d] = gsend[d] - target_text
        start(g_copy(d))
    gsend[0] = gsend[0] - target_text

    res = gtp[...] - dot(tw[...], hi, TN) - dot(tw[...], lo, TN)
    for s in range(8):
        row = s * HALF
        for g in range(4):
            gtc[s % 2, s // 2, g] = res[row : row + HALF, g * 128 : (g + 1) * 128]
    gc = copy(gtc.at[1 - k], gt_sib, gc_s.at[0], gc_r.at[0], sib)
    start(gc)

    target_loss = jnp.sum(
        jnp.sum(total_img * target_text, axis=0, keepdims=True), axis=1, keepdims=True
    )
    part = lse_part - target_loss * student_scale
    loss_src[...] = jnp.broadcast_to(part, (8, 128))

    def lb_copy(d):
        return copy(loss_src, loss_b.at[d - 1], lb_s.at[d - 1], lb_r.at[d - 1],
                    (lax.rem(b + d, 16), a))

    start_all(1, 16, lb_copy)

    gc.wait_recv()
    for blk in range(4):
        for g in range(4):
            gtc[k, blk, g] = gtc[k, blk, g] + gt_sib[blk, g]
    chip = x * 4 + yl * 2 + yh

    def rs_copy(d):
        i = lax.rem(chip + d, 16)
        xi, yli, yhi = i // 4, (i // 2) % 2, i % 2
        return copy(gtc.at[k, xi, yhi * 2 + yli], rs_buf.at[d - 1], rs_s.at[d - 1],
                    rs_r.at[d - 1], dev(xi, yli * 2 + k, yhi, z))

    start_all(1, 16, rs_copy)

    def lb_wait(d, acc):
        lb_copy(d).wait_recv()
        return acc + loss_b[d - 1]

    loss_src2[...] = lax.fori_loop(1, 16, lb_wait, loss_src[...])

    def la_copy(d):
        return copy(loss_src2, loss_a.at[d - 1], la_s.at[d - 1], la_r.at[d - 1],
                    (b, lax.rem(a + d, 8)))

    start_all(1, 8, la_copy)

    def rs_wait(d, _):
        rs_copy(d).wait_recv()
        fb_src[...] = fb_src[...] + rs_buf[d - 1]
        return 0

    fb_src[...] = gtc[k, x, yh * 2 + yl]
    lax.fori_loop(1, 16, rs_wait, 0)
    fb_src[...] = fb_src[...] * student_scale

    def fb_to(i):
        return (x * 4 + z, i)

    def fb_copy(i):
        return copy(fb_src, fb_buf.at[j * 2 + yh], fb_s.at[i], fb_r.at[j * 2 + yh], fb_to(i))

    def is_self(i):
        return (j == z) & (i == a)

    def fb_go(i, _):
        @pl.when(jnp.logical_not(is_self(i)))
        def _():
            fb_copy(i).start()

        return 0

    lax.fori_loop(0, 8, fb_go, 0)

    def fb_gone(i, _):
        @pl.when(jnp.logical_not(is_self(i)))
        def _():
            fb_copy(i).wait_send()

        return 0

    sent.append(lambda: lax.fori_loop(0, 8, fb_gone, 0))

    @pl.when(j == z)
    def _():
        fb_buf[j * 2 + yh] = fb_src[...]

    acc = gsend[0]
    for d in (1, 3, 2):
        g_copy(d).wait_recv()
        acc = acc + grecv[d - 1]
    gi_out[...] = acc * student_scale

    def la_wait(d, acc):
        la_copy(d).wait_recv()
        return acc + loss_a[d - 1]

    loss_out[...] = lax.fori_loop(1, 8, la_wait, loss_src2[...]) * (1.0 / (2.0 * 8 * 4608))

    def fb_wait(s, _):
        mine = (z == j) & (s == j * 2 + yh)

        @pl.when(jnp.logical_not(mine))
        def _():
            copy(fb_src, fb_buf.at[s], fb_s.at[s], fb_r.at[s], sib).wait_recv()

        return 0

    lax.fori_loop(0, 8, fb_wait, 0)
    for s in range(8):
        syl_, sk_, syh_ = s // 4, (s // 2) % 2, s % 2
        g = syh_ * 2 + syl_
        gt_out[sk_ * HALF : (sk_ + 1) * HALF, g * 128 : (g + 1) * 128] = fb_buf[s]

    for gone in sent:
        gone()


def per_device(student_image, student_text, teacher_image, teacher_text):
    vm = pl.BlockSpec(memory_space=pltpu.VMEM)
    dma = pltpu.SemaphoreType.DMA
    V = pltpu.VMEM
    sw, twd = student_image.shape[2], teacher_image.shape[2]
    loss, gi, gt = pl.pallas_call(
        kernel,
        name="distill",
        out_shape=(
            jax.ShapeDtypeStruct((8, 128), F32),
            jax.ShapeDtypeStruct((ROWS, sw), F32),
            jax.ShapeDtypeStruct((ROWS, sw), F32),
        ),
        in_specs=[vm] * 4,
        out_specs=(vm, vm, vm),
        scratch_shapes=[
            V((4, ROWS, twd), BF16), V((4, ROWS, sw), BF16),
            V((4 * ROWS, twd), BF16), V((4 * ROWS, sw), BF16),
            V((4, ROWS, COLS), F32), V((4, ROWS, COLS), F32),
            V((4, ROWS, COLS), F32), V((4, ROWS, COLS), F32),
            V((4, ROWS, COLS), BF16),
            V((NCH, 96, COLS), F32), V((NCH, 96, COLS), F32), V((ROWS, COLS), BF16),
            V((4, ROWS, sw), F32), V((3, ROWS, sw), F32),
            V((COLS, sw), F32), V((4, 4, HALF, 128), F32),
            V((15, HALF, 128), F32), V((HALF, 128), F32), V((8, HALF, 128), F32),
            V((2, 4, 4, HALF, 128), F32),
            V((384, 128), F32), V((2, 8, 384), F32), V((2, 3, 8, 384), F32),
            V((384, 128), F32), V((128, 384), F32),
            V((2, 8, COLS), F32), V((2, 15, 8, COLS), F32), V((8, COLS), F32),
            V((8, 128), F32), V((15, 8, 128), F32), V((8, 128), F32), V((7, 8, 128), F32),
            dma((2, 3, 2)), dma((2, 3, 2)),
            dma((2, 3)), dma((2,)), dma((2, 3)), dma((2, 3)), dma((2, 4)), dma((2, 4)),
            dma((2, 3)), dma((2, 3)), dma((2, 15)), dma((2, 15)),
            dma((3,)), dma((3,)), dma((3,)), dma((3,)), dma((1,)), dma((1,)),
            dma((15,)), dma((15,)), dma((8,)), dma((8,)),
            dma((15,)), dma((15,)), dma((7,)), dma((7,)),
        ],
        compiler_params=pltpu.CompilerParams(
            collective_id=0, has_side_effects=True, vmem_limit_bytes=60 * 1024 * 1024
        ),
        cost_estimate=pl.CostEstimate(
            flops=8 * 10**9, bytes_accessed=4 * 2**20, transcendentals=6 * 10**6
        ),
    )(student_image[0], student_text, teacher_image[0], teacher_text)
    return loss[0, 0], gi[None], gt


def solution(mesh):
    return jax.shard_map(
        per_device,
        mesh=mesh,
        in_specs=(
            P("aug", "batch", None),
            P("batch", None),
            P("aug", "batch", None),
            P("batch", None),
        ),
        out_specs=(P(), P("aug", "batch", None), P("batch", None)),
        check_vma=False,
    )
```

```python
import functools
import math

import jax
import jax.numpy as jnp
from jax import lax
from jax.experimental import pallas as pl
from jax.experimental.pallas import tpu as pltpu
from jax.sharding import PartitionSpec as P

MESH = pl.DeviceIdType.MESH
F32 = jnp.float32
BF16 = jnp.bfloat16
ROWS = 288
HALF = ROWS // 2
COLS = 4 * ROWS
NCH = 3
NT = (((1,), (1,)), ((), ()))
NN = (((1,), (0,)), ((), ()))
TN = (((0,), (0,)), ((), ()))


def dot(a, b, dims):
    return lax.dot_general(a, b, dims, preferred_element_type=F32)


def kernel(
    simg, stext, timg, ttext,
    loss_out, gi_out, gt_out,
    it, is_, tt, ts, pt, qt, ps, qs, w, tgt, tgt_mine, tgt_in, tw,
    isum, isum_in, isum8, hi, lo, tt_part, tt_in, tt_src, tt_all,
    gsend, grecv, gfar_in, gtp, gt_sib, ra_in, rb_in, ra_sum, rb_sum, ra2_in, rb2_in, fb_src, fb_buf, gtc,
    rowst, rowsend, rowrecv, rowfac, rowtmp, colst, quad_in, colq, colx_in, colfac,
    loss_src, loss_b, loss_src2, loss_a,
    zi_s, zi_r, t1_s, t1_r, t2_s, t2_r, t3_s, t3_r, t4_s, t4_r,
    iy_s, iy_r, iz_s, iz_r, tz_s, tz_r, ta_s, ta_r,
    quad_s, quad_r, row_s, row_r, col_s, col_r, tgt_s, tgt_r, g_s, g_r, gc_s, gc_r,
    rs_s, rs_r, fb_s, fb_r, lb_s, lb_r, la_s, la_r,
):
    b = lax.axis_index("batch")
    a = lax.axis_index("aug")
    x, j = b // 4, b % 4
    yl, k = j // 2, j % 2
    yh, z = a // 4, a % 4
    sib = (b + 1 - 2 * k, a)
    teacher_scale = 3.0 / math.sqrt(timg.shape[1])
    student_scale = 3.0 / math.sqrt(simg.shape[1])

    def dev(x_, j_, yh_, z_):
        return (x_ * 4 + j_, yh_ * 4 + z_)

    def znext(d):
        return (b, yh * 4 + lax.rem(z + d, 4))

    def copy(src, dst, ss, rs, to):
        return pltpu.make_async_remote_copy(
            src_ref=src, dst_ref=dst, send_sem=ss, recv_sem=rs, device_id=to, device_id_type=MESH
        )

    sent = []

    def start(c):
        c.start()
        sent.append(c.wait_send)

    def start_all(lo, hi, make):
        def go(i, _):
            make(i).start()
            return 0

        def gone(i, _):
            make(i).wait_send()
            return 0

        lax.fori_loop(lo, hi, go, 0)
        sent.append(lambda: lax.fori_loop(lo, hi, gone, 0))

    barrier = pltpu.get_barrier_semaphore()

    near = [(b, yh * 4 + lax.rem(z + d, 4)) for d in (1, 2, 3)]
    near += [(lax.rem(x + d, 4) * 4 + j, a) for d in (1, 2, 3)]
    near += [(x * 4 + lax.rem(j + d, 4), a) for d in (1, 2, 3)]
    near += [(x * 4 + lax.rem(j + d, 4), (1 - yh) * 4 + z) for d in range(4)]
    for peer in near:
        pl.semaphore_signal(barrier, 1, device_id=peer, device_id_type=MESH)
    pl.semaphore_wait(barrier, len(near))

    zm1, zp1, zp2 = lax.rem(z + 3, 4), lax.rem(z + 1, 4), lax.rem(z + 2, 4)
    own = (timg, simg)
    imgs = (it, is_)
    texts = (tt, ts)
    own_text = (ttext, stext)

    def half(h):
        return pl.ds(h * HALF, HALF)

    def img_send(m, d, h):
        return copy(
            own[m].at[half(h)], imgs[m].at[z, half(h)], zi_s.at[m, d, h], zi_r.at[m, d, h],
            znext(1 if d == 0 else 3),
        )

    def img_relay(m, d):
        slot = zm1 if d == 0 else zp1
        ref = imgs[m].at[slot, half(d)]
        return copy(ref, ref, zi_s.at[m, 2, d], zi_r.at[m, 2, d], znext(1 if d == 0 else 3))

    def img_recv(m, d, h):
        slot = zm1 if d == 0 else zp1
        ref = imgs[m].at[slot, half(h)]
        copy(ref, ref, zi_s.at[m, d, h], zi_r.at[m, d, h], znext(1)).wait_recv()

    def img_recv_far(m, d):
        ref = imgs[m].at[zp2, half(d)]
        copy(ref, ref, zi_s.at[m, 2, d], zi_r.at[m, 2, d], znext(1)).wait_recv()

    def img_start(m):
        for d, h in ((0, 0), (1, 1), (0, 1), (1, 0)):
            start(img_send(m, d, h))

    def img_pass_on(m):
        img_recv(m, 0, 0)
        start(img_relay(m, 0))
        img_recv(m, 1, 1)
        start(img_relay(m, 1))

    syl, sk = z // 2, z % 2
    is_source = j == z

    def tslab(m, blk, h):
        return texts[m].at[pl.ds(blk * ROWS + h * HALF, HALF)]

    def text_first(m):
        return (
            copy(own_text[m].at[pl.ds((1 - sk) * HALF, HALF)], tslab(m, x, 1 - sk),
                 t1_s.at[m, 0], t1_r.at[m], dev(x, syl * 2 + 1 - sk, yh, z)),
            copy(own_text[m].at[half(0)], tslab(m, x, 0),
                 t1_s.at[m, 1], t1_r.at[m], dev(x, (1 - syl) * 2, yh, z)),
            copy(own_text[m].at[half(1)], tslab(m, x, 1),
                 t1_s.at[m, 2], t1_r.at[m], dev(x, (1 - syl) * 2 + 1, 1 - yh, z)),
        )

    def text_start(m):
        @pl.when(is_source)
        def _():
            for c in text_first(m):
                c.start()
            tslab(m, x, k)[...] = own_text[m][pl.ds(k * HALF, HALF)]

        def gone():
            @pl.when(is_source)
            def _():
                for c in text_first(m):
                    c.wait_send()

        sent.append(gone)

    def text_x(m, d):
        return copy(tslab(m, x, k), tslab(m, x, k), t2_s.at[m, d - 1], t2_r.at[m, d - 1],
                    (lax.rem(x + d, 4) * 4 + j, a))

    def text_got(m, d):
        slab = tslab(m, lax.rem(x + 4 - d, 4), k)
        copy(slab, slab, t2_s.at[m, d - 1], t2_r.at[m, d - 1], sib).wait_recv()

    def tlanes(m, blk, i):
        width = texts[m].shape[1] // 2
        return texts[m].at[pl.ds(blk * ROWS + k * HALF, HALF), i * width : (i + 1) * width]

    def text_relay(m, i):
        ref = tlanes(m, lax.rem(x + 3 - 2 * i, 4), i)
        return copy(ref, ref, t4_s.at[m, i], t4_r.at[m, i], (lax.rem(x + 1 + 2 * i, 4) * 4 + j, a))

    def text_sib(m, d):
        blk = lax.rem(x + 4 - d, 4)
        return copy(tslab(m, blk, k), tslab(m, blk, k), t3_s.at[m, d], t3_r.at[m, d], sib)

    def text_spread(m):
        @pl.when(jnp.logical_not(is_source))
        def _():
            copy(tslab(m, x, k), tslab(m, x, k), t1_s.at[m, 0], t1_r.at[m], sib).wait_recv()

        for d in (1, 3):
            start(text_x(m, d))
        start(text_sib(m, 0))

    def text_pass_on(m):
        for d in (1, 3):
            text_got(m, d)
            start(text_relay(m, d // 2))
            start(text_sib(m, d))

    def text_far(m):
        for i in range(2):
            ref = tlanes(m, lax.rem(x + 2, 4), i)
            copy(ref, ref, t4_s.at[m, i], t4_r.at[m, i], sib).wait_recv()
        start(text_sib(m, 2))

    def text_wait(m):
        for d in range(4):
            blk = lax.rem(x + 4 - d, 4)
            copy(tslab(m, blk, 1 - k), tslab(m, blk, 1 - k), t3_s.at[m, d], t3_r.at[m, d],
                 sib).wait_recv()

    lane = lax.broadcasted_iota(jnp.int32, (ROWS, 128), 1)

    def fold(op, t):
        return functools.reduce(op, [t[:, i * 128 : (i + 1) * 128] for i in range(COLS // 128)])

    def scores(m, v, pr, qr, scale):
        t = dot(imgs[m][v], texts[m][...], NT) * scale
        cm = jnp.max(t, axis=0, keepdims=True)
        top = jnp.max(fold(jnp.maximum, t), axis=1, keepdims=True)
        q = jnp.exp(t - cm)
        qr[v] = q
        p = jnp.exp(t - top)
        pr[v] = p
        colst[m, pl.ds(v, 1), :] = cm
        colst[m, pl.ds(v + 4, 1), :] = jnp.sum(q, axis=0, keepdims=True)
        total = jnp.sum(fold(jnp.add, p), axis=1, keepdims=True)
        rowst[:ROWS, :] = jnp.where(
            lane == v, top, jnp.where(lane == v + 4, total, rowst[:ROWS, :])
        )

    def row_copy(m, d):
        return copy(rowsend.at[m], rowrecv.at[m, d - 1], row_s.at[m, d - 1], row_r.at[m, d - 1],
                    znext(d))

    def quad_copy(m, d):
        return copy(colst.at[m], quad_in.at[m, d - 1], quad_s.at[m, d - 1], quad_r.at[m, d - 1],
                    (x * 4 + lax.rem(j + d, 4), a))

    def col_copy(m, d):
        return copy(colq.at[m], colx_in.at[m, d - 1], col_s.at[m, d - 1], col_r.at[m, d - 1],
                    (lax.rem(x + d, 4) * 4 + j, a))

    def merged(mine, others):
        top = functools.reduce(jnp.maximum, [t[:4] for t in others], mine[:4])
        total = mine[4:] * jnp.exp(mine[:4] - top)
        for t in others:
            total = total + t[4:] * jnp.exp(t[:4] - top)
        return top, total

    def stats_start(m):
        for d in (1, 2, 3):
            start(quad_copy(m, d))
        rowsend[m] = jnp.transpose(rowst[...])[:8]
        for d in (1, 3, 2):
            start(row_copy(m, d))

    def stats_middle(m):
        for d in (1, 2, 3):
            quad_copy(m, d).wait_recv()
        top, total = merged(colst[m], [quad_in[m, d] for d in range(3)])
        colq[m, 0:4, :] = top
        colq[m, 4:8, :] = total
        for d in (1, 3, 2):
            start(col_copy(m, d))

    def stats_finish(m):
        for d in (1, 3, 2):
            row_copy(m, d).wait_recv()
        mine = rowsend[m]
        top, total = merged(mine, [rowrecv[m, d] for d in range(3)])
        row_lse = top + jnp.log(total)
        rowtmp[0:4, :] = jnp.exp(mine[:4] - row_lse)
        rowfac[m] = jnp.transpose(rowtmp[...])
        for d in (1, 3, 2):
            col_copy(m, d).wait_recv()
        top, total = merged(colq[m], [colx_in[m, d] for d in range(3)])
        col_lse = top + jnp.log(total)
        colfac[m, 0:4, :] = jnp.exp(colst[m, 0:4, :] - col_lse)
        return row_lse, col_lse

    rowst[...] = jnp.ones_like(rowst)
    rowtmp[...] = jnp.zeros_like(rowtmp)
    img_start(1)
    text_start(1)
    text_start(0)
    is_[z] = simg[...]
    it[z] = timg[...]
    text_spread(1)
    img_pass_on(1)
    img_start(0)
    text_pass_on(1)
    text_spread(0)
    text_far(1)
    text_wait(1)

    scores(1, z, ps, qs, student_scale)
    img_recv(1, 0, 1)
    scores(1, zm1, ps, qs, student_scale)
    img_recv(1, 1, 0)
    scores(1, zp1, ps, qs, student_scale)
    img_recv_far(1, 0)
    img_recv_far(1, 1)
    scores(1, zp2, ps, qs, student_scale)
    stats_start(1)

    partner = (b, (1 - yh) * 4 + z)
    total_img = (
        is_[0].astype(F32) + is_[1].astype(F32) + is_[2].astype(F32) + is_[3].astype(F32)
    )
    for g in range(4):
        isum[0, g] = total_img[:HALF, g * 128 : (g + 1) * 128]
        isum[1, g] = total_img[HALF:, g * 128 : (g + 1) * 128]
    iy = copy(isum.at[1 - yh, z], isum_in.at[z], iy_s.at[0], iy_r.at[0], partner)
    start(iy)
    text_pass_on(0)
    stats_middle(1)
    img_pass_on(0)
    text_far(0)
    text_wait(0)
    scores(0, z, pt, qt, teacher_scale)
    img_recv(0, 0, 1)
    scores(0, zm1, pt, qt, teacher_scale)
    img_recv(0, 1, 0)
    scores(0, zp1, pt, qt, teacher_scale)
    img_recv_far(0, 0)
    img_recv_far(0, 1)
    scores(0, zp2, pt, qt, teacher_scale)
    stats_start(0)

    def iz_copy(d):
        slot = isum_in.at[z]
        return copy(slot, slot, iz_s.at[d - 1], iz_r.at[d - 1], znext(d))

    def iz_wait(d):
        slot = isum_in.at[lax.rem(z + 4 - d, 4)]
        copy(slot, slot, iz_s.at[d - 1], iz_r.at[d - 1], partner).wait_recv()

    iy.wait_recv()
    for d in (1, 3, 2):
        start(iz_copy(d))

    row_lse, col_lse = stats_finish(1)
    rl = lax.broadcasted_iota(jnp.int32, (4, 384), 0)
    cl = lax.broadcasted_iota(jnp.int32, (4, 384), 1)
    row_part = jnp.sum(jnp.where((rl == z) & (cl < ROWS), row_lse, 0.0), axis=0, keepdims=True)
    lse_part = (
        jnp.sum(row_part, axis=1, keepdims=True)
        + jnp.sum(jnp.sum(col_lse, axis=0, keepdims=True), axis=1, keepdims=True) * (1.0 / 16.0)
    )

    stats_middle(0)

    for d in (2, 1, 3, 0):
        v = lax.rem(z + d, 4)
        factor = jnp.sum(jnp.where(lane == v, rowfac[1, :ROWS, :], 0.0), axis=1, keepdims=True)
        w[v] = (ps[v] * factor + qs[v] * colfac[1, pl.ds(v, 1), :]).astype(BF16)
        gsend[d] = dot(w[v], ts[...], NN)

    def g_far(h):
        return copy(gsend.at[2, half(h)], gfar_in.at[h], g_s.at[2, h], g_r.at[2, h],
                    znext(1 if h == 0 else 3))

    def g_copy(i, h):
        d = 1 + 2 * i
        return copy(gsend.at[d, half(h)], grecv.at[i, half(h)], g_s.at[i, h], g_r.at[i, h],
                    znext(d))

    start(g_far(0))
    start(g_far(1))
    start(g_copy(0, 1))
    start(g_copy(1, 0))

    stats_finish(0)


    def tgt_copy(n):
        return copy(tgt.at[n], tgt_in.at[n], tgt_s.at[n], tgt_r.at[n], partner)

    def own_targets(h, n):
        rows = pl.ds(pl.multiple_of(h * HALF + n * 48, 16), 48)
        acc = None
        for v in range(4):
            term = pt[v, rows] * rowfac[0, rows, v : v + 1] + qt[v, rows] * colfac[0, v : v + 1, :]
            acc = term if acc is None else acc + term
        return acc

    for n in range(NCH):
        tgt[n] = own_targets(1 - yh, n)
        start(tgt_copy(n))
    acc = dot(w[0], is_[0], TN)
    for v in range(1, 4):
        acc = acc + dot(w[v], is_[v], TN)
    gtp[...] = acc
    for n in range(NCH):
        tgt_mine[n] = own_targets(yh, n)

    for d in (1, 3, 2):
        iz_wait(d)
    for g in range(4):
        isum8[g] = isum_in[g] + isum[yh, g]
    for g in range(4):
        t = isum8[g]
        hi[:, g * 128 : (g + 1) * 128] = t.astype(BF16)
        lo[:, g * 128 : (g + 1) * 128] = (t - t.astype(BF16).astype(F32)).astype(BF16)
    for i in range(2):
        g_far(i).wait_recv()
        rows = slice(i * HALF, (i + 1) * HALF)
        gsend[1 + 2 * i, rows] = gsend[1 + 2 * i, rows] + gfar_in[i]
        start(g_copy(i, i))

    for n in range(NCH):
        tgt_copy(n).wait_recv()
        tw[n * 48 : (n + 1) * 48] = ((tgt_mine[n] + tgt_in[n]) * 0.125).astype(BF16)
    target_text = dot(tw[...], ts[...], NN)
    for g in range(4):
        tt_part[g] = target_text[:, g * 128 : (g + 1) * 128]

    def tz_copy(d):
        return copy(tt_part.at[lax.rem(z + d, 4)], tt_in.at[d - 1], tz_s.at[d - 1],
                    tz_r.at[d - 1], znext(d))

    for d in (2, 1, 3):
        start(tz_copy(d))

    res = gtp[...] - dot(tw[...], hi[...], TN) - dot(tw[...], lo[...], TN)
    for s in range(8):
        row = s * HALF
        for g in range(4):
            gtc[s % 2, s // 2, g] = res[row : row + HALF, g * 128 : (g + 1) * 128]
    gc = copy(gtc.at[1 - k], gt_sib, gc_s.at[0], gc_r.at[0], sib)
    start(gc)

    target_loss = isum8[0] * tt_part[0]
    for g in range(1, 4):
        target_loss = target_loss + isum8[g] * tt_part[g]
    target_loss = jnp.sum(jnp.sum(target_loss, axis=0, keepdims=True), axis=1, keepdims=True)
    part = lse_part - target_loss * student_scale
    loss_src[...] = jnp.broadcast_to(part, (8, 128))

    def lb_copy(d):
        return copy(loss_src, loss_b.at[d - 1], lb_s.at[d - 1], lb_r.at[d - 1],
                    (lax.rem(b + d, 16), a))

    start_all(1, 16, lb_copy)

    gc.wait_recv()
    for blk in range(4):
        for g in range(4):
            gtc[k, blk, g] = gtc[k, blk, g] + gt_sib[blk, g]
    y = yh * 2 + yl
    pieces = gtc.at[k]

    def ydev(d):
        yd = lax.rem(y + d, 4)
        return dev(x, (yd % 2) * 2 + k, yd // 2, z)

    def xdev(d):
        return dev(lax.rem(x + d, 4), j, yh, z)

    def ra_copy(d):
        return copy(pieces.at[lax.rem(x + d, 4), :, 0:72, :], ra_in.at[d - 1],
                    rs_s.at[0, d - 1], rs_r.at[0, d - 1], xdev(d))

    def rb_copy(d):
        return copy(pieces.at[:, lax.rem(y + d, 4), 72:144, :], rb_in.at[d - 1],
                    rs_s.at[1, d - 1], rs_r.at[1, d - 1], ydev(d))

    def ra2_copy(d):
        return copy(ra_sum.at[lax.rem(y + d, 4)], ra2_in.at[d - 1],
                    rs_s.at[2, d - 1], rs_r.at[2, d - 1], ydev(d))

    def rb2_copy(d):
        return copy(rb_sum.at[lax.rem(x + d, 4)], rb2_in.at[d - 1],
                    rs_s.at[3, d - 1], rs_r.at[3, d - 1], xdev(d))

    for d in (1, 3, 2):
        start(ra_copy(d))
        start(rb_copy(d))

    total = tt_part[z]
    for d in (1, 3, 2):
        tz_copy(d).wait_recv()
        total = total + tt_in[d - 1]
    tt_src[...] = total

    a_in = (1 - yh) * 4 + z
    ty = copy(tt_src, tt_all.at[a], ta_s.at[0], ta_r.at[a], partner)
    start(ty)

    def ta_copy(d):
        return copy(tt_src, tt_all.at[a], ta_s.at[d], ta_r.at[a], znext(d))

    def tb_copy(d):
        return copy(tt_all.at[a_in], tt_all.at[a_in], ta_s.at[3 + d], ta_r.at[a_in], znext(d))

    def t_wait(slot):
        copy(tt_src, tt_all.at[slot], ta_s.at[0], ta_r.at[slot], partner).wait_recv()

    for d in (1, 3, 2):
        start(ta_copy(d))
    tt_all[a] = total

    def lb_wait(d, acc):
        lb_copy(d).wait_recv()
        return acc + loss_b[d - 1]

    loss_src2[...] = lax.fori_loop(1, 16, lb_wait, loss_src[...])

    def la_copy(d):
        return copy(loss_src2, loss_a.at[d - 1], la_s.at[d - 1], la_r.at[d - 1],
                    (b, lax.rem(a + d, 8)))

    start_all(1, 8, la_copy)

    ra_sum[...] = gtc[k, x, :, 0:72, :]
    rb_sum[...] = gtc[k, :, y, 72:144, :]
    for d in (1, 3, 2):
        ra_copy(d).wait_recv()
        ra_sum[...] = ra_sum[...] + ra_in[d - 1]
    for d in (1, 3, 2):
        start(ra2_copy(d))
    for d in (1, 3, 2):
        rb_copy(d).wait_recv()
        rb_sum[...] = rb_sum[...] + rb_in[d - 1]
    for d in (1, 3, 2):
        start(rb2_copy(d))
    t_wait(a_in)
    for d in (1, 3, 2):
        start(tb_copy(d))
    first, last = ra_sum[y], rb_sum[x]
    for d in (1, 3, 2):
        ra2_copy(d).wait_recv()
        first = first + ra2_in[d - 1]
    for d in (1, 3, 2):
        rb2_copy(d).wait_recv()
        last = last + rb2_in[d - 1]
    fb_src[0:72, :] = first * student_scale
    fb_src[72:144, :] = last * student_scale

    def fb_to(i):
        return (x * 4 + z, i)

    def fb_copy(i):
        return copy(fb_src, fb_buf.at[j * 2 + yh], fb_s.at[i], fb_r.at[j * 2 + yh], fb_to(i))

    def is_self(i):
        return (j == z) & (i == a)

    def fb_go(i, _):
        @pl.when(jnp.logical_not(is_self(i)))
        def _():
            fb_copy(i).start()

        return 0

    lax.fori_loop(0, 8, fb_go, 0)

    def fb_gone(i, _):
        @pl.when(jnp.logical_not(is_self(i)))
        def _():
            fb_copy(i).wait_send()

        return 0

    sent.append(lambda: lax.fori_loop(0, 8, fb_gone, 0))

    @pl.when(j == z)
    def _():
        fb_buf[j * 2 + yh] = fb_src[...]

    acc = gsend[0]
    for i in range(2):
        g_copy(i, 0).wait_recv()
        g_copy(i, 1).wait_recv()
        acc = acc + grecv[i]

    for d in (1, 3, 2):
        zd = lax.rem(z + d, 4)
        t_wait(yh * 4 + zd)
        t_wait((1 - yh) * 4 + zd)
    for h in range(2):
        rows = slice(h * HALF, (h + 1) * HALF)
        for g in range(4):
            lanes = slice(g * 128, (g + 1) * 128)
            gi_out[rows, lanes] = (acc[rows, lanes] - tt_all[h * 4 + g]) * student_scale

    def la_wait(d, acc):
        la_copy(d).wait_recv()
        return acc + loss_a[d - 1]

    loss_out[...] = lax.fori_loop(1, 8, la_wait, loss_src2[...]) * (1.0 / (2.0 * 8 * 4608))

    def fb_wait(s, _):
        mine = (z == j) & (s == j * 2 + yh)

        @pl.when(jnp.logical_not(mine))
        def _():
            copy(fb_src, fb_buf.at[s], fb_s.at[s], fb_r.at[s], sib).wait_recv()

        return 0

    lax.fori_loop(0, 8, fb_wait, 0)
    for s in range(8):
        syl_, sk_, syh_ = s // 4, (s // 2) % 2, s % 2
        g = syh_ * 2 + syl_
        gt_out[sk_ * HALF : (sk_ + 1) * HALF, g * 128 : (g + 1) * 128] = fb_buf[s]

    for gone in sent:
        gone()


def per_device(student_image, student_text, teacher_image, teacher_text):
    vm = pl.BlockSpec(memory_space=pltpu.VMEM)
    dma = pltpu.SemaphoreType.DMA
    V = pltpu.VMEM
    sw, twd = student_image.shape[2], teacher_image.shape[2]
    loss, gi, gt = pl.pallas_call(
        kernel,
        name="distill",
        out_shape=(
            jax.ShapeDtypeStruct((8, 128), F32),
            jax.ShapeDtypeStruct((ROWS, sw), F32),
            jax.ShapeDtypeStruct((ROWS, sw), F32),
        ),
        in_specs=[vm] * 4,
        out_specs=(vm, vm, vm),
        scratch_shapes=[
            V((4, ROWS, twd), BF16), V((4, ROWS, sw), BF16),
            V((4 * ROWS, twd), BF16), V((4 * ROWS, sw), BF16),
            V((4, ROWS, COLS), F32), V((4, ROWS, COLS), F32),
            V((4, ROWS, COLS), F32), V((4, ROWS, COLS), F32),
            V((4, ROWS, COLS), BF16),
            V((NCH, 48, COLS), F32), V((NCH, 48, COLS), F32), V((NCH, 48, COLS), F32),
            V((HALF, COLS), BF16),
            V((2, 4, HALF, 128), F32), V((4, HALF, 128), F32), V((4, HALF, 128), F32),
            V((HALF, sw), BF16), V((HALF, sw), BF16),
            V((4, HALF, 128), F32), V((3, HALF, 128), F32), V((HALF, 128), F32),
            V((8, HALF, 128), F32),
            V((4, ROWS, sw), F32), V((2, ROWS, sw), F32), V((2, HALF, sw), F32),
            V((COLS, sw), F32), V((4, 4, HALF, 128), F32),
            V((3, 4, 72, 128), F32), V((3, 4, 72, 128), F32), V((4, 72, 128), F32),
            V((4, 72, 128), F32), V((3, 72, 128), F32), V((3, 72, 128), F32),
            V((HALF, 128), F32), V((8, HALF, 128), F32),
            V((2, 4, 4, HALF, 128), F32),
            V((384, 128), F32), V((2, 8, 384), F32), V((2, 3, 8, 384), F32),
            V((2, 384, 128), F32), V((128, 384), F32),
            V((2, 8, COLS), F32), V((2, 3, 8, COLS), F32), V((2, 8, COLS), F32),
            V((2, 3, 8, COLS), F32), V((2, 8, COLS), F32),
            V((8, 128), F32), V((15, 8, 128), F32), V((8, 128), F32), V((7, 8, 128), F32),
            dma((2, 3, 2)), dma((2, 3, 2)),
            dma((2, 3)), dma((2,)), dma((2, 3)), dma((2, 3)), dma((2, 4)), dma((2, 4)),
            dma((2, 2)), dma((2, 2)),
            dma((1,)), dma((1,)), dma((3,)), dma((3,)), dma((3,)), dma((3,)), dma((7,)), dma((8,)),
            dma((2, 3)), dma((2, 3)), dma((2, 3)), dma((2, 3)), dma((2, 3)), dma((2, 3)),
            dma((3,)), dma((3,)), dma((3, 2)), dma((3, 2)), dma((1,)), dma((1,)),
            dma((4, 3)), dma((4, 3)), dma((8,)), dma((8,)),
            dma((15,)), dma((15,)), dma((7,)), dma((7,)),
        ],
        compiler_params=pltpu.CompilerParams(
            collective_id=0, has_side_effects=True, vmem_limit_bytes=60 * 1024 * 1024
        ),
        cost_estimate=pl.CostEstimate(
            flops=8 * 10**9, bytes_accessed=4 * 2**20, transcendentals=6 * 10**6
        ),
    )(student_image[0], student_text, teacher_image[0], teacher_text)
    return loss[0, 0], gi[None], gt


def solution(mesh):
    return jax.shard_map(
        per_device,
        mesh=mesh,
        in_specs=(
            P("aug", "batch", None),
            P("batch", None),
            P("aug", "batch", None),
            P("batch", None),
        ),
        out_specs=(P(), P("aug", "batch", None), P("batch", None)),
        check_vma=False,
    )
```

```python
import functools
import math

import jax
import jax.numpy as jnp
from jax import lax
from jax.experimental import pallas as pl
from jax.experimental.pallas import tpu as pltpu
from jax.sharding import PartitionSpec as P

MESH = pl.DeviceIdType.MESH
F32 = jnp.float32
BF16 = jnp.bfloat16
ROWS = 288
HALF = ROWS // 2
COLS = 4 * ROWS
NCH = 3
NT = (((1,), (1,)), ((), ()))
NN = (((1,), (0,)), ((), ()))
TN = (((0,), (0,)), ((), ()))


def dot(a, b, dims):
    return lax.dot_general(a, b, dims, preferred_element_type=F32)


def kernel(
    simg, stext, timg, ttext,
    loss_out, grads_out,
    it, is_, tt, ts, pt, qt, ps, qs, w, tgt, tgt_mine, tgt_in, tw,
    isum, isum_in, isum8, hi, lo, tt_part, tt_in, tt_src, tt_all,
    gsend, grecv, gfar_in, gtp, gt_sib, ra_in, rb_in, ra_sum, rb_sum, ra2_in, rb2_in, fb_src, fb_buf, gtc,
    rowst, rowsend, rowrecv, rowfac, rowtmp, colst, quad_in, colq, colx_in, colfac,
    loss_src, loss_b, loss_src2, loss_a,
    zi_s, zi_r, t1_s, t1_r, t2_s, t2_r, t3_s, t3_r, t4_s, t4_r,
    iy_s, iy_r, iz_s, iz_r, tz_s, tz_r, ta_s, ta_r,
    quad_s, quad_r, row_s, row_r, col_s, col_r, tgt_s, tgt_r, g_s, g_r, gc_s, gc_r,
    rs_s, rs_r, fz_s, fz_r, fb_s, fb_r, lb_s, lb_r, la_s, la_r,
):
    b = lax.axis_index("batch")
    a = lax.axis_index("aug")
    x, j = b // 4, b % 4
    yl, k = j // 2, j % 2
    yh, z = a // 4, a % 4
    sib = (b + 1 - 2 * k, a)
    teacher_scale = 3.0 / math.sqrt(timg.shape[1])
    student_scale = 3.0 / math.sqrt(simg.shape[1])

    def dev(x_, j_, yh_, z_):
        return (x_ * 4 + j_, yh_ * 4 + z_)

    def znext(d):
        return (b, yh * 4 + lax.rem(z + d, 4))

    def copy(src, dst, ss, rs, to):
        return pltpu.make_async_remote_copy(
            src_ref=src, dst_ref=dst, send_sem=ss, recv_sem=rs, device_id=to, device_id_type=MESH
        )

    sent = []

    def start(c):
        c.start()
        sent.append(c.wait_send)

    def start_all(lo, hi, make):
        def go(i, _):
            make(i).start()
            return 0

        def gone(i, _):
            make(i).wait_send()
            return 0

        lax.fori_loop(lo, hi, go, 0)
        sent.append(lambda: lax.fori_loop(lo, hi, gone, 0))

    barrier = pltpu.get_barrier_semaphore()

    near = [(b, yh * 4 + lax.rem(z + d, 4)) for d in (1, 2, 3)]
    near += [(lax.rem(x + d, 4) * 4 + j, a) for d in (1, 2, 3)]
    near += [(x * 4 + lax.rem(j + d, 4), a) for d in (1, 2, 3)]
    near += [(x * 4 + lax.rem(j + d, 4), (1 - yh) * 4 + z) for d in range(4)]
    for peer in near:
        pl.semaphore_signal(barrier, 1, device_id=peer, device_id_type=MESH)
    pl.semaphore_wait(barrier, len(near))

    zm1, zp1, zp2 = lax.rem(z + 3, 4), lax.rem(z + 1, 4), lax.rem(z + 2, 4)
    own = (timg, simg)
    imgs = (it, is_)
    texts = (tt, ts)
    own_text = (ttext, stext)

    def half(h):
        return pl.ds(h * HALF, HALF)

    def img_send(m, d, h):
        return copy(
            own[m].at[half(h)], imgs[m].at[z, half(h)], zi_s.at[m, d, h], zi_r.at[m, d, h],
            znext(1 if d == 0 else 3),
        )

    def img_relay(m, d):
        slot = zm1 if d == 0 else zp1
        ref = imgs[m].at[slot, half(d)]
        return copy(ref, ref, zi_s.at[m, 2, d], zi_r.at[m, 2, d], znext(1 if d == 0 else 3))

    def img_recv(m, d, h):
        slot = zm1 if d == 0 else zp1
        ref = imgs[m].at[slot, half(h)]
        copy(ref, ref, zi_s.at[m, d, h], zi_r.at[m, d, h], znext(1)).wait_recv()

    def img_recv_far(m, d):
        ref = imgs[m].at[zp2, half(d)]
        copy(ref, ref, zi_s.at[m, 2, d], zi_r.at[m, 2, d], znext(1)).wait_recv()

    def img_start(m):
        start(img_send(m, 0, 0))
        start(img_send(m, 1, 1))

    def img_rest(m):
        start(img_send(m, 0, 1))
        start(img_send(m, 1, 0))

    def img_pass_on(m):
        img_recv(m, 0, 0)
        start(img_relay(m, 0))
        img_recv(m, 1, 1)
        start(img_relay(m, 1))

    syl, sk = z // 2, z % 2
    is_source = j == z

    def tslab(m, blk, h):
        return texts[m].at[pl.ds(blk * ROWS + h * HALF, HALF)]

    def text_first(m):
        return (
            copy(own_text[m].at[pl.ds((1 - sk) * HALF, HALF)], tslab(m, x, 1 - sk),
                 t1_s.at[m, 0], t1_r.at[m], dev(x, syl * 2 + 1 - sk, yh, z)),
            copy(own_text[m].at[half(0)], tslab(m, x, 0),
                 t1_s.at[m, 1], t1_r.at[m], dev(x, (1 - syl) * 2, yh, z)),
            copy(own_text[m].at[half(1)], tslab(m, x, 1),
                 t1_s.at[m, 2], t1_r.at[m], dev(x, (1 - syl) * 2 + 1, 1 - yh, z)),
        )

    def text_start(m):
        @pl.when(is_source)
        def _():
            for c in text_first(m):
                c.start()
            tslab(m, x, k)[...] = own_text[m][pl.ds(k * HALF, HALF)]

        def gone():
            @pl.when(is_source)
            def _():
                for c in text_first(m):
                    c.wait_send()

        sent.append(gone)

    def text_x(m, d):
        return copy(tslab(m, x, k), tslab(m, x, k), t2_s.at[m, d - 1], t2_r.at[m, d - 1],
                    (lax.rem(x + d, 4) * 4 + j, a))

    def text_got(m, d):
        slab = tslab(m, lax.rem(x + 4 - d, 4), k)
        copy(slab, slab, t2_s.at[m, d - 1], t2_r.at[m, d - 1], sib).wait_recv()

    def tlanes(m, blk, i):
        width = texts[m].shape[1] // 2
        return texts[m].at[pl.ds(blk * ROWS + k * HALF, HALF), i * width : (i + 1) * width]

    def text_relay(m, i):
        ref = tlanes(m, lax.rem(x + 3 - 2 * i, 4), i)
        return copy(ref, ref, t4_s.at[m, i], t4_r.at[m, i], (lax.rem(x + 1 + 2 * i, 4) * 4 + j, a))

    def text_sib(m, d):
        blk = lax.rem(x + 4 - d, 4)
        return copy(tslab(m, blk, k), tslab(m, blk, k), t3_s.at[m, d], t3_r.at[m, d], sib)

    def text_spread(m):
        @pl.when(jnp.logical_not(is_source))
        def _():
            copy(tslab(m, x, k), tslab(m, x, k), t1_s.at[m, 0], t1_r.at[m], sib).wait_recv()

        for d in (1, 3):
            start(text_x(m, d))
        start(text_sib(m, 0))

    def text_pass_on(m):
        for d in (1, 3):
            text_got(m, d)
            start(text_relay(m, d // 2))
            start(text_sib(m, d))

    def text_far(m):
        for i in range(2):
            ref = tlanes(m, lax.rem(x + 2, 4), i)
            copy(ref, ref, t4_s.at[m, i], t4_r.at[m, i], sib).wait_recv()
        start(text_sib(m, 2))

    def text_wait(m):
        for d in range(4):
            blk = lax.rem(x + 4 - d, 4)
            copy(tslab(m, blk, 1 - k), tslab(m, blk, 1 - k), t3_s.at[m, d], t3_r.at[m, d],
                 sib).wait_recv()

    lane = lax.broadcasted_iota(jnp.int32, (ROWS, 128), 1)

    def fold(op, t):
        return functools.reduce(op, [t[:, i * 128 : (i + 1) * 128] for i in range(COLS // 128)])

    def scores(m, v, pr, qr, scale):
        t = dot(imgs[m][v], texts[m][...], NT) * scale
        cm = jnp.max(t, axis=0, keepdims=True)
        top = jnp.max(fold(jnp.maximum, t), axis=1, keepdims=True)
        q = jnp.exp(t - cm)
        qr[v] = q
        p = jnp.exp(t - top)
        pr[v] = p
        colst[m, pl.ds(v, 1), :] = cm
        colst[m, pl.ds(v + 4, 1), :] = jnp.sum(q, axis=0, keepdims=True)
        total = jnp.sum(fold(jnp.add, p), axis=1, keepdims=True)
        rowst[:ROWS, :] = jnp.where(
            lane == v, top, jnp.where(lane == v + 4, total, rowst[:ROWS, :])
        )

    def row_copy(m, d):
        return copy(rowsend.at[m], rowrecv.at[m, d - 1], row_s.at[m, d - 1], row_r.at[m, d - 1],
                    znext(d))

    def quad_copy(m, d):
        return copy(colst.at[m], quad_in.at[m, d - 1], quad_s.at[m, d - 1], quad_r.at[m, d - 1],
                    (x * 4 + lax.rem(j + d, 4), a))

    def col_copy(m, d):
        return copy(colq.at[m], colx_in.at[m, d - 1], col_s.at[m, d - 1], col_r.at[m, d - 1],
                    (lax.rem(x + d, 4) * 4 + j, a))

    def merged(mine, others):
        top = functools.reduce(jnp.maximum, [t[:4] for t in others], mine[:4])
        total = mine[4:] * jnp.exp(mine[:4] - top)
        for t in others:
            total = total + t[4:] * jnp.exp(t[:4] - top)
        return top, total

    def stats_start(m):
        for d in (1, 2, 3):
            start(quad_copy(m, d))
        rowsend[m] = jnp.transpose(rowst[...])[:8]
        for d in (1, 3, 2):
            start(row_copy(m, d))

    def stats_middle(m):
        for d in (1, 2, 3):
            quad_copy(m, d).wait_recv()
        top, total = merged(colst[m], [quad_in[m, d] for d in range(3)])
        colq[m, 0:4, :] = top
        colq[m, 4:8, :] = total
        for d in (1, 3, 2):
            start(col_copy(m, d))

    def stats_finish(m):
        for d in (1, 3, 2):
            row_copy(m, d).wait_recv()
        mine = rowsend[m]
        top, total = merged(mine, [rowrecv[m, d] for d in range(3)])
        row_lse = top + jnp.log(total)
        rowtmp[0:4, :] = jnp.exp(mine[:4] - row_lse)
        rowfac[m] = jnp.transpose(rowtmp[...])
        for d in (1, 3, 2):
            col_copy(m, d).wait_recv()
        top, total = merged(colq[m], [colx_in[m, d] for d in range(3)])
        col_lse = top + jnp.log(total)
        colfac[m, 0:4, :] = jnp.exp(colst[m, 0:4, :] - col_lse)
        return row_lse, col_lse

    rowst[...] = jnp.ones_like(rowst)
    rowtmp[...] = jnp.zeros_like(rowtmp)
    img_start(1)
    img_rest(1)
    text_start(1)
    img_start(0)
    text_start(0)
    is_[z] = simg[...]
    it[z] = timg[...]
    text_spread(1)
    img_pass_on(1)
    img_rest(0)
    text_pass_on(1)
    text_spread(0)
    text_far(1)
    text_wait(1)

    scores(1, z, ps, qs, student_scale)
    img_recv(1, 0, 1)
    scores(1, zm1, ps, qs, student_scale)
    img_recv(1, 1, 0)
    scores(1, zp1, ps, qs, student_scale)
    img_pass_on(0)
    text_pass_on(0)
    img_recv_far(1, 0)
    img_recv_far(1, 1)
    scores(1, zp2, ps, qs, student_scale)
    stats_start(1)

    partner = (b, (1 - yh) * 4 + z)
    total_img = (
        is_[0].astype(F32) + is_[1].astype(F32) + is_[2].astype(F32) + is_[3].astype(F32)
    )
    for g in range(4):
        isum[0, g] = total_img[:HALF, g * 128 : (g + 1) * 128]
        isum[1, g] = total_img[HALF:, g * 128 : (g + 1) * 128]
    iy = copy(isum.at[1 - yh, z], isum_in.at[z], iy_s.at[0], iy_r.at[0], partner)
    start(iy)
    text_far(0)
    text_wait(0)

    scores(0, z, pt, qt, teacher_scale)
    stats_middle(1)
    img_recv(0, 0, 1)
    scores(0, zm1, pt, qt, teacher_scale)
    img_recv(0, 1, 0)
    scores(0, zp1, pt, qt, teacher_scale)
    img_recv_far(0, 0)
    img_recv_far(0, 1)
    scores(0, zp2, pt, qt, teacher_scale)
    stats_start(0)

    def iz_copy(d):
        slot = isum_in.at[z]
        return copy(slot, slot, iz_s.at[d - 1], iz_r.at[d - 1], znext(d))

    def iz_wait(d):
        slot = isum_in.at[lax.rem(z + 4 - d, 4)]
        copy(slot, slot, iz_s.at[d - 1], iz_r.at[d - 1], partner).wait_recv()

    iy.wait_recv()
    for d in (1, 3, 2):
        start(iz_copy(d))

    row_lse, col_lse = stats_finish(1)
    rl = lax.broadcasted_iota(jnp.int32, (4, 384), 0)
    cl = lax.broadcasted_iota(jnp.int32, (4, 384), 1)
    row_part = jnp.sum(jnp.where((rl == z) & (cl < ROWS), row_lse, 0.0), axis=0, keepdims=True)
    lse_part = (
        jnp.sum(row_part, axis=1, keepdims=True)
        + jnp.sum(jnp.sum(col_lse, axis=0, keepdims=True), axis=1, keepdims=True) * (1.0 / 16.0)
    )

    for d in (2, 1, 3, 0):
        v = lax.rem(z + d, 4)
        factor = jnp.sum(jnp.where(lane == v, rowfac[1, :ROWS, :], 0.0), axis=1, keepdims=True)
        w[v] = (ps[v] * factor + qs[v] * colfac[1, pl.ds(v, 1), :]).astype(BF16)
        gsend[d] = dot(w[v], ts[...], NN)

    def g_far(h):
        return copy(gsend.at[2, half(h)], gfar_in.at[h], g_s.at[2, h], g_r.at[2, h],
                    znext(1 if h == 0 else 3))

    def g_copy(i, h):
        d = 1 + 2 * i
        return copy(gsend.at[d, half(h)], grecv.at[i, half(h)], g_s.at[i, h], g_r.at[i, h],
                    znext(d))

    start(g_far(0))
    start(g_far(1))
    start(g_copy(0, 1))
    start(g_copy(1, 0))

    stats_middle(0)

    acc = dot(w[0], is_[0], TN)
    for v in range(1, 4):
        acc = acc + dot(w[v], is_[v], TN)
    gtp[...] = acc

    stats_finish(0)


    def tgt_copy(n):
        return copy(tgt.at[n], tgt_in.at[n], tgt_s.at[n], tgt_r.at[n], partner)

    def own_targets(h, n):
        rows = pl.ds(pl.multiple_of(h * HALF + n * 48, 16), 48)
        acc = None
        for v in range(4):
            term = pt[v, rows] * rowfac[0, rows, v : v + 1] + qt[v, rows] * colfac[0, v : v + 1, :]
            acc = term if acc is None else acc + term
        return acc

    for n in range(NCH):
        tgt[n] = own_targets(1 - yh, n)
        start(tgt_copy(n))
    for n in range(NCH):
        tgt_mine[n] = own_targets(yh, n)

    for d in (1, 3, 2):
        iz_wait(d)
    for g in range(4):
        isum8[g] = isum_in[g] + isum[yh, g]
    for g in range(4):
        t = isum8[g]
        hi[:, g * 128 : (g + 1) * 128] = t.astype(BF16)
        lo[:, g * 128 : (g + 1) * 128] = (t - t.astype(BF16).astype(F32)).astype(BF16)
    for i in range(2):
        g_far(i).wait_recv()
        rows = slice(i * HALF, (i + 1) * HALF)
        gsend[1 + 2 * i, rows] = gsend[1 + 2 * i, rows] + gfar_in[i]
        start(g_copy(i, i))

    for n in range(NCH):
        tgt_copy(n).wait_recv()
        tw[n * 48 : (n + 1) * 48] = ((tgt_mine[n] + tgt_in[n]) * 0.125).astype(BF16)
    target_text = dot(tw[...], ts[...], NN)
    for g in range(4):
        tt_part[g] = target_text[:, g * 128 : (g + 1) * 128]

    def tz_copy(d):
        return copy(tt_part.at[lax.rem(z + d, 4)], tt_in.at[d - 1], tz_s.at[d - 1],
                    tz_r.at[d - 1], znext(d))

    for d in (2, 1, 3):
        start(tz_copy(d))

    res = gtp[...] - dot(tw[...], hi[...], TN) - dot(tw[...], lo[...], TN)
    for s in range(8):
        row = s * HALF
        for g in range(4):
            gtc[s % 2, s // 2, g] = res[row : row + HALF, g * 128 : (g + 1) * 128]
    def gc_copy(i):
        rows = slice(i * 72, (i + 1) * 72)
        return copy(gtc.at[1 - k, :, :, rows, :], gt_sib.at[:, :, rows, :], gc_s.at[i],
                    gc_r.at[i], sib)

    start(gc_copy(0))
    start(gc_copy(1))

    target_loss = isum8[0] * tt_part[0]
    for g in range(1, 4):
        target_loss = target_loss + isum8[g] * tt_part[g]
    target_loss = jnp.sum(jnp.sum(target_loss, axis=0, keepdims=True), axis=1, keepdims=True)
    part = lse_part - target_loss * student_scale
    loss_src[...] = jnp.broadcast_to(part, (8, 128))

    def lb_copy(d):
        return copy(loss_src, loss_b.at[d - 1], lb_s.at[d - 1], lb_r.at[d - 1],
                    (lax.rem(b + d, 16), a))

    start_all(1, 16, lb_copy)

    y = yh * 2 + yl
    pieces = gtc.at[k]

    def ydev(d):
        yd = lax.rem(y + d, 4)
        return dev(x, (yd % 2) * 2 + k, yd // 2, z)

    def xdev(d):
        return dev(lax.rem(x + d, 4), j, yh, z)

    def ra_copy(d):
        return copy(pieces.at[lax.rem(x + d, 4), :, 0:72, :], ra_in.at[d - 1],
                    rs_s.at[0, d - 1], rs_r.at[0, d - 1], xdev(d))

    def rb_copy(d):
        return copy(pieces.at[:, lax.rem(y + d, 4), 72:144, :], rb_in.at[d - 1],
                    rs_s.at[1, d - 1], rs_r.at[1, d - 1], ydev(d))

    def ra2_copy(d):
        return copy(ra_sum.at[lax.rem(y + d, 4)], ra2_in.at[d - 1],
                    rs_s.at[2, d - 1], rs_r.at[2, d - 1], ydev(d))

    def rb2_copy(d):
        return copy(rb_sum.at[lax.rem(x + d, 4)], rb2_in.at[d - 1],
                    rs_s.at[3, d - 1], rs_r.at[3, d - 1], xdev(d))

    for i in range(2):
        gc_copy(i).wait_recv()
        rows = slice(i * 72, (i + 1) * 72)
        for blk in range(4):
            for g in range(4):
                gtc[k, blk, g, rows, :] = gtc[k, blk, g, rows, :] + gt_sib[blk, g, rows, :]
        for d in ((1, 3, 2), (1, 3))[i]:
            start((ra_copy, rb_copy)[i](d))

    total = tt_part[z]
    for d in (1, 3, 2):
        tz_copy(d).wait_recv()
        total = total + tt_in[d - 1]
    tt_src[...] = total

    a_in = (1 - yh) * 4 + z
    ty = copy(tt_src, tt_all.at[a], ta_s.at[0], ta_r.at[a], partner)
    start(ty)
    start(rb_copy(2))

    def ta_copy(d):
        return copy(tt_src, tt_all.at[a], ta_s.at[d], ta_r.at[a], znext(d))

    def tb_copy(d):
        return copy(tt_all.at[a_in], tt_all.at[a_in], ta_s.at[3 + d], ta_r.at[a_in], znext(d))

    def t_wait(slot):
        copy(tt_src, tt_all.at[slot], ta_s.at[0], ta_r.at[slot], partner).wait_recv()

    for d in (1, 3, 2):
        start(ta_copy(d))
    tt_all[a] = total

    def lb_wait(d, acc):
        lb_copy(d).wait_recv()
        return acc + loss_b[d - 1]

    loss_src2[...] = lax.fori_loop(1, 16, lb_wait, loss_src[...])

    def la_copy(d):
        return copy(loss_src2, loss_a.at[d - 1], la_s.at[d - 1], la_r.at[d - 1],
                    (b, lax.rem(a + d, 8)))

    start_all(1, 8, la_copy)

    ra_sum[...] = gtc[k, x, :, 0:72, :]
    rb_sum[...] = gtc[k, :, y, 72:144, :]
    for d in (1, 3, 2):
        ra_copy(d).wait_recv()
        ra_sum[...] = ra_sum[...] + ra_in[d - 1]
    for d in (1, 3, 2):
        start(ra2_copy(d))
    for d in (1, 3, 2):
        rb_copy(d).wait_recv()
        rb_sum[...] = rb_sum[...] + rb_in[d - 1]
    for d in (1, 3, 2):
        start(rb2_copy(d))
    t_wait(a_in)
    for d in (1, 3, 2):
        start(tb_copy(d))
    first, last = ra_sum[y], rb_sum[x]
    for d in (1, 3, 2):
        ra2_copy(d).wait_recv()
        first = first + ra2_in[d - 1]
    for d in (1, 3, 2):
        rb2_copy(d).wait_recv()
        last = last + rb2_in[d - 1]
    fb_src[z, 0:72, :] = first
    fb_src[z, 72:144, :] = last

    def fz_copy(d):
        return copy(fb_src.at[z], fb_src.at[z], fz_s.at[d - 1], fz_r.at[d - 1], znext(d))

    def fb_copy(c, h):
        return copy(fb_src.at[c], fb_buf.at[j * 2 + yh], fb_s.at[c, h], fb_r.at[j * 2 + yh],
                    dev(x, c, h, z))

    def is_self(c, h):
        return (j == c) & (yh == h)

    def fb_send(c):
        for h in range(2):
            @pl.when(jnp.logical_not(is_self(c, h)))
            def _():
                fb_copy(c, h).start()

    def fb_gone():
        for c in range(4):
            for h in range(2):
                @pl.when(jnp.logical_not(is_self(c, h)))
                def _():
                    fb_copy(c, h).wait_send()

    sent.append(fb_gone)
    for d in (1, 3, 2):
        start(fz_copy(d))
    fb_send(z)
    for d in (1, 3, 2):
        c = lax.rem(z + 4 - d, 4)
        copy(fb_src.at[c], fb_src.at[c], fz_s.at[d - 1], fz_r.at[d - 1], partner).wait_recv()
        fb_send(c)
    fb_buf[j * 2 + yh] = fb_src[j]

    acc = gsend[0]
    for i in range(2):
        g_copy(i, 0).wait_recv()
        g_copy(i, 1).wait_recv()
        acc = acc + grecv[i]

    for d in (1, 3, 2):
        zd = lax.rem(z + d, 4)
        t_wait(yh * 4 + zd)
        t_wait((1 - yh) * 4 + zd)
    for h in range(2):
        rows = slice(h * HALF, (h + 1) * HALF)
        for g in range(4):
            lanes = slice(g * 128, (g + 1) * 128)
            grads_out[0, rows, lanes] = acc[rows, lanes] - tt_all[h * 4 + g]

    def la_wait(d, acc):
        la_copy(d).wait_recv()
        return acc + loss_a[d - 1]

    whole = lax.fori_loop(1, 8, la_wait, loss_src2[...])
    loss_out[0, 0] = jnp.sum(whole[0:1, 0:1]) * (1.0 / (2.0 * 8 * 4608))

    def fb_wait(s, _):
        @pl.when(s != j * 2 + yh)
        def _():
            copy(fb_src.at[0], fb_buf.at[s], fb_s.at[0, 0], fb_r.at[s], partner).wait_recv()

        return 0

    lax.fori_loop(0, 8, fb_wait, 0)
    for s in range(8):
        syl_, sk_, syh_ = s // 4, (s // 2) % 2, s % 2
        g = syh_ * 2 + syl_
        grads_out[1, sk_ * HALF : (sk_ + 1) * HALF, g * 128 : (g + 1) * 128] = fb_buf[s]

    for gone in sent:
        gone()


def per_device(student_image, student_text, teacher_image, teacher_text):
    vm = pl.BlockSpec(memory_space=pltpu.VMEM)
    dma = pltpu.SemaphoreType.DMA
    V = pltpu.VMEM
    sw, twd = student_image.shape[2], teacher_image.shape[2]
    loss, grads = pl.pallas_call(
        kernel,
        name="distill",
        out_shape=(
            jax.ShapeDtypeStruct((1, 1), F32),
            jax.ShapeDtypeStruct((2, ROWS, sw), F32),
        ),
        in_specs=[vm] * 4,
        out_specs=(pl.BlockSpec(memory_space=pltpu.SMEM), vm),
        scratch_shapes=[
            V((4, ROWS, twd), BF16), V((4, ROWS, sw), BF16),
            V((4 * ROWS, twd), BF16), V((4 * ROWS, sw), BF16),
            V((4, ROWS, COLS), F32), V((4, ROWS, COLS), F32),
            V((4, ROWS, COLS), F32), V((4, ROWS, COLS), F32),
            V((4, ROWS, COLS), BF16),
            V((NCH, 48, COLS), F32), V((NCH, 48, COLS), F32), V((NCH, 48, COLS), F32),
            V((HALF, COLS), BF16),
            V((2, 4, HALF, 128), F32), V((4, HALF, 128), F32), V((4, HALF, 128), F32),
            V((HALF, sw), BF16), V((HALF, sw), BF16),
            V((4, HALF, 128), F32), V((3, HALF, 128), F32), V((HALF, 128), F32),
            V((8, HALF, 128), F32),
            V((4, ROWS, sw), F32), V((2, ROWS, sw), F32), V((2, HALF, sw), F32),
            V((COLS, sw), F32), V((4, 4, HALF, 128), F32),
            V((3, 4, 72, 128), F32), V((3, 4, 72, 128), F32), V((4, 72, 128), F32),
            V((4, 72, 128), F32), V((3, 72, 128), F32), V((3, 72, 128), F32),
            V((4, HALF, 128), F32), V((8, HALF, 128), F32),
            V((2, 4, 4, HALF, 128), F32),
            V((384, 128), F32), V((2, 8, 384), F32), V((2, 3, 8, 384), F32),
            V((2, 384, 128), F32), V((128, 384), F32),
            V((2, 8, COLS), F32), V((2, 3, 8, COLS), F32), V((2, 8, COLS), F32),
            V((2, 3, 8, COLS), F32), V((2, 8, COLS), F32),
            V((8, 128), F32), V((15, 8, 128), F32), V((8, 128), F32), V((7, 8, 128), F32),
            dma((2, 3, 2)), dma((2, 3, 2)),
            dma((2, 3)), dma((2,)), dma((2, 3)), dma((2, 3)), dma((2, 4)), dma((2, 4)),
            dma((2, 2)), dma((2, 2)),
            dma((1,)), dma((1,)), dma((3,)), dma((3,)), dma((3,)), dma((3,)), dma((7,)), dma((8,)),
            dma((2, 3)), dma((2, 3)), dma((2, 3)), dma((2, 3)), dma((2, 3)), dma((2, 3)),
            dma((3,)), dma((3,)), dma((3, 2)), dma((3, 2)), dma((2,)), dma((2,)),
            dma((4, 3)), dma((4, 3)), dma((3,)), dma((3,)), dma((4, 2)), dma((8,)),
            dma((15,)), dma((15,)), dma((7,)), dma((7,)),
        ],
        compiler_params=pltpu.CompilerParams(
            collective_id=0, has_side_effects=True, vmem_limit_bytes=60 * 1024 * 1024
        ),
        cost_estimate=pl.CostEstimate(
            flops=8 * 10**9, bytes_accessed=4 * 2**20, transcendentals=6 * 10**6
        ),
    )(student_image[0], student_text, teacher_image[0], teacher_text)
    scale = 3.0 / math.sqrt(sw)
    return loss.reshape(()), (grads[0] * scale)[None], grads[1] * scale


def solution(mesh):
    return jax.shard_map(
        per_device,
        mesh=mesh,
        in_specs=(
            P("aug", "batch", None),
            P("batch", None),
            P("aug", "batch", None),
            P("batch", None),
        ),
        out_specs=(P(), P("aug", "batch", None), P("batch", None)),
        check_vma=False,
    )
```

```python
import functools
import math

import jax
import jax.numpy as jnp
from jax import lax
from jax.experimental import pallas as pl
from jax.experimental.pallas import tpu as pltpu
from jax.sharding import PartitionSpec as P

MESH = pl.DeviceIdType.MESH
F32 = jnp.float32
BF16 = jnp.bfloat16
ROWS = 288
HALF = ROWS // 2
COLS = 4 * ROWS
NCH = 3
NT = (((1,), (1,)), ((), ()))
NN = (((1,), (0,)), ((), ()))
TN = (((0,), (0,)), ((), ()))


def dot(a, b, dims):
    return lax.dot_general(a, b, dims, preferred_element_type=F32)


def kernel(
    simg, stext, timg, ttext,
    loss_out, grads_out,
    it, is_, tt, ts, pt, qt, ps, qs, w, tgt, tgt_mine, tgt_in, tw,
    isum, isum_in, isum8, hi, lo, tt_part, tt_in, tt_src, tt_all,
    gsend, grecv, gfar_in, gtp, gt_sib, ra_in, rb_in, ra_sum, rb_sum, ra2_in, rb2_in, fb_src, fb_buf, gtc,
    rowst, rowsend, rowrecv, rowfac, rowtmp, colst, quad_in, colq, colx_in, colfac, cfar, cfar_in,
    loss_src, loss_b, loss_src2, loss_a,
    zi_s, zi_r, t1_s, t1_r, t2_s, t2_r, t3_s, t3_r, t4_s, t4_r, t5_s, t5_r,
    iy_s, iy_r, iz_s, iz_r, tz_s, tz_r, ta_s, ta_r,
    far_s, far_r, quad_s, quad_r, row_s, row_r, col_s, col_r, tgt_s, tgt_r, g_s, g_r, gc_s, gc_r,
    rs_s, rs_r, fz_s, fz_r, fb_s, fb_r, lb_s, lb_r, la_s, la_r,
):
    b = lax.axis_index("batch")
    a = lax.axis_index("aug")
    x, j = b // 4, b % 4
    yl, k = j // 2, j % 2
    yh, z = a // 4, a % 4
    sib = (b + 1 - 2 * k, a)
    teacher_scale = 3.0 / math.sqrt(timg.shape[1])
    student_scale = 3.0 / math.sqrt(simg.shape[1])

    def dev(x_, j_, yh_, z_):
        return (x_ * 4 + j_, yh_ * 4 + z_)

    def znext(d):
        return (b, yh * 4 + lax.rem(z + d, 4))

    def copy(src, dst, ss, rs, to):
        return pltpu.make_async_remote_copy(
            src_ref=src, dst_ref=dst, send_sem=ss, recv_sem=rs, device_id=to, device_id_type=MESH
        )

    sent = []

    def start(c):
        c.start()
        sent.append(c.wait_send)

    def start_if(cond, c):
        @pl.when(cond)
        def _():
            c.start()

        def gone():
            @pl.when(cond)
            def _():
                c.wait_send()

        sent.append(gone)

    def start_all(lo, hi, make):
        def go(i, _):
            make(i).start()
            return 0

        def gone(i, _):
            make(i).wait_send()
            return 0

        lax.fori_loop(lo, hi, go, 0)
        sent.append(lambda: lax.fori_loop(lo, hi, gone, 0))

    barrier = pltpu.get_barrier_semaphore()

    near = [(b, yh * 4 + lax.rem(z + d, 4)) for d in (1, 2, 3)]
    near += [(lax.rem(x + d, 4) * 4 + j, a) for d in (1, 2, 3)]
    near += [(x * 4 + lax.rem(j + d, 4), a) for d in (1, 2, 3)]
    near += [(x * 4 + lax.rem(j + d, 4), (1 - yh) * 4 + z) for d in range(4)]
    for peer in near:
        pl.semaphore_signal(barrier, 1, device_id=peer, device_id_type=MESH)
    pl.semaphore_wait(barrier, len(near))

    zm1, zp1, zp2 = lax.rem(z + 3, 4), lax.rem(z + 1, 4), lax.rem(z + 2, 4)
    own = (timg, simg)
    imgs = (it, is_)
    texts = (tt, ts)
    own_text = (ttext, stext)

    def half(h):
        return pl.ds(h * HALF, HALF)

    def img_send(m, d, h):
        return copy(
            own[m].at[half(h)], imgs[m].at[z, half(h)], zi_s.at[m, d, h], zi_r.at[m, d, h],
            znext(1 if d == 0 else 3),
        )

    def img_relay(m, d):
        slot = zm1 if d == 0 else zp1
        ref = imgs[m].at[slot, half(d)]
        return copy(ref, ref, zi_s.at[m, 2, d], zi_r.at[m, 2, d], znext(1 if d == 0 else 3))

    def img_recv(m, d, h):
        slot = zm1 if d == 0 else zp1
        ref = imgs[m].at[slot, half(h)]
        copy(ref, ref, zi_s.at[m, d, h], zi_r.at[m, d, h], znext(1)).wait_recv()

    def img_recv_far(m, d):
        ref = imgs[m].at[zp2, half(d)]
        copy(ref, ref, zi_s.at[m, 2, d], zi_r.at[m, 2, d], znext(1)).wait_recv()

    def img_start(m):
        start(img_send(m, 0, 0))
        start(img_send(m, 1, 1))

    def img_rest(m):
        start(img_send(m, 0, 1))
        start(img_send(m, 1, 0))

    def img_pass_on(m):
        img_recv(m, 0, 0)
        start(img_relay(m, 0))
        img_recv(m, 1, 1)
        start(img_relay(m, 1))

    syl, sk = z // 2, z % 2
    is_source = j == z

    def tslab(m, blk, h):
        return texts[m].at[pl.ds(blk * ROWS + h * HALF, HALF)]

    def text_first(m):
        return (
            copy(own_text[m].at[pl.ds((1 - sk) * HALF, HALF)], tslab(m, x, 1 - sk),
                 t1_s.at[m, 0], t1_r.at[m], dev(x, syl * 2 + 1 - sk, yh, z)),
            copy(own_text[m].at[half(0)], tslab(m, x, 0),
                 t1_s.at[m, 1], t1_r.at[m], dev(x, (1 - syl) * 2, yh, z)),
            copy(own_text[m].at[half(1)], tslab(m, x, 1),
                 t1_s.at[m, 2], t1_r.at[m], dev(x, (1 - syl) * 2 + 1, 1 - yh, z)),
        )

    def text_start(m):
        @pl.when(is_source)
        def _():
            for c in text_first(m):
                c.start()
            tslab(m, x, k)[...] = own_text[m][pl.ds(k * HALF, HALF)]

        def gone():
            @pl.when(is_source)
            def _():
                for c in text_first(m):
                    c.wait_send()

        sent.append(gone)

    def text_x(m, d):
        return copy(tslab(m, x, k), tslab(m, x, k), t2_s.at[m, d - 1], t2_r.at[m, d - 1],
                    (lax.rem(x + d, 4) * 4 + j, a))

    def text_got(m, d):
        slab = tslab(m, lax.rem(x + 4 - d, 4), k)
        copy(slab, slab, t2_s.at[m, d - 1], t2_r.at[m, d - 1], sib).wait_recv()

    def tlanes(m, blk, i):
        width = texts[m].shape[1] // 2
        return texts[m].at[pl.ds(blk * ROWS + k * HALF, HALF), i * width : (i + 1) * width]

    def text_relay(m, i):
        ref = tlanes(m, lax.rem(x + 3 - 2 * i, 4), i)
        return copy(ref, ref, t4_s.at[m, i], t4_r.at[m, i], (lax.rem(x + 1 + 2 * i, 4) * 4 + j, a))

    def text_sib(m, d):
        blk = lax.rem(x + 4 - d, 4)
        return copy(tslab(m, blk, k), tslab(m, blk, k), t3_s.at[m, d], t3_r.at[m, d], sib)

    holds = yl == syl
    lacks = yl != syl

    def text_cross(d):
        slab = tslab(1, lax.rem(x + 4 - d, 4), k)
        to = dev(x, (1 - syl) * 2 + k, yh + k * (1 - 2 * yh), z)
        return copy(slab, slab, t5_s.at[d - 1], t5_r.at[d - 1], to)

    def crossed(d):
        @pl.when(lacks)
        def _():
            slab = tslab(1, lax.rem(x + 4 - d, 4), k)
            copy(slab, slab, t5_s.at[d - 1], t5_r.at[d - 1], sib).wait_recv()

    def text_spread(m, here):
        @pl.when(here & jnp.logical_not(is_source))
        def _():
            copy(tslab(m, x, k), tslab(m, x, k), t1_s.at[m, 0], t1_r.at[m], sib).wait_recv()

        for d in (1, 3):
            if m == 0 or here is holds:
                start_if(here, text_x(m, d))
        start_if(here, text_sib(m, 0))

    def text_pass_on(m):
        for d in (1, 3):
            if m:
                @pl.when(holds)
                def _():
                    text_got(m, d)

                start_if(holds, text_relay(m, d // 2))
                start_if(holds, text_cross(d))
                crossed(d)
            else:
                text_got(m, d)
                start(text_relay(m, d // 2))
            start(text_sib(m, d))

    def text_far(m):
        def arrived():
            for i in range(2):
                ref = tlanes(m, lax.rem(x + 2, 4), i)
                copy(ref, ref, t4_s.at[m, i], t4_r.at[m, i], sib).wait_recv()

        if m:
            pl.when(holds)(arrived)
            start_if(holds, text_cross(2))
            crossed(2)
        else:
            arrived()
        start(text_sib(m, 2))

    def text_wait(m):
        for d in range(4):
            blk = lax.rem(x + 4 - d, 4)
            copy(tslab(m, blk, 1 - k), tslab(m, blk, 1 - k), t3_s.at[m, d], t3_r.at[m, d],
                 sib).wait_recv()

    lane = lax.broadcasted_iota(jnp.int32, (ROWS, 128), 1)

    def fold(op, t):
        return functools.reduce(op, [t[:, i * 128 : (i + 1) * 128] for i in range(COLS // 128)])

    def scores(m, v, pr, qr, scale, far=False):
        t = dot(imgs[m][v], texts[m][...], NT) * scale
        cm = jnp.max(t, axis=0, keepdims=True)
        top = jnp.max(fold(jnp.maximum, t), axis=1, keepdims=True)
        q = jnp.exp(t - cm)
        qr[v] = q
        p = jnp.exp(t - top)
        pr[v] = p
        cs = jnp.sum(q, axis=0, keepdims=True)
        if far:
            cfar[0:1, :] = cm
            cfar[1:2, :] = cs
        else:
            colst[m, pl.ds(v, 1), :] = cm
            colst[m, pl.ds(v + 4, 1), :] = cs
        total = jnp.sum(fold(jnp.add, p), axis=1, keepdims=True)
        rowst[:ROWS, :] = jnp.where(
            lane == v, top, jnp.where(lane == v + 4, total, rowst[:ROWS, :])
        )

    def row_copy(m, d):
        return copy(rowsend.at[m], rowrecv.at[m, d - 1], row_s.at[m, d - 1], row_r.at[m, d - 1],
                    znext(d))

    def quad_copy(m, d):
        return copy(colst.at[m], quad_in.at[m, d - 1], quad_s.at[m, d - 1], quad_r.at[m, d - 1],
                    (x * 4 + lax.rem(j + d, 4), a))

    def col_copy(m, d):
        return copy(colq.at[m], colx_in.at[m, d - 1], col_s.at[m, d - 1], col_r.at[m, d - 1],
                    (lax.rem(x + d, 4) * 4 + j, a))

    def merged(mine, others):
        top = functools.reduce(jnp.maximum, [t[:4] for t in others], mine[:4])
        total = mine[4:] * jnp.exp(mine[:4] - top)
        for t in others:
            total = total + t[4:] * jnp.exp(t[:4] - top)
        return top, total

    def far_copy(d):
        return copy(cfar, cfar_in.at[d - 1], far_s.at[d - 1], far_r.at[d - 1],
                    (lax.rem(b + d, 16), a))

    def far_finish():
        def arrived(d, top):
            far_copy(d).wait_recv()
            return jnp.maximum(top, cfar_in[d - 1, 0:1, :])

        mine = cfar[0:1, :]
        top = lax.fori_loop(1, 16, arrived, mine)

        def add(d, total):
            return total + cfar_in[d, 1:2, :] * jnp.exp(cfar_in[d, 0:1, :] - top)

        total = lax.fori_loop(0, 15, add, cfar[1:2, :] * jnp.exp(mine - top))
        colfac[0, pl.ds(zp2, 1), :] = jnp.exp(mine - top - jnp.log(total))

    def cols_start(m):
        for d in (1, 2, 3):
            start(quad_copy(m, d))

    def rows_start(m):
        rowsend[m] = jnp.transpose(rowst[...])[:8]
        for d in (1, 3, 2):
            start(row_copy(m, d))

    def stats_middle(m):
        for d in (1, 2, 3):
            quad_copy(m, d).wait_recv()
        top, total = merged(colst[m], [quad_in[m, d] for d in range(3)])
        colq[m, 0:4, :] = top
        colq[m, 4:8, :] = total
        for d in (1, 3, 2):
            start(col_copy(m, d))

    def stats_finish(m):
        for d in (1, 3, 2):
            row_copy(m, d).wait_recv()
        mine = rowsend[m]
        top, total = merged(mine, [rowrecv[m, d] for d in range(3)])
        row_lse = top + jnp.log(total)
        rowtmp[0:4, :] = jnp.exp(mine[:4] - row_lse)
        rowfac[m] = jnp.transpose(rowtmp[...])
        for d in (1, 3, 2):
            col_copy(m, d).wait_recv()
        top, total = merged(colq[m], [colx_in[m, d] for d in range(3)])
        col_lse = top + jnp.log(total)
        colfac[m, 0:4, :] = jnp.exp(colst[m, 0:4, :] - col_lse)
        return row_lse, col_lse

    rowst[...] = jnp.ones_like(rowst)
    rowtmp[...] = jnp.zeros_like(rowtmp)
    colst[0] = jnp.ones_like(colst[0])
    img_start(1)
    img_rest(1)
    text_start(1)
    img_start(0)
    text_start(0)
    is_[z] = simg[...]
    it[z] = timg[...]
    text_spread(1, holds)
    text_spread(1, lacks)
    text_spread(0, lacks)
    img_pass_on(1)
    img_rest(0)
    text_pass_on(1)
    text_spread(0, holds)
    text_far(1)
    text_wait(1)

    scores(1, z, ps, qs, student_scale)
    img_recv(1, 0, 1)
    scores(1, zm1, ps, qs, student_scale)
    img_recv(1, 1, 0)
    scores(1, zp1, ps, qs, student_scale)
    img_pass_on(0)
    text_pass_on(0)
    img_recv_far(1, 0)
    img_recv_far(1, 1)
    scores(1, zp2, ps, qs, student_scale)
    cols_start(1)
    rows_start(1)

    partner = (b, (1 - yh) * 4 + z)
    total_img = (
        is_[0].astype(F32) + is_[1].astype(F32) + is_[2].astype(F32) + is_[3].astype(F32)
    )
    for g in range(4):
        isum[0, g] = total_img[:HALF, g * 128 : (g + 1) * 128]
        isum[1, g] = total_img[HALF:, g * 128 : (g + 1) * 128]
    iy = copy(isum.at[1 - yh, z], isum_in.at[z], iy_s.at[0], iy_r.at[0], partner)
    start(iy)
    text_far(0)
    text_wait(0)

    scores(0, z, pt, qt, teacher_scale)
    stats_middle(1)
    img_recv(0, 0, 1)
    scores(0, zm1, pt, qt, teacher_scale)
    img_recv(0, 1, 0)
    scores(0, zp1, pt, qt, teacher_scale)
    cols_start(0)
    stats_middle(0)
    img_recv_far(0, 0)
    img_recv_far(0, 1)
    scores(0, zp2, pt, qt, teacher_scale, far=True)
    start_all(1, 16, far_copy)
    rows_start(0)

    def iz_copy(d):
        slot = isum_in.at[z]
        return copy(slot, slot, iz_s.at[d - 1], iz_r.at[d - 1], znext(d))

    def iz_wait(d):
        slot = isum_in.at[lax.rem(z + 4 - d, 4)]
        copy(slot, slot, iz_s.at[d - 1], iz_r.at[d - 1], partner).wait_recv()

    iy.wait_recv()
    for d in (1, 3, 2):
        start(iz_copy(d))

    row_lse, col_lse = stats_finish(1)
    rl = lax.broadcasted_iota(jnp.int32, (4, 384), 0)
    cl = lax.broadcasted_iota(jnp.int32, (4, 384), 1)
    row_part = jnp.sum(jnp.where((rl == z) & (cl < ROWS), row_lse, 0.0), axis=0, keepdims=True)
    lse_part = (
        jnp.sum(row_part, axis=1, keepdims=True)
        + jnp.sum(jnp.sum(col_lse, axis=0, keepdims=True), axis=1, keepdims=True) * (1.0 / 16.0)
    )

    for d in (2, 1, 3, 0):
        v = lax.rem(z + d, 4)
        factor = jnp.sum(jnp.where(lane == v, rowfac[1, :ROWS, :], 0.0), axis=1, keepdims=True)
        w[v] = (ps[v] * factor + qs[v] * colfac[1, pl.ds(v, 1), :]).astype(BF16)
        gsend[d] = dot(w[v], ts[...], NN)

    def g_far(h):
        return copy(gsend.at[2, half(h)], gfar_in.at[h], g_s.at[2, h], g_r.at[2, h],
                    znext(1 if h == 0 else 3))

    def g_copy(i, h):
        d = 1 + 2 * i
        return copy(gsend.at[d, half(h)], grecv.at[i, half(h)], g_s.at[i, h], g_r.at[i, h],
                    znext(d))

    start(g_far(0))
    start(g_far(1))
    start(g_copy(0, 1))
    start(g_copy(1, 0))


    stats_finish(0)
    far_finish()


    def tgt_copy(n):
        return copy(tgt.at[n], tgt_in.at[n], tgt_s.at[n], tgt_r.at[n], partner)

    def own_targets(h, n):
        rows = pl.ds(pl.multiple_of(h * HALF + n * 48, 16), 48)
        acc = None
        for v in range(4):
            term = pt[v, rows] * rowfac[0, rows, v : v + 1] + qt[v, rows] * colfac[0, v : v + 1, :]
            acc = term if acc is None else acc + term
        return acc

    for n in range(NCH):
        tgt[n] = own_targets(1 - yh, n)
        start(tgt_copy(n))
    acc = dot(w[0], is_[0], TN)
    for v in range(1, 4):
        acc = acc + dot(w[v], is_[v], TN)
    gtp[...] = acc
    for n in range(NCH):
        tgt_mine[n] = own_targets(yh, n)

    for d in (1, 3, 2):
        iz_wait(d)
    for g in range(4):
        isum8[g] = isum_in[g] + isum[yh, g]
    for g in range(4):
        t = isum8[g]
        hi[:, g * 128 : (g + 1) * 128] = t.astype(BF16)
        lo[:, g * 128 : (g + 1) * 128] = (t - t.astype(BF16).astype(F32)).astype(BF16)
    for i in range(2):
        g_far(i).wait_recv()
        rows = slice(i * HALF, (i + 1) * HALF)
        gsend[1 + 2 * i, rows] = gsend[1 + 2 * i, rows] + gfar_in[i]
        start(g_copy(i, i))

    for n in range(NCH):
        tgt_copy(n).wait_recv()
        tw[n * 48 : (n + 1) * 48] = ((tgt_mine[n] + tgt_in[n]) * 0.125).astype(BF16)
    target_text = dot(tw[...], ts[...], NN)
    for g in range(4):
        tt_part[g] = target_text[:, g * 128 : (g + 1) * 128]

    def tz_copy(d):
        return copy(tt_part.at[lax.rem(z + d, 4)], tt_in.at[d - 1], tz_s.at[d - 1],
                    tz_r.at[d - 1], znext(d))

    for d in (2, 1, 3):
        start(tz_copy(d))

    res = gtp[...] - dot(tw[...], hi[...], TN) - dot(tw[...], lo[...], TN)
    for s in range(8):
        row = s * HALF
        for g in range(4):
            gtc[s % 2, s // 2, g] = res[row : row + HALF, g * 128 : (g + 1) * 128]
    def gc_copy(i):
        rows = slice(i * 72, (i + 1) * 72)
        return copy(gtc.at[1 - k, :, :, rows, :], gt_sib.at[:, :, rows, :], gc_s.at[i],
                    gc_r.at[i], sib)

    start(gc_copy(0))
    start(gc_copy(1))

    target_loss = isum8[0] * tt_part[0]
    for g in range(1, 4):
        target_loss = target_loss + isum8[g] * tt_part[g]
    target_loss = jnp.sum(jnp.sum(target_loss, axis=0, keepdims=True), axis=1, keepdims=True)
    part = lse_part - target_loss * student_scale
    loss_src[...] = jnp.broadcast_to(part, (8, 128))

    def lb_copy(d):
        return copy(loss_src, loss_b.at[d - 1], lb_s.at[d - 1], lb_r.at[d - 1],
                    (lax.rem(b + d, 16), a))

    start_all(1, 16, lb_copy)

    y = yh * 2 + yl
    pieces = gtc.at[k]

    def ydev(d):
        yd = lax.rem(y + d, 4)
        return dev(x, (yd % 2) * 2 + k, yd // 2, z)

    def xdev(d):
        return dev(lax.rem(x + d, 4), j, yh, z)

    def ra_copy(d):
        return copy(pieces.at[lax.rem(x + d, 4), :, 0:72, :], ra_in.at[d - 1],
                    rs_s.at[0, d - 1], rs_r.at[0, d - 1], xdev(d))

    def rb_copy(d):
        return copy(pieces.at[:, lax.rem(y + d, 4), 72:144, :], rb_in.at[d - 1],
                    rs_s.at[1, d - 1], rs_r.at[1, d - 1], ydev(d))

    def ra2_copy(d):
        return copy(ra_sum.at[lax.rem(y + d, 4)], ra2_in.at[d - 1],
                    rs_s.at[2, d - 1], rs_r.at[2, d - 1], ydev(d))

    def rb2_copy(d):
        return copy(rb_sum.at[lax.rem(x + d, 4)], rb2_in.at[d - 1],
                    rs_s.at[3, d - 1], rs_r.at[3, d - 1], xdev(d))

    for i in range(2):
        gc_copy(i).wait_recv()
        rows = slice(i * 72, (i + 1) * 72)
        for blk in range(4):
            for g in range(4):
                gtc[k, blk, g, rows, :] = gtc[k, blk, g, rows, :] + gt_sib[blk, g, rows, :]
        for d in ((1, 3, 2), (1, 3))[i]:
            start((ra_copy, rb_copy)[i](d))

    total = tt_part[z]
    for d in (1, 3, 2):
        tz_copy(d).wait_recv()
        total = total + tt_in[d - 1]
    tt_src[...] = total

    a_in = (1 - yh) * 4 + z
    ty = copy(tt_src, tt_all.at[a], ta_s.at[0], ta_r.at[a], partner)
    start(ty)
    start(rb_copy(2))

    def ta_copy(d):
        return copy(tt_src, tt_all.at[a], ta_s.at[d], ta_r.at[a], znext(d))

    def tb_copy(d):
        return copy(tt_all.at[a_in], tt_all.at[a_in], ta_s.at[3 + d], ta_r.at[a_in], znext(d))

    def t_wait(slot):
        copy(tt_src, tt_all.at[slot], ta_s.at[0], ta_r.at[slot], partner).wait_recv()

    for d in (1, 3, 2):
        start(ta_copy(d))
    tt_all[a] = total

    def lb_wait(d, acc):
        lb_copy(d).wait_recv()
        return acc + loss_b[d - 1]

    loss_src2[...] = lax.fori_loop(1, 16, lb_wait, loss_src[...])

    def la_copy(d):
        return copy(loss_src2, loss_a.at[d - 1], la_s.at[d - 1], la_r.at[d - 1],
                    (b, lax.rem(a + d, 8)))

    start_all(1, 8, la_copy)

    ra_sum[...] = gtc[k, x, :, 0:72, :]
    rb_sum[...] = gtc[k, :, y, 72:144, :]
    for d in (1, 3, 2):
        ra_copy(d).wait_recv()
        ra_sum[...] = ra_sum[...] + ra_in[d - 1]
    for d in (1, 3, 2):
        start(ra2_copy(d))
    for d in (1, 3, 2):
        rb_copy(d).wait_recv()
        rb_sum[...] = rb_sum[...] + rb_in[d - 1]
    for d in (1, 3, 2):
        start(rb2_copy(d))
    t_wait(a_in)
    for d in (1, 3, 2):
        start(tb_copy(d))
    first, last = ra_sum[y], rb_sum[x]
    for d in (1, 3, 2):
        ra2_copy(d).wait_recv()
        first = first + ra2_in[d - 1]
    for d in (1, 3, 2):
        rb2_copy(d).wait_recv()
        last = last + rb2_in[d - 1]
    fb_src[z, 0:72, :] = first
    fb_src[z, 72:144, :] = last

    def fz_copy(d):
        return copy(fb_src.at[z], fb_src.at[z], fz_s.at[d - 1], fz_r.at[d - 1], znext(d))

    def fb_copy(c, h):
        return copy(fb_src.at[c], fb_buf.at[j * 2 + yh], fb_s.at[c, h], fb_r.at[j * 2 + yh],
                    dev(x, c, h, z))

    def is_self(c, h):
        return (j == c) & (yh == h)

    def fb_send(c):
        for h in range(2):
            @pl.when(jnp.logical_not(is_self(c, h)))
            def _():
                fb_copy(c, h).start()

    def fb_gone():
        for c in range(4):
            for h in range(2):
                @pl.when(jnp.logical_not(is_self(c, h)))
                def _():
                    fb_copy(c, h).wait_send()

    sent.append(fb_gone)
    for d in (1, 3, 2):
        start(fz_copy(d))
    fb_send(z)
    for d in (1, 3, 2):
        c = lax.rem(z + 4 - d, 4)
        copy(fb_src.at[c], fb_src.at[c], fz_s.at[d - 1], fz_r.at[d - 1], partner).wait_recv()
        fb_send(c)
    fb_buf[j * 2 + yh] = fb_src[j]

    acc = gsend[0]
    for i in range(2):
        g_copy(i, 0).wait_recv()
        g_copy(i, 1).wait_recv()
        acc = acc + grecv[i]

    for d in (1, 3, 2):
        zd = lax.rem(z + d, 4)
        t_wait(yh * 4 + zd)
        t_wait((1 - yh) * 4 + zd)
    for h in range(2):
        rows = slice(h * HALF, (h + 1) * HALF)
        for g in range(4):
            lanes = slice(g * 128, (g + 1) * 128)
            grads_out[0, rows, lanes] = acc[rows, lanes] - tt_all[h * 4 + g]

    def la_wait(d, acc):
        la_copy(d).wait_recv()
        return acc + loss_a[d - 1]

    whole = lax.fori_loop(1, 8, la_wait, loss_src2[...])
    loss_out[0, 0] = jnp.sum(whole[0:1, 0:1]) * (1.0 / (2.0 * 8 * 4608))

    def fb_wait(s, _):
        @pl.when(s != j * 2 + yh)
        def _():
            copy(fb_src.at[0], fb_buf.at[s], fb_s.at[0, 0], fb_r.at[s], partner).wait_recv()

        return 0

    lax.fori_loop(0, 8, fb_wait, 0)
    for s in range(8):
        syl_, sk_, syh_ = s // 4, (s // 2) % 2, s % 2
        g = syh_ * 2 + syl_
        grads_out[1, sk_ * HALF : (sk_ + 1) * HALF, g * 128 : (g + 1) * 128] = fb_buf[s]

    for gone in sent:
        gone()


def per_device(student_image, student_text, teacher_image, teacher_text):
    vm = pl.BlockSpec(memory_space=pltpu.VMEM)
    dma = pltpu.SemaphoreType.DMA
    V = pltpu.VMEM
    sw, twd = student_image.shape[2], teacher_image.shape[2]
    loss, grads = pl.pallas_call(
        kernel,
        name="distill",
        out_shape=(
            jax.ShapeDtypeStruct((1, 1), F32),
            jax.ShapeDtypeStruct((2, ROWS, sw), F32),
        ),
        in_specs=[vm] * 4,
        out_specs=(pl.BlockSpec(memory_space=pltpu.SMEM), vm),
        scratch_shapes=[
            V((4, ROWS, twd), BF16), V((4, ROWS, sw), BF16),
            V((4 * ROWS, twd), BF16), V((4 * ROWS, sw), BF16),
            V((4, ROWS, COLS), F32), V((4, ROWS, COLS), F32),
            V((4, ROWS, COLS), F32), V((4, ROWS, COLS), F32),
            V((4, ROWS, COLS), BF16),
            V((NCH, 48, COLS), F32), V((NCH, 48, COLS), F32), V((NCH, 48, COLS), F32),
            V((HALF, COLS), BF16),
            V((2, 4, HALF, 128), F32), V((4, HALF, 128), F32), V((4, HALF, 128), F32),
            V((HALF, sw), BF16), V((HALF, sw), BF16),
            V((4, HALF, 128), F32), V((3, HALF, 128), F32), V((HALF, 128), F32),
            V((8, HALF, 128), F32),
            V((4, ROWS, sw), F32), V((2, ROWS, sw), F32), V((2, HALF, sw), F32),
            V((COLS, sw), F32), V((4, 4, HALF, 128), F32),
            V((3, 4, 72, 128), F32), V((3, 4, 72, 128), F32), V((4, 72, 128), F32),
            V((4, 72, 128), F32), V((3, 72, 128), F32), V((3, 72, 128), F32),
            V((4, HALF, 128), F32), V((8, HALF, 128), F32),
            V((2, 4, 4, HALF, 128), F32),
            V((384, 128), F32), V((2, 8, 384), F32), V((2, 3, 8, 384), F32),
            V((2, 384, 128), F32), V((128, 384), F32),
            V((2, 8, COLS), F32), V((2, 3, 8, COLS), F32), V((2, 8, COLS), F32),
            V((2, 3, 8, COLS), F32), V((2, 8, COLS), F32),
            V((2, COLS), F32), V((15, 2, COLS), F32),
            V((8, 128), F32), V((15, 8, 128), F32), V((8, 128), F32), V((7, 8, 128), F32),
            dma((2, 3, 2)), dma((2, 3, 2)),
            dma((2, 3)), dma((2,)), dma((2, 3)), dma((2, 3)), dma((2, 4)), dma((2, 4)),
            dma((2, 2)), dma((2, 2)), dma((3,)), dma((3,)),
            dma((1,)), dma((1,)), dma((3,)), dma((3,)), dma((3,)), dma((3,)), dma((7,)), dma((8,)),
            dma((15,)), dma((15,)),
            dma((2, 3)), dma((2, 3)), dma((2, 3)), dma((2, 3)), dma((2, 3)), dma((2, 3)),
            dma((3,)), dma((3,)), dma((3, 2)), dma((3, 2)), dma((2,)), dma((2,)),
            dma((4, 3)), dma((4, 3)), dma((3,)), dma((3,)), dma((4, 2)), dma((8,)),
            dma((15,)), dma((15,)), dma((7,)), dma((7,)),
        ],
        compiler_params=pltpu.CompilerParams(
            collective_id=0, has_side_effects=True, vmem_limit_bytes=60 * 1024 * 1024
        ),
        cost_estimate=pl.CostEstimate(
            flops=8 * 10**9, bytes_accessed=4 * 2**20, transcendentals=6 * 10**6
        ),
    )(student_image[0], student_text, teacher_image[0], teacher_text)
    scale = 3.0 / math.sqrt(sw)
    return loss.reshape(()), (grads[0] * scale)[None], grads[1] * scale


def solution(mesh):
    return jax.shard_map(
        per_device,
        mesh=mesh,
        in_specs=(
            P("aug", "batch", None),
            P("batch", None),
            P("aug", "batch", None),
            P("batch", None),
        ),
        out_specs=(P(), P("aug", "batch", None), P("batch", None)),
        check_vma=False,
    )
```

```python
import functools
import math

import jax
import jax.numpy as jnp
from jax import lax
from jax.experimental import pallas as pl
from jax.experimental.pallas import tpu as pltpu
from jax.sharding import PartitionSpec as P

MESH = pl.DeviceIdType.MESH
F32 = jnp.float32
BF16 = jnp.bfloat16
ROWS = 288
HALF = ROWS // 2
COLS = 4 * ROWS
NCH = 3
NT = (((1,), (1,)), ((), ()))
NN = (((1,), (0,)), ((), ()))
TN = (((0,), (0,)), ((), ()))


def dot(a, b, dims):
    return lax.dot_general(a, b, dims, preferred_element_type=F32)


def kernel(
    simg, stext, timg, ttext,
    loss_out, grads_out,
    it, is_, tt, ts, pt, qt, ps, qs, w, tgt, tgt_mine, tgt_in, tw,
    isum, isum_in, isum8, hi, lo, tt_part, tt_in, tt_src, tt_all,
    gsend, grecv, gfar_in, gtp, gt_sib, ra_in, rb_in, ra_sum, rb_sum, ra2_in, rb2_in, fb_src, fb_buf, gtc,
    rowst, rowsend, rowrecv, rowfac, rowtmp, colst, quad_in, colq, colx_in, colfac, cfar, cfar_in,
    loss_src, loss_b, loss_src2, loss_a,
    own_s, zi_s, zi_r, t1_s, t1_r, t2_s, t2_r, t3_s, t3_r, t4_s, t4_r, t5_s, t5_r,
    iy_s, iy_r, iz_s, iz_r, tz_s, tz_r, ta_s, ta_r,
    far_s, far_r, quad_s, quad_r, row_s, row_r, col_s, col_r, tgt_s, tgt_r, g_s, g_r, gc_s, gc_r,
    rs_s, rs_r, fz_s, fz_r, fb_s, fb_r, lb_s, lb_r, la_s, la_r,
):
    b = lax.axis_index("batch")
    a = lax.axis_index("aug")
    x, j = b // 4, b % 4
    yl, k = j // 2, j % 2
    yh, z = a // 4, a % 4
    sib = (b + 1 - 2 * k, a)
    teacher_scale = 3.0 / math.sqrt(timg.shape[1])
    student_scale = 3.0 / math.sqrt(simg.shape[1])

    def dev(x_, j_, yh_, z_):
        return (x_ * 4 + j_, yh_ * 4 + z_)

    def znext(d):
        return (b, yh * 4 + lax.rem(z + d, 4))

    def copy(src, dst, ss, rs, to):
        return pltpu.make_async_remote_copy(
            src_ref=src, dst_ref=dst, send_sem=ss, recv_sem=rs, device_id=to, device_id_type=MESH
        )

    sent = []

    def start(c):
        c.start()
        sent.append(c.wait_send)

    def start_if(cond, c):
        @pl.when(cond)
        def _():
            c.start()

        def gone():
            @pl.when(cond)
            def _():
                c.wait_send()

        sent.append(gone)

    def start_all(lo, hi, make):
        def go(i, _):
            make(i).start()
            return 0

        def gone(i, _):
            make(i).wait_send()
            return 0

        lax.fori_loop(lo, hi, go, 0)
        sent.append(lambda: lax.fori_loop(lo, hi, gone, 0))

    barrier = pltpu.get_barrier_semaphore()

    near = [(b, yh * 4 + lax.rem(z + d, 4)) for d in (1, 2, 3)]
    near += [(lax.rem(x + d, 4) * 4 + j, a) for d in (1, 2, 3)]
    near += [(x * 4 + lax.rem(j + d, 4), a) for d in (1, 2, 3)]
    near += [(x * 4 + lax.rem(j + d, 4), (1 - yh) * 4 + z) for d in range(4)]
    for peer in near:
        pl.semaphore_signal(barrier, 1, device_id=peer, device_id_type=MESH)
    pl.semaphore_wait(barrier, len(near))

    zm1, zp1, zp2 = lax.rem(z + 3, 4), lax.rem(z + 1, 4), lax.rem(z + 2, 4)
    own = (timg, simg)
    imgs = (it, is_)
    texts = (tt, ts)
    own_text = (ttext, stext)

    def half(h):
        return pl.ds(h * HALF, HALF)

    def img_send(m, d, h):
        return copy(
            own[m].at[half(h)], imgs[m].at[z, half(h)], zi_s.at[m, d, h], zi_r.at[m, d, h],
            znext(1 if d == 0 else 3),
        )

    def img_relay(m, d):
        slot = zm1 if d == 0 else zp1
        ref = imgs[m].at[slot, half(d)]
        return copy(ref, ref, zi_s.at[m, 2, d], zi_r.at[m, 2, d], znext(1 if d == 0 else 3))

    def img_recv(m, d, h):
        slot = zm1 if d == 0 else zp1
        ref = imgs[m].at[slot, half(h)]
        copy(ref, ref, zi_s.at[m, d, h], zi_r.at[m, d, h], znext(1)).wait_recv()

    def img_recv_far(m, d):
        ref = imgs[m].at[zp2, half(d)]
        copy(ref, ref, zi_s.at[m, 2, d], zi_r.at[m, 2, d], znext(1)).wait_recv()

    def img_start(m):
        start(img_send(m, 0, 0))
        start(img_send(m, 1, 1))

    def img_rest(m):
        start(img_send(m, 0, 1))
        start(img_send(m, 1, 0))

    def img_pass_on(m):
        img_recv(m, 0, 0)
        start(img_relay(m, 0))
        img_recv(m, 1, 1)
        start(img_relay(m, 1))

    syl, sk = z // 2, z % 2
    is_source = j == z

    def tslab(m, blk, h):
        return texts[m].at[pl.ds(blk * ROWS + h * HALF, HALF)]

    def text_first(m):
        return (
            copy(own_text[m].at[pl.ds((1 - sk) * HALF, HALF)], tslab(m, x, 1 - sk),
                 t1_s.at[m, 0], t1_r.at[m], dev(x, syl * 2 + 1 - sk, yh, z)),
            copy(own_text[m].at[half(0)], tslab(m, x, 0),
                 t1_s.at[m, 1], t1_r.at[m], dev(x, (1 - syl) * 2, yh, z)),
            copy(own_text[m].at[half(1)], tslab(m, x, 1),
                 t1_s.at[m, 2], t1_r.at[m], dev(x, (1 - syl) * 2 + 1, 1 - yh, z)),
        )

    def text_own(m):
        return pltpu.make_async_copy(
            own_text[m].at[pl.ds(k * HALF, HALF)], tslab(m, x, k), own_s.at[2 + m]
        )

    def img_own(m):
        return pltpu.make_async_copy(own[m], imgs[m].at[z], own_s.at[m])

    def text_start(m):
        @pl.when(is_source)
        def _():
            for c in text_first(m):
                c.start()
            text_own(m).start()

        def gone():
            @pl.when(is_source)
            def _():
                for c in text_first(m):
                    c.wait_send()

        sent.append(gone)

    def text_x(m, d):
        return copy(tslab(m, x, k), tslab(m, x, k), t2_s.at[m, d - 1], t2_r.at[m, d - 1],
                    (lax.rem(x + d, 4) * 4 + j, a))

    def text_got(m, d):
        slab = tslab(m, lax.rem(x + 4 - d, 4), k)
        copy(slab, slab, t2_s.at[m, d - 1], t2_r.at[m, d - 1], sib).wait_recv()

    def tlanes(m, blk, i):
        width = texts[m].shape[1] // 2
        return texts[m].at[pl.ds(blk * ROWS + k * HALF, HALF), i * width : (i + 1) * width]

    def text_relay(m, i):
        ref = tlanes(m, lax.rem(x + 3 - 2 * i, 4), i)
        return copy(ref, ref, t4_s.at[m, i], t4_r.at[m, i], (lax.rem(x + 1 + 2 * i, 4) * 4 + j, a))

    def text_sib(m, d):
        blk = lax.rem(x + 4 - d, 4)
        return copy(tslab(m, blk, k), tslab(m, blk, k), t3_s.at[m, d], t3_r.at[m, d], sib)

    holds = yl == syl
    lacks = yl != syl

    def text_cross(d):
        slab = tslab(1, lax.rem(x + 4 - d, 4), k)
        to = dev(x, (1 - syl) * 2 + k, yh + k * (1 - 2 * yh), z)
        return copy(slab, slab, t5_s.at[d - 1], t5_r.at[d - 1], to)

    def crossed(d):
        @pl.when(lacks)
        def _():
            slab = tslab(1, lax.rem(x + 4 - d, 4), k)
            copy(slab, slab, t5_s.at[d - 1], t5_r.at[d - 1], sib).wait_recv()

    def text_spread(m, here):
        @pl.when(here & jnp.logical_not(is_source))
        def _():
            copy(tslab(m, x, k), tslab(m, x, k), t1_s.at[m, 0], t1_r.at[m], sib).wait_recv()

        @pl.when(here & is_source)
        def _():
            text_own(m).wait()

        for d in (1, 3):
            if m == 0 or here is holds:
                start_if(here, text_x(m, d))
        start_if(here, text_sib(m, 0))

    def text_pass_on(m):
        for d in (1, 3):
            if m:
                @pl.when(holds)
                def _():
                    text_got(m, d)

                start_if(holds, text_relay(m, d // 2))
                start_if(holds, text_cross(d))
                crossed(d)
            else:
                text_got(m, d)
                start(text_relay(m, d // 2))
            start(text_sib(m, d))

    def text_far(m):
        def arrived():
            for i in range(2):
                ref = tlanes(m, lax.rem(x + 2, 4), i)
                copy(ref, ref, t4_s.at[m, i], t4_r.at[m, i], sib).wait_recv()

        if m:
            pl.when(holds)(arrived)
            start_if(holds, text_cross(2))
            crossed(2)
        else:
            arrived()
        start(text_sib(m, 2))

    def text_wait(m):
        for d in range(4):
            blk = lax.rem(x + 4 - d, 4)
            copy(tslab(m, blk, 1 - k), tslab(m, blk, 1 - k), t3_s.at[m, d], t3_r.at[m, d],
                 sib).wait_recv()

    lane = lax.broadcasted_iota(jnp.int32, (ROWS, 128), 1)

    def fold(op, t):
        return functools.reduce(op, [t[:, i * 128 : (i + 1) * 128] for i in range(COLS // 128)])

    def scores(m, v, pr, qr, scale, far=False):
        t = dot(imgs[m][v], texts[m][...], NT) * scale
        cm = jnp.max(t, axis=0, keepdims=True)
        top = jnp.max(fold(jnp.maximum, t), axis=1, keepdims=True)
        q = jnp.exp(t - cm)
        qr[v] = q
        p = jnp.exp(t - top)
        pr[v] = p
        cs = jnp.sum(q, axis=0, keepdims=True)
        if far:
            cfar[0:1, :] = cm
            cfar[1:2, :] = cs
        else:
            colst[m, pl.ds(v, 1), :] = cm
            colst[m, pl.ds(v + 4, 1), :] = cs
        total = jnp.sum(fold(jnp.add, p), axis=1, keepdims=True)
        rowst[:ROWS, :] = jnp.where(
            lane == v, top, jnp.where(lane == v + 4, total, rowst[:ROWS, :])
        )

    def row_copy(m, d):
        return copy(rowsend.at[m], rowrecv.at[m, d - 1], row_s.at[m, d - 1], row_r.at[m, d - 1],
                    znext(d))

    def quad_copy(m, d):
        return copy(colst.at[m], quad_in.at[m, d - 1], quad_s.at[m, d - 1], quad_r.at[m, d - 1],
                    (x * 4 + lax.rem(j + d, 4), a))

    def col_copy(m, d):
        return copy(colq.at[m], colx_in.at[m, d - 1], col_s.at[m, d - 1], col_r.at[m, d - 1],
                    (lax.rem(x + d, 4) * 4 + j, a))

    def merged(mine, others):
        top = functools.reduce(jnp.maximum, [t[:4] for t in others], mine[:4])
        total = mine[4:] * jnp.exp(mine[:4] - top)
        for t in others:
            total = total + t[4:] * jnp.exp(t[:4] - top)
        return top, total

    def far_copy(d):
        return copy(cfar, cfar_in.at[d - 1], far_s.at[d - 1], far_r.at[d - 1],
                    (lax.rem(b + d, 16), a))

    def far_finish():
        def arrived(d, top):
            far_copy(d).wait_recv()
            return jnp.maximum(top, cfar_in[d - 1, 0:1, :])

        mine = cfar[0:1, :]
        top = lax.fori_loop(1, 16, arrived, mine)

        def add(d, total):
            return total + cfar_in[d, 1:2, :] * jnp.exp(cfar_in[d, 0:1, :] - top)

        total = lax.fori_loop(0, 15, add, cfar[1:2, :] * jnp.exp(mine - top))
        colfac[0, pl.ds(zp2, 1), :] = jnp.exp(mine - top - jnp.log(total))

    def cols_start(m):
        for d in (1, 2, 3):
            start(quad_copy(m, d))

    def rows_start(m):
        rowsend[m] = jnp.transpose(rowst[...])[:8]
        for d in (1, 3, 2):
            start(row_copy(m, d))

    def stats_middle(m):
        for d in (1, 2, 3):
            quad_copy(m, d).wait_recv()
        top, total = merged(colst[m], [quad_in[m, d] for d in range(3)])
        colq[m, 0:4, :] = top
        colq[m, 4:8, :] = total
        for d in (1, 3, 2):
            start(col_copy(m, d))

    def stats_finish(m):
        for d in (1, 3, 2):
            row_copy(m, d).wait_recv()
        mine = rowsend[m]
        top, total = merged(mine, [rowrecv[m, d] for d in range(3)])
        row_lse = top + jnp.log(total)
        rowtmp[0:4, :] = jnp.exp(mine[:4] - row_lse)
        rowfac[m] = jnp.transpose(rowtmp[...])
        for d in (1, 3, 2):
            col_copy(m, d).wait_recv()
        top, total = merged(colq[m], [colx_in[m, d] for d in range(3)])
        col_lse = top + jnp.log(total)
        colfac[m, 0:4, :] = jnp.exp(colst[m, 0:4, :] - col_lse)
        return row_lse, col_lse

    rowst[...] = jnp.ones_like(rowst)
    rowtmp[...] = jnp.zeros_like(rowtmp)
    colst[0] = jnp.ones_like(colst[0])
    img_start(1)
    img_rest(1)
    text_start(1)
    img_start(0)
    text_start(0)
    img_own(1).start()
    img_own(0).start()
    text_spread(1, holds)
    text_spread(1, lacks)
    text_spread(0, lacks)
    img_pass_on(1)
    img_rest(0)
    text_pass_on(1)
    text_spread(0, holds)
    text_far(1)
    text_wait(1)

    img_own(1).wait()
    scores(1, z, ps, qs, student_scale)
    img_recv(1, 0, 1)
    scores(1, zm1, ps, qs, student_scale)
    img_recv(1, 1, 0)
    scores(1, zp1, ps, qs, student_scale)
    img_pass_on(0)
    text_pass_on(0)
    img_recv_far(1, 0)
    img_recv_far(1, 1)
    scores(1, zp2, ps, qs, student_scale)
    cols_start(1)
    rows_start(1)

    partner = (b, (1 - yh) * 4 + z)
    total_img = (
        is_[0].astype(F32) + is_[1].astype(F32) + is_[2].astype(F32) + is_[3].astype(F32)
    )
    for g in range(4):
        isum[0, g] = total_img[:HALF, g * 128 : (g + 1) * 128]
        isum[1, g] = total_img[HALF:, g * 128 : (g + 1) * 128]
    iy = copy(isum.at[1 - yh, z], isum_in.at[z], iy_s.at[0], iy_r.at[0], partner)
    start(iy)
    text_far(0)
    text_wait(0)

    img_own(0).wait()
    scores(0, z, pt, qt, teacher_scale)
    stats_middle(1)
    img_recv(0, 0, 1)
    scores(0, zm1, pt, qt, teacher_scale)
    img_recv(0, 1, 0)
    scores(0, zp1, pt, qt, teacher_scale)
    cols_start(0)
    stats_middle(0)
    img_recv_far(0, 0)
    img_recv_far(0, 1)
    scores(0, zp2, pt, qt, teacher_scale, far=True)
    start_all(1, 16, far_copy)
    rows_start(0)

    def iz_copy(d):
        slot = isum_in.at[z]
        return copy(slot, slot, iz_s.at[d - 1], iz_r.at[d - 1], znext(d))

    def iz_wait(d):
        slot = isum_in.at[lax.rem(z + 4 - d, 4)]
        copy(slot, slot, iz_s.at[d - 1], iz_r.at[d - 1], partner).wait_recv()

    iy.wait_recv()
    for d in (1, 3, 2):
        start(iz_copy(d))

    row_lse, col_lse = stats_finish(1)
    rl = lax.broadcasted_iota(jnp.int32, (4, 384), 0)
    cl = lax.broadcasted_iota(jnp.int32, (4, 384), 1)
    row_part = jnp.sum(jnp.where((rl == z) & (cl < ROWS), row_lse, 0.0), axis=0, keepdims=True)
    lse_part = (
        jnp.sum(row_part, axis=1, keepdims=True)
        + jnp.sum(jnp.sum(col_lse, axis=0, keepdims=True), axis=1, keepdims=True) * (1.0 / 16.0)
    )

    for d in (2, 1, 3, 0):
        v = lax.rem(z + d, 4)
        factor = jnp.sum(jnp.where(lane == v, rowfac[1, :ROWS, :], 0.0), axis=1, keepdims=True)
        w[v] = (ps[v] * factor + qs[v] * colfac[1, pl.ds(v, 1), :]).astype(BF16)
        gsend[d] = dot(w[v], ts[...], NN)

    def g_far(h):
        return copy(gsend.at[2, half(h)], gfar_in.at[h], g_s.at[2, h], g_r.at[2, h],
                    znext(1 if h == 0 else 3))

    def g_copy(i, h):
        d = 1 + 2 * i
        return copy(gsend.at[d, half(h)], grecv.at[i, half(h)], g_s.at[i, h], g_r.at[i, h],
                    znext(d))

    start(g_far(0))
    start(g_far(1))
    start(g_copy(0, 1))
    start(g_copy(1, 0))


    stats_finish(0)
    far_finish()


    def tgt_copy(n):
        return copy(tgt.at[n], tgt_in.at[n], tgt_s.at[n], tgt_r.at[n], partner)

    def own_targets(h, n):
        rows = pl.ds(pl.multiple_of(h * HALF + n * 48, 16), 48)
        acc = None
        for v in range(4):
            term = pt[v, rows] * rowfac[0, rows, v : v + 1] + qt[v, rows] * colfac[0, v : v + 1, :]
            acc = term if acc is None else acc + term
        return acc

    for n in range(NCH):
        tgt[n] = own_targets(1 - yh, n)
        start(tgt_copy(n))
    acc = dot(w[0], is_[0], TN)
    for v in range(1, 4):
        acc = acc + dot(w[v], is_[v], TN)
    gtp[...] = acc
    for n in range(NCH):
        tgt_mine[n] = own_targets(yh, n)

    for d in (1, 3, 2):
        iz_wait(d)
    for g in range(4):
        isum8[g] = isum_in[g] + isum[yh, g]
    for g in range(4):
        t = isum8[g]
        hi[:, g * 128 : (g + 1) * 128] = t.astype(BF16)
        lo[:, g * 128 : (g + 1) * 128] = (t - t.astype(BF16).astype(F32)).astype(BF16)
    for i in range(2):
        g_far(i).wait_recv()
        rows = slice(i * HALF, (i + 1) * HALF)
        gsend[1 + 2 * i, rows] = gsend[1 + 2 * i, rows] + gfar_in[i]
        start(g_copy(i, i))

    for n in range(NCH):
        tgt_copy(n).wait_recv()
        tw[n * 48 : (n + 1) * 48] = ((tgt_mine[n] + tgt_in[n]) * 0.125).astype(BF16)
    target_text = dot(tw[...], ts[...], NN)
    for g in range(4):
        tt_part[g] = target_text[:, g * 128 : (g + 1) * 128]

    def tz_copy(d):
        return copy(tt_part.at[lax.rem(z + d, 4)], tt_in.at[d - 1], tz_s.at[d - 1],
                    tz_r.at[d - 1], znext(d))

    for d in (2, 1, 3):
        start(tz_copy(d))

    res = gtp[...] - dot(tw[...], hi[...], TN) - dot(tw[...], lo[...], TN)
    for s in range(8):
        row = s * HALF
        for g in range(4):
            gtc[s % 2, s // 2, g] = res[row : row + HALF, g * 128 : (g + 1) * 128]
    def gc_copy(i):
        rows = slice(i * 72, (i + 1) * 72)
        return copy(gtc.at[1 - k, :, :, rows, :], gt_sib.at[:, :, rows, :], gc_s.at[i],
                    gc_r.at[i], sib)

    start(gc_copy(0))
    start(gc_copy(1))

    target_loss = isum8[0] * tt_part[0]
    for g in range(1, 4):
        target_loss = target_loss + isum8[g] * tt_part[g]
    target_loss = jnp.sum(jnp.sum(target_loss, axis=0, keepdims=True), axis=1, keepdims=True)
    part = lse_part - target_loss * student_scale
    loss_src[...] = jnp.broadcast_to(part, (8, 128))

    def lb_copy(d):
        return copy(loss_src, loss_b.at[d - 1], lb_s.at[d - 1], lb_r.at[d - 1],
                    (lax.rem(b + d, 16), a))

    start_all(1, 16, lb_copy)

    y = yh * 2 + yl
    pieces = gtc.at[k]

    def ydev(d):
        yd = lax.rem(y + d, 4)
        return dev(x, (yd % 2) * 2 + k, yd // 2, z)

    def xdev(d):
        return dev(lax.rem(x + d, 4), j, yh, z)

    def ra_copy(d):
        return copy(pieces.at[lax.rem(x + d, 4), :, 0:72, :], ra_in.at[d - 1],
                    rs_s.at[0, d - 1], rs_r.at[0, d - 1], xdev(d))

    def rb_copy(d):
        return copy(pieces.at[:, lax.rem(y + d, 4), 72:144, :], rb_in.at[d - 1],
                    rs_s.at[1, d - 1], rs_r.at[1, d - 1], ydev(d))

    def ra2_copy(d):
        return copy(ra_sum.at[lax.rem(y + d, 4)], ra2_in.at[d - 1],
                    rs_s.at[2, d - 1], rs_r.at[2, d - 1], ydev(d))

    def rb2_copy(d):
        return copy(rb_sum.at[lax.rem(x + d, 4)], rb2_in.at[d - 1],
                    rs_s.at[3, d - 1], rs_r.at[3, d - 1], xdev(d))

    for i in range(2):
        gc_copy(i).wait_recv()
        rows = slice(i * 72, (i + 1) * 72)
        for blk in range(4):
            for g in range(4):
                gtc[k, blk, g, rows, :] = gtc[k, blk, g, rows, :] + gt_sib[blk, g, rows, :]
        for d in ((1, 3, 2), (1, 3))[i]:
            start((ra_copy, rb_copy)[i](d))

    total = tt_part[z]
    for d in (1, 3, 2):
        tz_copy(d).wait_recv()
        total = total + tt_in[d - 1]
    tt_src[...] = total

    a_in = (1 - yh) * 4 + z
    ty = copy(tt_src, tt_all.at[a], ta_s.at[0], ta_r.at[a], partner)
    start(ty)
    start(rb_copy(2))

    def ta_copy(d):
        return copy(tt_src, tt_all.at[a], ta_s.at[d], ta_r.at[a], znext(d))

    def tb_copy(d):
        return copy(tt_all.at[a_in], tt_all.at[a_in], ta_s.at[3 + d], ta_r.at[a_in], znext(d))

    def t_wait(slot):
        copy(tt_src, tt_all.at[slot], ta_s.at[0], ta_r.at[slot], partner).wait_recv()

    for d in (1, 3, 2):
        start(ta_copy(d))
    tt_all[a] = total

    def lb_wait(d, acc):
        lb_copy(d).wait_recv()
        return acc + loss_b[d - 1]

    loss_src2[...] = lax.fori_loop(1, 16, lb_wait, loss_src[...])

    def la_copy(d):
        return copy(loss_src2, loss_a.at[d - 1], la_s.at[d - 1], la_r.at[d - 1],
                    (b, lax.rem(a + d, 8)))

    start_all(1, 8, la_copy)

    ra_sum[...] = gtc[k, x, :, 0:72, :]
    rb_sum[...] = gtc[k, :, y, 72:144, :]
    for d in (1, 3, 2):
        ra_copy(d).wait_recv()
        ra_sum[...] = ra_sum[...] + ra_in[d - 1]
    for d in (1, 3, 2):
        start(ra2_copy(d))
    for d in (1, 3, 2):
        rb_copy(d).wait_recv()
        rb_sum[...] = rb_sum[...] + rb_in[d - 1]
    for d in (1, 3, 2):
        start(rb2_copy(d))
    t_wait(a_in)
    for d in (1, 3, 2):
        start(tb_copy(d))
    first, last = ra_sum[y], rb_sum[x]
    for d in (1, 3, 2):
        ra2_copy(d).wait_recv()
        first = first + ra2_in[d - 1]
    for d in (1, 3, 2):
        rb2_copy(d).wait_recv()
        last = last + rb2_in[d - 1]
    fb_src[z, 0:72, :] = first
    fb_src[z, 72:144, :] = last

    def fz_copy(d):
        return copy(fb_src.at[z], fb_src.at[z], fz_s.at[d - 1], fz_r.at[d - 1], znext(d))

    def fb_copy(c, h):
        return copy(fb_src.at[c], fb_buf.at[j * 2 + yh], fb_s.at[c, h], fb_r.at[j * 2 + yh],
                    dev(x, c, h, z))

    def is_self(c, h):
        return (j == c) & (yh == h)

    def fb_send(c):
        for h in range(2):
            @pl.when(jnp.logical_not(is_self(c, h)))
            def _():
                fb_copy(c, h).start()

    def fb_gone():
        for c in range(4):
            for h in range(2):
                @pl.when(jnp.logical_not(is_self(c, h)))
                def _():
                    fb_copy(c, h).wait_send()

    sent.append(fb_gone)
    for d in (1, 3, 2):
        start(fz_copy(d))
    fb_send(z)
    for d in (1, 3, 2):
        c = lax.rem(z + 4 - d, 4)
        copy(fb_src.at[c], fb_src.at[c], fz_s.at[d - 1], fz_r.at[d - 1], partner).wait_recv()
        fb_send(c)
    fb_buf[j * 2 + yh] = fb_src[j]

    acc = gsend[0]
    for i in range(2):
        g_copy(i, 0).wait_recv()
        g_copy(i, 1).wait_recv()
        acc = acc + grecv[i]

    for d in (1, 3, 2):
        zd = lax.rem(z + d, 4)
        t_wait(yh * 4 + zd)
        t_wait((1 - yh) * 4 + zd)
    for h in range(2):
        rows = slice(h * HALF, (h + 1) * HALF)
        for g in range(4):
            lanes = slice(g * 128, (g + 1) * 128)
            grads_out[0, rows, lanes] = acc[rows, lanes] - tt_all[h * 4 + g]

    def la_wait(d, acc):
        la_copy(d).wait_recv()
        return acc + loss_a[d - 1]

    whole = lax.fori_loop(1, 8, la_wait, loss_src2[...])
    loss_out[0, 0] = jnp.sum(whole[0:1, 0:1]) * (1.0 / (2.0 * 8 * 4608))

    def fb_wait(s, _):
        @pl.when(s != j * 2 + yh)
        def _():
            copy(fb_src.at[0], fb_buf.at[s], fb_s.at[0, 0], fb_r.at[s], partner).wait_recv()

        return 0

    lax.fori_loop(0, 8, fb_wait, 0)
    for s in range(8):
        syl_, sk_, syh_ = s // 4, (s // 2) % 2, s % 2
        g = syh_ * 2 + syl_
        grads_out[1, sk_ * HALF : (sk_ + 1) * HALF, g * 128 : (g + 1) * 128] = fb_buf[s]

    for gone in sent:
        gone()


def per_device(student_image, student_text, teacher_image, teacher_text):
    vm = pl.BlockSpec(memory_space=pltpu.VMEM)
    dma = pltpu.SemaphoreType.DMA
    V = pltpu.VMEM
    sw, twd = student_image.shape[2], teacher_image.shape[2]
    loss, grads = pl.pallas_call(
        kernel,
        name="distill",
        out_shape=(
            jax.ShapeDtypeStruct((1, 1), F32),
            pltpu.VMEM((2, ROWS, sw), F32),
        ),
        in_specs=[pl.BlockSpec(memory_space=pl.ANY)] * 4,
        out_specs=(pl.BlockSpec(memory_space=pltpu.SMEM), vm),
        scratch_shapes=[
            V((4, ROWS, twd), BF16), V((4, ROWS, sw), BF16),
            V((4 * ROWS, twd), BF16), V((4 * ROWS, sw), BF16),
            V((4, ROWS, COLS), F32), V((4, ROWS, COLS), F32),
            V((4, ROWS, COLS), F32), V((4, ROWS, COLS), F32),
            V((4, ROWS, COLS), BF16),
            V((NCH, 48, COLS), F32), V((NCH, 48, COLS), F32), V((NCH, 48, COLS), F32),
            V((HALF, COLS), BF16),
            V((2, 4, HALF, 128), F32), V((4, HALF, 128), F32), V((4, HALF, 128), F32),
            V((HALF, sw), BF16), V((HALF, sw), BF16),
            V((4, HALF, 128), F32), V((3, HALF, 128), F32), V((HALF, 128), F32),
            V((8, HALF, 128), F32),
            V((4, ROWS, sw), F32), V((2, ROWS, sw), F32), V((2, HALF, sw), F32),
            V((COLS, sw), F32), V((4, 4, HALF, 128), F32),
            V((3, 4, 72, 128), F32), V((3, 4, 72, 128), F32), V((4, 72, 128), F32),
            V((4, 72, 128), F32), V((3, 72, 128), F32), V((3, 72, 128), F32),
            V((4, HALF, 128), F32), V((8, HALF, 128), F32),
            V((2, 4, 4, HALF, 128), F32),
            V((384, 128), F32), V((2, 8, 384), F32), V((2, 3, 8, 384), F32),
            V((2, 384, 128), F32), V((128, 384), F32),
            V((2, 8, COLS), F32), V((2, 3, 8, COLS), F32), V((2, 8, COLS), F32),
            V((2, 3, 8, COLS), F32), V((2, 8, COLS), F32),
            V((2, COLS), F32), V((15, 2, COLS), F32),
            V((8, 128), F32), V((15, 8, 128), F32), V((8, 128), F32), V((7, 8, 128), F32),
            dma((4,)), dma((2, 3, 2)), dma((2, 3, 2)),
            dma((2, 3)), dma((2,)), dma((2, 3)), dma((2, 3)), dma((2, 4)), dma((2, 4)),
            dma((2, 2)), dma((2, 2)), dma((3,)), dma((3,)),
            dma((1,)), dma((1,)), dma((3,)), dma((3,)), dma((3,)), dma((3,)), dma((7,)), dma((8,)),
            dma((15,)), dma((15,)),
            dma((2, 3)), dma((2, 3)), dma((2, 3)), dma((2, 3)), dma((2, 3)), dma((2, 3)),
            dma((3,)), dma((3,)), dma((3, 2)), dma((3, 2)), dma((2,)), dma((2,)),
            dma((4, 3)), dma((4, 3)), dma((3,)), dma((3,)), dma((4, 2)), dma((8,)),
            dma((15,)), dma((15,)), dma((7,)), dma((7,)),
        ],
        compiler_params=pltpu.CompilerParams(
            collective_id=0, has_side_effects=True, vmem_limit_bytes=58 * 1024 * 1024
        ),
        cost_estimate=pl.CostEstimate(
            flops=8 * 10**9, bytes_accessed=4 * 2**20, transcendentals=6 * 10**6
        ),
    )(student_image[0], student_text, teacher_image[0], teacher_text)
    scale = 3.0 / math.sqrt(sw)
    return loss.reshape(()), (grads[0] * scale)[None], grads[1] * scale


def solution(mesh):
    return jax.shard_map(
        per_device,
        mesh=mesh,
        in_specs=(
            P("aug", "batch", None),
            P("batch", None),
            P("aug", "batch", None),
            P("batch", None),
        ),
        out_specs=(P(), P("aug", "batch", None), P("batch", None)),
        check_vma=False,
    )
```

```python
import functools
import math

import jax
import jax.numpy as jnp
from jax import lax
from jax.experimental import pallas as pl
from jax.experimental.pallas import tpu as pltpu
from jax.sharding import PartitionSpec as P

MESH = pl.DeviceIdType.MESH
F32 = jnp.float32
BF16 = jnp.bfloat16
ROWS = 288
HALF = ROWS // 2
COLS = 4 * ROWS
NCH = 3
NT = (((1,), (1,)), ((), ()))
NN = (((1,), (0,)), ((), ()))
TN = (((0,), (0,)), ((), ()))


def dot(a, b, dims):
    return lax.dot_general(a, b, dims, preferred_element_type=F32)


def kernel(
    simg, stext, timg, ttext,
    loss_out, grads_out,
    it, is_, tt, ts, pt, qt, ps, qs, w, tgt, tgt_mine, tgt_in, tw,
    isum, isum_in, isum8, hi, lo, tt_part, tt_in, tt_src, tt_all,
    gsend, grecv, gfar_in, gtp, gt_sib, ra_in, rb_in, ra_sum, rb_sum, ra2_in, rb2_in, fb_src, fb_buf, gtc,
    rowst, rowsend, rowrecv, rowfac, rowtmp, colst, quad_in, colq, colx_in, colfac, cfar, cfar_in,
    loss_src, loss_b, loss_src2, loss_a,
    own_s, zi_s, zi_r, t1_s, t1_r, t2_s, t2_r, t3_s, t3_r, t4_s, t4_r, t5_s, t5_r,
    iy_s, iy_r, iz_s, iz_r, tz_s, tz_r, ta_s, ta_r,
    far_s, far_r, quad_s, quad_r, row_s, row_r, col_s, col_r, tgt_s, tgt_r, g_s, g_r, gc_s, gc_r,
    rs_s, rs_r, fz_s, fz_r, fb_s, fb_r, lb_s, lb_r, la_s, la_r,
):
    b = lax.axis_index("batch")
    a = lax.axis_index("aug")
    x, j = b // 4, b % 4
    yl, k = j // 2, j % 2
    yh, z = a // 4, a % 4
    sib = (b + 1 - 2 * k, a)
    teacher_scale = 3.0 / math.sqrt(timg.shape[1])
    student_scale = 3.0 / math.sqrt(simg.shape[1])

    def dev(x_, j_, yh_, z_):
        return (x_ * 4 + j_, yh_ * 4 + z_)

    def znext(d):
        return (b, yh * 4 + lax.rem(z + d, 4))

    def copy(src, dst, ss, rs, to):
        return pltpu.make_async_remote_copy(
            src_ref=src, dst_ref=dst, send_sem=ss, recv_sem=rs, device_id=to, device_id_type=MESH
        )

    sent = []

    def start(c):
        c.start()
        sent.append(c.wait_send)

    def start_if(cond, c):
        @pl.when(cond)
        def _():
            c.start()

        def gone():
            @pl.when(cond)
            def _():
                c.wait_send()

        sent.append(gone)

    def start_group(copies, into, ss, rs):
        for c in copies:
            c.start()
        sent.append(copy(into, into, ss, rs, sib).wait_send)

    def take_group(into, ss, rs):
        copy(into, into, ss, rs, sib).wait_recv()

    def start_all(lo, hi, make, into, ss, rs):
        def go(i, _):
            make(i).start()
            return 0

        lax.fori_loop(lo, hi, go, 0)
        sent.append(copy(into, into, ss, rs, sib).wait_send)

    barrier = pltpu.get_barrier_semaphore()

    near = [(b, yh * 4 + lax.rem(z + d, 4)) for d in (1, 2, 3)]
    near += [(lax.rem(x + d, 4) * 4 + j, a) for d in (1, 2, 3)]
    near += [(x * 4 + lax.rem(j + d, 4), a) for d in (1, 2, 3)]
    near += [(x * 4 + lax.rem(j + d, 4), (1 - yh) * 4 + z) for d in range(4)]
    for peer in near:
        pl.semaphore_signal(barrier, 1, device_id=peer, device_id_type=MESH)
    pl.semaphore_wait(barrier, len(near))

    zm1, zp1, zp2 = lax.rem(z + 3, 4), lax.rem(z + 1, 4), lax.rem(z + 2, 4)
    own = (timg, simg)
    imgs = (it, is_)
    texts = (tt, ts)
    own_text = (ttext, stext)

    def half(h):
        return pl.ds(h * HALF, HALF)

    def img_send(m, d, h):
        return copy(
            own[m].at[half(h)], imgs[m].at[z, half(h)], zi_s.at[m, d, h], zi_r.at[m, d, h],
            znext(1 if d == 0 else 3),
        )

    def img_relay(m, d):
        slot = zm1 if d == 0 else zp1
        ref = imgs[m].at[slot, half(d)]
        return copy(ref, ref, zi_s.at[m, 2, d], zi_r.at[m, 2, d], znext(1 if d == 0 else 3))

    def img_recv(m, d, h):
        slot = zm1 if d == 0 else zp1
        ref = imgs[m].at[slot, half(h)]
        copy(ref, ref, zi_s.at[m, d, h], zi_r.at[m, d, h], znext(1)).wait_recv()

    def img_recv_far(m, d):
        ref = imgs[m].at[zp2, half(d)]
        copy(ref, ref, zi_s.at[m, 2, d], zi_r.at[m, 2, d], znext(1)).wait_recv()

    def img_start(m):
        start(img_send(m, 0, 0))
        start(img_send(m, 1, 1))

    def img_rest(m):
        start(img_send(m, 0, 1))
        start(img_send(m, 1, 0))

    def img_pass_on(m):
        img_recv(m, 0, 0)
        start(img_relay(m, 0))
        img_recv(m, 1, 1)
        start(img_relay(m, 1))

    syl, sk = z // 2, z % 2
    is_source = j == z

    def tslab(m, blk, h):
        return texts[m].at[pl.ds(blk * ROWS + h * HALF, HALF)]

    def text_first(m):
        return (
            copy(own_text[m].at[pl.ds((1 - sk) * HALF, HALF)], tslab(m, x, 1 - sk),
                 t1_s.at[m, 0], t1_r.at[m], dev(x, syl * 2 + 1 - sk, yh, z)),
            copy(own_text[m].at[half(0)], tslab(m, x, 0),
                 t1_s.at[m, 1], t1_r.at[m], dev(x, (1 - syl) * 2, yh, z)),
            copy(own_text[m].at[half(1)], tslab(m, x, 1),
                 t1_s.at[m, 2], t1_r.at[m], dev(x, (1 - syl) * 2 + 1, 1 - yh, z)),
        )

    def text_own(m):
        return pltpu.make_async_copy(
            own_text[m].at[pl.ds(k * HALF, HALF)], tslab(m, x, k), own_s.at[2 + m]
        )

    def img_own(m):
        return pltpu.make_async_copy(own[m], imgs[m].at[z], own_s.at[m])

    def text_start(m):
        @pl.when(is_source)
        def _():
            for c in text_first(m):
                c.start()
            text_own(m).start()

        def gone():
            @pl.when(is_source)
            def _():
                for c in text_first(m):
                    c.wait_send()

        sent.append(gone)

    def text_x(m, d):
        return copy(tslab(m, x, k), tslab(m, x, k), t2_s.at[m, d - 1], t2_r.at[m, d - 1],
                    (lax.rem(x + d, 4) * 4 + j, a))

    def text_got(m, d):
        slab = tslab(m, lax.rem(x + 4 - d, 4), k)
        copy(slab, slab, t2_s.at[m, d - 1], t2_r.at[m, d - 1], sib).wait_recv()

    def tlanes(m, blk, i):
        width = texts[m].shape[1] // 2
        return texts[m].at[pl.ds(blk * ROWS + k * HALF, HALF), i * width : (i + 1) * width]

    def text_relay(m, i):
        ref = tlanes(m, lax.rem(x + 3 - 2 * i, 4), i)
        return copy(ref, ref, t4_s.at[m, i], t4_r.at[m, i], (lax.rem(x + 1 + 2 * i, 4) * 4 + j, a))

    def text_sib(m, d):
        blk = lax.rem(x + 4 - d, 4)
        return copy(tslab(m, blk, k), tslab(m, blk, k), t3_s.at[m, d], t3_r.at[m, d], sib)

    holds = yl == syl
    lacks = yl != syl

    def text_cross(d):
        slab = tslab(1, lax.rem(x + 4 - d, 4), k)
        to = dev(x, (1 - syl) * 2 + k, yh + k * (1 - 2 * yh), z)
        return copy(slab, slab, t5_s.at[d - 1], t5_r.at[d - 1], to)

    def crossed(d):
        @pl.when(lacks)
        def _():
            slab = tslab(1, lax.rem(x + 4 - d, 4), k)
            copy(slab, slab, t5_s.at[d - 1], t5_r.at[d - 1], sib).wait_recv()

    def text_spread(m, here):
        @pl.when(here & jnp.logical_not(is_source))
        def _():
            copy(tslab(m, x, k), tslab(m, x, k), t1_s.at[m, 0], t1_r.at[m], sib).wait_recv()

        @pl.when(here & is_source)
        def _():
            text_own(m).wait()

        for d in (1, 3):
            if m == 0 or here is holds:
                start_if(here, text_x(m, d))
        start_if(here, text_sib(m, 0))

    def text_pass_on(m):
        for d in (1, 3):
            if m:
                @pl.when(holds)
                def _():
                    text_got(m, d)

                start_if(holds, text_relay(m, d // 2))
                start_if(holds, text_cross(d))
                crossed(d)
            else:
                text_got(m, d)
                start(text_relay(m, d // 2))
            start(text_sib(m, d))

    def text_far(m):
        def arrived():
            for i in range(2):
                ref = tlanes(m, lax.rem(x + 2, 4), i)
                copy(ref, ref, t4_s.at[m, i], t4_r.at[m, i], sib).wait_recv()

        if m:
            pl.when(holds)(arrived)
            start_if(holds, text_cross(2))
            crossed(2)
        else:
            arrived()
        start(text_sib(m, 2))

    def text_wait(m):
        for d in range(4):
            blk = lax.rem(x + 4 - d, 4)
            copy(tslab(m, blk, 1 - k), tslab(m, blk, 1 - k), t3_s.at[m, d], t3_r.at[m, d],
                 sib).wait_recv()

    lane = lax.broadcasted_iota(jnp.int32, (ROWS, 128), 1)

    def fold(op, t):
        return functools.reduce(op, [t[:, i * 128 : (i + 1) * 128] for i in range(COLS // 128)])

    def scores(m, v, pr, qr, scale, far=False):
        t = dot(imgs[m][v], texts[m][...], NT) * scale
        cm = jnp.max(t, axis=0, keepdims=True)
        top = jnp.max(fold(jnp.maximum, t), axis=1, keepdims=True)
        q = jnp.exp(t - cm)
        qr[v] = q
        p = jnp.exp(t - top)
        pr[v] = p
        cs = jnp.sum(q, axis=0, keepdims=True)
        if far:
            cfar[0:1, :] = cm
            cfar[1:2, :] = cs
        else:
            colst[m, pl.ds(v, 1), :] = cm
            colst[m, pl.ds(v + 4, 1), :] = cs
        total = jnp.sum(fold(jnp.add, p), axis=1, keepdims=True)
        rowst[:ROWS, :] = jnp.where(
            lane == v, top, jnp.where(lane == v + 4, total, rowst[:ROWS, :])
        )

    def row_copy(m, d):
        return copy(rowsend.at[m], rowrecv.at[m, d - 1], row_s.at[m], row_r.at[m],
                    znext(d))

    def quad_copy(m, d):
        return copy(colst.at[m], quad_in.at[m, d - 1], quad_s.at[m], quad_r.at[m],
                    (x * 4 + lax.rem(j + d, 4), a))

    def col_copy(m, d):
        return copy(colq.at[m], colx_in.at[m, d - 1], col_s.at[m], col_r.at[m],
                    (lax.rem(x + d, 4) * 4 + j, a))

    def merged(mine, others):
        top = functools.reduce(jnp.maximum, [t[:4] for t in others], mine[:4])
        total = mine[4:] * jnp.exp(mine[:4] - top)
        for t in others:
            total = total + t[4:] * jnp.exp(t[:4] - top)
        return top, total

    def far_copy(d):
        return copy(cfar, cfar_in.at[d - 1], far_s.at[0], far_r.at[0],
                    (lax.rem(b + d, 16), a))

    def far_finish():
        take_group(cfar_in, far_s.at[0], far_r.at[0])

        def arrived(d, top):
            return jnp.maximum(top, cfar_in[d - 1, 0:1, :])

        mine = cfar[0:1, :]
        top = lax.fori_loop(1, 16, arrived, mine)

        def add(d, total):
            return total + cfar_in[d, 1:2, :] * jnp.exp(cfar_in[d, 0:1, :] - top)

        total = lax.fori_loop(0, 15, add, cfar[1:2, :] * jnp.exp(mine - top))
        colfac[0, pl.ds(zp2, 1), :] = jnp.exp(mine - top - jnp.log(total))

    def cols_start(m):
        start_group([quad_copy(m, d) for d in (1, 2, 3)], quad_in.at[m], quad_s.at[m], quad_r.at[m])

    def rows_start(m):
        rowsend[m] = jnp.transpose(rowst[...])[:8]
        start_group([row_copy(m, d) for d in (1, 3, 2)], rowrecv.at[m], row_s.at[m], row_r.at[m])

    def stats_middle(m):
        take_group(quad_in.at[m], quad_s.at[m], quad_r.at[m])
        top, total = merged(colst[m], [quad_in[m, d] for d in range(3)])
        colq[m, 0:4, :] = top
        colq[m, 4:8, :] = total
        start_group([col_copy(m, d) for d in (1, 3, 2)], colx_in.at[m], col_s.at[m], col_r.at[m])

    def stats_finish(m):
        take_group(rowrecv.at[m], row_s.at[m], row_r.at[m])
        mine = rowsend[m]
        top, total = merged(mine, [rowrecv[m, d] for d in range(3)])
        row_lse = top + jnp.log(total)
        rowtmp[0:4, :] = jnp.exp(mine[:4] - row_lse)
        rowfac[m] = jnp.transpose(rowtmp[...])
        take_group(colx_in.at[m], col_s.at[m], col_r.at[m])
        top, total = merged(colq[m], [colx_in[m, d] for d in range(3)])
        col_lse = top + jnp.log(total)
        colfac[m, 0:4, :] = jnp.exp(colst[m, 0:4, :] - col_lse)
        return row_lse, col_lse

    rowst[...] = jnp.ones_like(rowst)
    rowtmp[...] = jnp.zeros_like(rowtmp)
    colst[0] = jnp.ones_like(colst[0])
    img_start(1)
    img_rest(1)
    text_start(1)
    img_start(0)
    text_start(0)
    img_own(1).start()
    img_own(0).start()
    text_spread(1, holds)
    text_spread(1, lacks)
    text_spread(0, lacks)
    img_pass_on(1)
    img_rest(0)
    text_pass_on(1)
    text_spread(0, holds)
    text_far(1)
    text_wait(1)

    img_own(1).wait()
    scores(1, z, ps, qs, student_scale)
    img_recv(1, 0, 1)
    scores(1, zm1, ps, qs, student_scale)
    img_recv(1, 1, 0)
    scores(1, zp1, ps, qs, student_scale)
    img_pass_on(0)
    text_pass_on(0)
    img_recv_far(1, 0)
    img_recv_far(1, 1)
    scores(1, zp2, ps, qs, student_scale)
    cols_start(1)
    rows_start(1)

    partner = (b, (1 - yh) * 4 + z)
    total_img = (
        is_[0].astype(F32) + is_[1].astype(F32) + is_[2].astype(F32) + is_[3].astype(F32)
    )
    for g in range(4):
        isum[0, g] = total_img[:HALF, g * 128 : (g + 1) * 128]
        isum[1, g] = total_img[HALF:, g * 128 : (g + 1) * 128]
    iy = copy(isum.at[1 - yh, z], isum_in.at[z], iy_s.at[0], iy_r.at[0], partner)
    start(iy)
    text_far(0)
    text_wait(0)

    img_own(0).wait()
    scores(0, z, pt, qt, teacher_scale)
    stats_middle(1)
    img_recv(0, 0, 1)
    scores(0, zm1, pt, qt, teacher_scale)
    img_recv(0, 1, 0)
    scores(0, zp1, pt, qt, teacher_scale)
    cols_start(0)
    stats_middle(0)
    img_recv_far(0, 0)
    img_recv_far(0, 1)
    scores(0, zp2, pt, qt, teacher_scale, far=True)
    start_all(1, 16, far_copy, cfar_in, far_s.at[0], far_r.at[0])
    rows_start(0)

    def iz_copy(d):
        slot = isum_in.at[z]
        return copy(slot, slot, iz_s.at[d - 1], iz_r.at[d - 1], znext(d))

    def iz_wait(d):
        slot = isum_in.at[lax.rem(z + 4 - d, 4)]
        copy(slot, slot, iz_s.at[d - 1], iz_r.at[d - 1], partner).wait_recv()

    iy.wait_recv()
    for d in (1, 3, 2):
        start(iz_copy(d))

    row_lse, col_lse = stats_finish(1)
    rl = lax.broadcasted_iota(jnp.int32, (4, 384), 0)
    cl = lax.broadcasted_iota(jnp.int32, (4, 384), 1)
    row_part = jnp.sum(jnp.where((rl == z) & (cl < ROWS), row_lse, 0.0), axis=0, keepdims=True)
    lse_part = (
        jnp.sum(row_part, axis=1, keepdims=True)
        + jnp.sum(jnp.sum(col_lse, axis=0, keepdims=True), axis=1, keepdims=True) * (1.0 / 16.0)
    )

    for d in (2, 1, 3, 0):
        v = lax.rem(z + d, 4)
        factor = jnp.sum(jnp.where(lane == v, rowfac[1, :ROWS, :], 0.0), axis=1, keepdims=True)
        w[v] = (ps[v] * factor + qs[v] * colfac[1, pl.ds(v, 1), :]).astype(BF16)
        gsend[d] = dot(w[v], ts[...], NN)

    def g_far(h):
        return copy(gsend.at[2, half(h)], gfar_in.at[h], g_s.at[2, h], g_r.at[2, h],
                    znext(1 if h == 0 else 3))

    def g_copy(i, h):
        d = 1 + 2 * i
        return copy(gsend.at[d, half(h)], grecv.at[i, half(h)], g_s.at[i, h], g_r.at[i, h],
                    znext(d))

    start(g_far(0))
    start(g_far(1))
    start(g_copy(0, 1))
    start(g_copy(1, 0))


    stats_finish(0)
    far_finish()


    def tgt_copy(n):
        return copy(tgt.at[n], tgt_in.at[n], tgt_s.at[n], tgt_r.at[n], partner)

    def own_targets(h, n):
        rows = pl.ds(pl.multiple_of(h * HALF + n * 48, 16), 48)
        acc = None
        for v in range(4):
            term = pt[v, rows] * rowfac[0, rows, v : v + 1] + qt[v, rows] * colfac[0, v : v + 1, :]
            acc = term if acc is None else acc + term
        return acc

    for n in range(NCH):
        tgt[n] = own_targets(1 - yh, n)
        start(tgt_copy(n))
    acc = dot(w[0], is_[0], TN)
    for v in range(1, 4):
        acc = acc + dot(w[v], is_[v], TN)
    gtp[...] = acc
    for n in range(NCH):
        tgt_mine[n] = own_targets(yh, n)

    for d in (1, 3, 2):
        iz_wait(d)
    for g in range(4):
        isum8[g] = isum_in[g] + isum[yh, g]
    for g in range(4):
        t = isum8[g]
        hi[:, g * 128 : (g + 1) * 128] = t.astype(BF16)
        lo[:, g * 128 : (g + 1) * 128] = (t - t.astype(BF16).astype(F32)).astype(BF16)
    for i in range(2):
        g_far(i).wait_recv()
        rows = slice(i * HALF, (i + 1) * HALF)
        gsend[1 + 2 * i, rows] = gsend[1 + 2 * i, rows] + gfar_in[i]
        start(g_copy(i, i))

    for n in range(NCH):
        tgt_copy(n).wait_recv()
        tw[n * 48 : (n + 1) * 48] = ((tgt_mine[n] + tgt_in[n]) * 0.125).astype(BF16)
    res = gtp[...] - dot(tw[...], hi[...], TN) - dot(tw[...], lo[...], TN)
    for s in range(8):
        row = s * HALF
        for g in range(4):
            gtc[s % 2, s // 2, g] = res[row : row + HALF, g * 128 : (g + 1) * 128]
    def gc_copy(i):
        rows = slice(i * 72, (i + 1) * 72)
        return copy(gtc.at[1 - k, :, :, rows, :], gt_sib.at[:, :, rows, :], gc_s.at[i],
                    gc_r.at[i], sib)

    start(gc_copy(0))
    start(gc_copy(1))

    target_text = dot(tw[...], ts[...], NN)
    for g in range(4):
        tt_part[g] = target_text[:, g * 128 : (g + 1) * 128]

    def tz_copy(d):
        return copy(tt_part.at[lax.rem(z + d, 4)], tt_in.at[d - 1], tz_s.at[0],
                    tz_r.at[0], znext(d))

    start_group([tz_copy(d) for d in (2, 1, 3)], tt_in, tz_s.at[0], tz_r.at[0])

    target_loss = isum8[0] * tt_part[0]
    for g in range(1, 4):
        target_loss = target_loss + isum8[g] * tt_part[g]
    target_loss = jnp.sum(jnp.sum(target_loss, axis=0, keepdims=True), axis=1, keepdims=True)
    part = lse_part - target_loss * student_scale
    loss_src[...] = jnp.broadcast_to(part, (8, 128))

    def lb_copy(d):
        return copy(loss_src, loss_b.at[d - 1], lb_s.at[0], lb_r.at[0],
                    (lax.rem(b + d, 16), a))

    start_all(1, 16, lb_copy, loss_b, lb_s.at[0], lb_r.at[0])

    y = yh * 2 + yl
    pieces = gtc.at[k]

    def ydev(d):
        yd = lax.rem(y + d, 4)
        return dev(x, (yd % 2) * 2 + k, yd // 2, z)

    def xdev(d):
        return dev(lax.rem(x + d, 4), j, yh, z)

    def ra_copy(d):
        return copy(pieces.at[lax.rem(x + d, 4), :, 0:72, :], ra_in.at[d - 1],
                    rs_s.at[0], rs_r.at[0], xdev(d))

    def rb_copy(d):
        return copy(pieces.at[:, lax.rem(y + d, 4), 72:144, :], rb_in.at[d - 1],
                    rs_s.at[1], rs_r.at[1], ydev(d))

    def ra2_copy(d):
        return copy(ra_sum.at[lax.rem(y + d, 4)], ra2_in.at[d - 1],
                    rs_s.at[2], rs_r.at[2], ydev(d))

    def rb2_copy(d):
        return copy(rb_sum.at[lax.rem(x + d, 4)], rb2_in.at[d - 1],
                    rs_s.at[3], rs_r.at[3], xdev(d))

    for i in range(2):
        gc_copy(i).wait_recv()
        rows = slice(i * 72, (i + 1) * 72)
        for blk in range(4):
            for g in range(4):
                gtc[k, blk, g, rows, :] = gtc[k, blk, g, rows, :] + gt_sib[blk, g, rows, :]
        if i == 0:
            start_group([ra_copy(d) for d in (1, 3, 2)], ra_in, rs_s.at[0], rs_r.at[0])
        else:
            start_group([rb_copy(d) for d in (1, 3)], rb_in, rs_s.at[1], rs_r.at[1])

    total = tt_part[z]
    take_group(tt_in, tz_s.at[0], tz_r.at[0])
    for d in (1, 3, 2):
        total = total + tt_in[d - 1]
    tt_src[...] = total

    a_in = (1 - yh) * 4 + z
    ty = copy(tt_src, tt_all.at[a], ta_s.at[0], ta_r.at[a], partner)
    start(ty)
    rb_copy(2).start()

    def ta_copy(d):
        return copy(tt_src, tt_all.at[a], ta_s.at[d], ta_r.at[a], znext(d))

    def tb_copy(d):
        return copy(tt_all.at[a_in], tt_all.at[a_in], ta_s.at[3 + d], ta_r.at[a_in], znext(d))

    def t_wait(slot):
        copy(tt_src, tt_all.at[slot], ta_s.at[0], ta_r.at[slot], partner).wait_recv()

    for d in (1, 3, 2):
        start(ta_copy(d))
    tt_all[a] = total

    take_group(loss_b, lb_s.at[0], lb_r.at[0])

    def lb_wait(d, acc):
        return acc + loss_b[d - 1]

    loss_src2[...] = lax.fori_loop(1, 16, lb_wait, loss_src[...])

    def la_copy(d):
        return copy(loss_src2, loss_a.at[d - 1], la_s.at[0], la_r.at[0],
                    (b, lax.rem(a + d, 8)))

    start_all(1, 8, la_copy, loss_a, la_s.at[0], la_r.at[0])

    ra_sum[...] = gtc[k, x, :, 0:72, :]
    rb_sum[...] = gtc[k, :, y, 72:144, :]
    take_group(ra_in, rs_s.at[0], rs_r.at[0])
    for d in (1, 3, 2):
        ra_sum[...] = ra_sum[...] + ra_in[d - 1]
    start_group([ra2_copy(d) for d in (1, 3, 2)], ra2_in, rs_s.at[2], rs_r.at[2])
    take_group(rb_in, rs_s.at[1], rs_r.at[1])
    for d in (1, 3, 2):
        rb_sum[...] = rb_sum[...] + rb_in[d - 1]
    start_group([rb2_copy(d) for d in (1, 3, 2)], rb2_in, rs_s.at[3], rs_r.at[3])
    t_wait(a_in)
    for d in (1, 3, 2):
        start(tb_copy(d))
    def fz_copy(c, i, d):
        ref = fb_src.at[c, i * 72 : (i + 1) * 72]
        return copy(ref, ref, fz_s.at[i, d - 1], fz_r.at[i, d - 1], znext(d))

    first = ra_sum[y]
    take_group(ra2_in, rs_s.at[2], rs_r.at[2])
    for d in (1, 3, 2):
        first = first + ra2_in[d - 1]
    fb_src[z, 0:72, :] = first
    for d in (1, 3, 2):
        start(fz_copy(z, 0, d))
    last = rb_sum[x]
    take_group(rb2_in, rs_s.at[3], rs_r.at[3])
    for d in (1, 3, 2):
        last = last + rb2_in[d - 1]
    fb_src[z, 72:144, :] = last
    for d in (1, 3, 2):
        start(fz_copy(z, 1, d))

    def fb_copy(c, h):
        return copy(fb_src.at[c], fb_buf.at[j * 2 + yh], fb_s.at[c, h], fb_r.at[j * 2 + yh],
                    dev(x, c, h, z))

    def is_self(c, h):
        return (j == c) & (yh == h)

    def fb_send(c):
        for h in range(2):
            @pl.when(jnp.logical_not(is_self(c, h)))
            def _():
                fb_copy(c, h).start()

    def fb_gone():
        for c in range(4):
            for h in range(2):
                @pl.when(jnp.logical_not(is_self(c, h)))
                def _():
                    fb_copy(c, h).wait_send()

    sent.append(fb_gone)
    fb_send(z)
    for d in (1, 3, 2):
        c = lax.rem(z + 4 - d, 4)
        fz_copy(c, 0, d).wait_recv()
        fz_copy(c, 1, d).wait_recv()
        fb_send(c)
    fb_buf[j * 2 + yh] = fb_src[j]

    acc = gsend[0]
    for i in range(2):
        g_copy(i, 0).wait_recv()
        g_copy(i, 1).wait_recv()
        acc = acc + grecv[i]

    for d in (1, 3, 2):
        zd = lax.rem(z + d, 4)
        t_wait(yh * 4 + zd)
        t_wait((1 - yh) * 4 + zd)
    for h in range(2):
        rows = slice(h * HALF, (h + 1) * HALF)
        for g in range(4):
            lanes = slice(g * 128, (g + 1) * 128)
            grads_out[0, rows, lanes] = acc[rows, lanes] - tt_all[h * 4 + g]

    take_group(loss_a, la_s.at[0], la_r.at[0])

    def la_wait(d, acc):
        return acc + loss_a[d - 1]

    whole = lax.fori_loop(1, 8, la_wait, loss_src2[...])
    loss_out[0, 0] = jnp.sum(whole[0:1, 0:1]) * (1.0 / (2.0 * 8 * 4608))

    def fb_wait(s, _):
        @pl.when(s != j * 2 + yh)
        def _():
            copy(fb_src.at[0], fb_buf.at[s], fb_s.at[0, 0], fb_r.at[s], partner).wait_recv()

        return 0

    lax.fori_loop(0, 8, fb_wait, 0)
    for s in range(8):
        syl_, sk_, syh_ = s // 4, (s // 2) % 2, s % 2
        g = syh_ * 2 + syl_
        grads_out[1, sk_ * HALF : (sk_ + 1) * HALF, g * 128 : (g + 1) * 128] = fb_buf[s]

    for gone in sent:
        gone()


def per_device(student_image, student_text, teacher_image, teacher_text):
    vm = pl.BlockSpec(memory_space=pltpu.VMEM)
    dma = pltpu.SemaphoreType.DMA
    V = pltpu.VMEM
    sw, twd = student_image.shape[2], teacher_image.shape[2]
    loss, grads = pl.pallas_call(
        kernel,
        name="distill",
        out_shape=(
            jax.ShapeDtypeStruct((1, 1), F32),
            pltpu.VMEM((2, ROWS, sw), F32),
        ),
        in_specs=[pl.BlockSpec(memory_space=pl.ANY)] * 4,
        out_specs=(pl.BlockSpec(memory_space=pltpu.SMEM), vm),
        scratch_shapes=[
            V((4, ROWS, twd), BF16), V((4, ROWS, sw), BF16),
            V((4 * ROWS, twd), BF16), V((4 * ROWS, sw), BF16),
            V((4, ROWS, COLS), F32), V((4, ROWS, COLS), F32),
            V((4, ROWS, COLS), F32), V((4, ROWS, COLS), F32),
            V((4, ROWS, COLS), BF16),
            V((NCH, 48, COLS), F32), V((NCH, 48, COLS), F32), V((NCH, 48, COLS), F32),
            V((HALF, COLS), BF16),
            V((2, 4, HALF, 128), F32), V((4, HALF, 128), F32), V((4, HALF, 128), F32),
            V((HALF, sw), BF16), V((HALF, sw), BF16),
            V((4, HALF, 128), F32), V((3, HALF, 128), F32), V((HALF, 128), F32),
            V((8, HALF, 128), F32),
            V((4, ROWS, sw), F32), V((2, ROWS, sw), F32), V((2, HALF, sw), F32),
            V((COLS, sw), F32), V((4, 4, HALF, 128), F32),
            V((3, 4, 72, 128), F32), V((3, 4, 72, 128), F32), V((4, 72, 128), F32),
            V((4, 72, 128), F32), V((3, 72, 128), F32), V((3, 72, 128), F32),
            V((4, HALF, 128), F32), V((8, HALF, 128), F32),
            V((2, 4, 4, HALF, 128), F32),
            V((384, 128), F32), V((2, 8, 384), F32), V((2, 3, 8, 384), F32),
            V((2, 384, 128), F32), V((128, 384), F32),
            V((2, 8, COLS), F32), V((2, 3, 8, COLS), F32), V((2, 8, COLS), F32),
            V((2, 3, 8, COLS), F32), V((2, 8, COLS), F32),
            V((2, COLS), F32), V((15, 2, COLS), F32),
            V((8, 128), F32), V((15, 8, 128), F32), V((8, 128), F32), V((7, 8, 128), F32),
            dma((4,)), dma((2, 3, 2)), dma((2, 3, 2)),
            dma((2, 3)), dma((2,)), dma((2, 3)), dma((2, 3)), dma((2, 4)), dma((2, 4)),
            dma((2, 2)), dma((2, 2)), dma((3,)), dma((3,)),
            dma((1,)), dma((1,)), dma((3,)), dma((3,)), dma((1,)), dma((1,)), dma((7,)), dma((8,)),
            dma((1,)), dma((1,)), dma((2,)), dma((2,)), dma((2,)), dma((2,)), dma((2,)), dma((2,)),
            dma((3,)), dma((3,)), dma((3, 2)), dma((3, 2)), dma((2,)), dma((2,)),
            dma((4,)), dma((4,)), dma((2, 3)), dma((2, 3)), dma((4, 2)), dma((8,)),
            dma((1,)), dma((1,)), dma((1,)), dma((1,)),
        ],
        compiler_params=pltpu.CompilerParams(
            collective_id=0, has_side_effects=True, vmem_limit_bytes=58 * 1024 * 1024
        ),
        cost_estimate=pl.CostEstimate(
            flops=8 * 10**9, bytes_accessed=4 * 2**20, transcendentals=6 * 10**6
        ),
    )(student_image[0], student_text, teacher_image[0], teacher_text)
    scale = 3.0 / math.sqrt(sw)
    return loss.reshape(()), (grads[0] * scale)[None], grads[1] * scale


def solution(mesh):
    return jax.shard_map(
        per_device,
        mesh=mesh,
        in_specs=(
            P("aug", "batch", None),
            P("batch", None),
            P("aug", "batch", None),
            P("batch", None),
        ),
        out_specs=(P(), P("aug", "batch", None), P("batch", None)),
        check_vma=False,
    )
```

```python
import functools
import math

import jax
import jax.numpy as jnp
from jax import lax
from jax.experimental import pallas as pl
from jax.experimental.pallas import tpu as pltpu
from jax.sharding import PartitionSpec as P

MESH = pl.DeviceIdType.MESH
F32 = jnp.float32
BF16 = jnp.bfloat16
ROWS = 288
HALF = ROWS // 2
COLS = 4 * ROWS
NCH = 3
NT = (((1,), (1,)), ((), ()))
NN = (((1,), (0,)), ((), ()))
TN = (((0,), (0,)), ((), ()))


def dot(a, b, dims):
    return lax.dot_general(a, b, dims, preferred_element_type=F32)


def kernel(
    simg, stext, timg, ttext,
    loss_out, grads_out,
    it, is_, tt, ts, pt, qt, ps, qs, w, tgt, tgt_mine, tgt_in, tw,
    isum, isum_in, isum8, hi, lo, tt_part, tt_in, tt_src, tt_all,
    gsend, grecv, gfar_in, gtp, gt_sib, ra_in, rb_in, ra_sum, rb_sum, ra2_in, rb2_in, fb_src, fb_buf, gtc,
    rowst, rowsend, rowrecv, rowfac, rowtmp, colst, quad_in, colq, colx_in, colfac, cfar, cfar_in,
    loss_src, loss_b, loss_src2, loss_a,
    own_s, zi_s, zi_r, t1_s, t1_r, t2_s, t2_r, t3_s, t3_r, t4_s, t4_r, t5_s, t5_r,
    iy_s, iy_r, iz_s, iz_r, tz_s, tz_r, ta_s, ta_r,
    far_s, far_r, quad_s, quad_r, row_s, row_r, col_s, col_r, tgt_s, tgt_r, g_s, g_r, gc_s, gc_r,
    rs_s, rs_r, fz_s, fz_r, fb_s, fb_r, lb_s, lb_r, la_s, la_r,
):
    b = lax.axis_index("batch")
    a = lax.axis_index("aug")
    x, j = b // 4, b % 4
    yl, k = j // 2, j % 2
    yh, z = a // 4, a % 4
    sib = (b + 1 - 2 * k, a)
    teacher_scale = 3.0 / math.sqrt(timg.shape[1])
    student_scale = 3.0 / math.sqrt(simg.shape[1])

    def dev(x_, j_, yh_, z_):
        return (x_ * 4 + j_, yh_ * 4 + z_)

    def znext(d):
        return (b, yh * 4 + lax.rem(z + d, 4))

    def copy(src, dst, ss, rs, to):
        return pltpu.make_async_remote_copy(
            src_ref=src, dst_ref=dst, send_sem=ss, recv_sem=rs, device_id=to, device_id_type=MESH
        )

    sent = []

    def start(c):
        c.start()
        sent.append(c.wait_send)

    def start_if(cond, c):
        @pl.when(cond)
        def _():
            c.start()

        def gone():
            @pl.when(cond)
            def _():
                c.wait_send()

        sent.append(gone)

    def start_group(copies, into, ss, rs):
        for c in copies:
            c.start()
        sent.append(copy(into, into, ss, rs, sib).wait_send)

    def sent_in_all(ref, ss, rs):
        sent.append(copy(ref, ref, ss, rs, sib).wait_send)

    def take_group(into, ss, rs):
        copy(into, into, ss, rs, sib).wait_recv()

    def start_all(lo, hi, make, into, ss, rs):
        def go(i, _):
            make(i).start()
            return 0

        lax.fori_loop(lo, hi, go, 0)
        sent.append(copy(into, into, ss, rs, sib).wait_send)

    barrier = pltpu.get_barrier_semaphore()

    near = [(b, yh * 4 + lax.rem(z + d, 4)) for d in (1, 2, 3)]
    near += [(lax.rem(x + d, 4) * 4 + j, a) for d in (1, 2, 3)]
    near += [(x * 4 + lax.rem(j + d, 4), a) for d in (1, 2, 3)]
    near += [(x * 4 + lax.rem(j + d, 4), (1 - yh) * 4 + z) for d in range(4)]
    for peer in near:
        pl.semaphore_signal(barrier, 1, device_id=peer, device_id_type=MESH)
    pl.semaphore_wait(barrier, len(near))

    zm1, zp1, zp2 = lax.rem(z + 3, 4), lax.rem(z + 1, 4), lax.rem(z + 2, 4)
    own = (timg, simg)
    imgs = (it, is_)
    texts = (tt, ts)
    own_text = (ttext, stext)

    def half(h):
        return pl.ds(h * HALF, HALF)

    def img_send(m, d, h):
        return copy(
            own[m].at[half(h)], imgs[m].at[z, half(h)], zi_s.at[m], zi_r.at[m, d, h],
            znext(1 if d == 0 else 3),
        )

    def img_relay(m, d):
        slot = zm1 if d == 0 else zp1
        ref = imgs[m].at[slot, half(d)]
        return copy(ref, ref, zi_s.at[m], zi_r.at[m, 2, d], znext(1 if d == 0 else 3))

    def img_recv(m, d, h):
        slot = zm1 if d == 0 else zp1
        ref = imgs[m].at[slot, half(h)]
        copy(ref, ref, zi_s.at[m], zi_r.at[m, d, h], znext(1)).wait_recv()

    def img_recv_far(m, d):
        ref = imgs[m].at[zp2, half(d)]
        copy(ref, ref, zi_s.at[m], zi_r.at[m, 2, d], znext(1)).wait_recv()

    def img_start(m):
        img_send(m, 0, 0).start()
        img_send(m, 1, 1).start()

    def img_rest(m):
        img_send(m, 0, 1).start()
        img_send(m, 1, 0).start()

    def img_pass_on(m):
        img_recv(m, 0, 0)
        img_relay(m, 0).start()
        img_recv(m, 1, 1)
        img_relay(m, 1).start()
        sent_in_all(imgs[m].at[0:3], zi_s.at[m], zi_r.at[m, 2, 1])

    syl, sk = z // 2, z % 2
    is_source = j == z

    def tslab(m, blk, h):
        return texts[m].at[pl.ds(blk * ROWS + h * HALF, HALF)]

    def text_first(m):
        return (
            copy(own_text[m].at[pl.ds((1 - sk) * HALF, HALF)], tslab(m, x, 1 - sk),
                 t1_s.at[m, 0], t1_r.at[m], dev(x, syl * 2 + 1 - sk, yh, z)),
            copy(own_text[m].at[half(0)], tslab(m, x, 0),
                 t1_s.at[m, 1], t1_r.at[m], dev(x, (1 - syl) * 2, yh, z)),
            copy(own_text[m].at[half(1)], tslab(m, x, 1),
                 t1_s.at[m, 2], t1_r.at[m], dev(x, (1 - syl) * 2 + 1, 1 - yh, z)),
        )

    def text_own(m):
        return pltpu.make_async_copy(
            own_text[m].at[pl.ds(k * HALF, HALF)], tslab(m, x, k), own_s.at[2 + m]
        )

    def img_own(m):
        return pltpu.make_async_copy(own[m], imgs[m].at[z], own_s.at[m])

    def text_start(m):
        @pl.when(is_source)
        def _():
            for c in text_first(m):
                c.start()
            text_own(m).start()

        def gone():
            @pl.when(is_source)
            def _():
                for c in text_first(m):
                    c.wait_send()

        sent.append(gone)

    def text_x(m, d):
        return copy(tslab(m, x, k), tslab(m, x, k), t2_s.at[m, d - 1], t2_r.at[m, d - 1],
                    (lax.rem(x + d, 4) * 4 + j, a))

    def text_got(m, d):
        slab = tslab(m, lax.rem(x + 4 - d, 4), k)
        copy(slab, slab, t2_s.at[m, d - 1], t2_r.at[m, d - 1], sib).wait_recv()

    def tlanes(m, blk, i):
        width = texts[m].shape[1] // 2
        return texts[m].at[pl.ds(blk * ROWS + k * HALF, HALF), i * width : (i + 1) * width]

    def text_relay(m, i):
        ref = tlanes(m, lax.rem(x + 3 - 2 * i, 4), i)
        return copy(ref, ref, t4_s.at[m, i], t4_r.at[m, i], (lax.rem(x + 1 + 2 * i, 4) * 4 + j, a))

    def text_sib(m, d):
        blk = lax.rem(x + 4 - d, 4)
        return copy(tslab(m, blk, k), tslab(m, blk, k), t3_s.at[m, d], t3_r.at[m, d], sib)

    holds = yl == syl
    lacks = yl != syl

    def text_cross(d):
        slab = tslab(1, lax.rem(x + 4 - d, 4), k)
        to = dev(x, (1 - syl) * 2 + k, yh + k * (1 - 2 * yh), z)
        return copy(slab, slab, t5_s.at[d - 1], t5_r.at[d - 1], to)

    def crossed(d):
        @pl.when(lacks)
        def _():
            slab = tslab(1, lax.rem(x + 4 - d, 4), k)
            copy(slab, slab, t5_s.at[d - 1], t5_r.at[d - 1], sib).wait_recv()

    def text_spread(m, here):
        @pl.when(here & jnp.logical_not(is_source))
        def _():
            copy(tslab(m, x, k), tslab(m, x, k), t1_s.at[m, 0], t1_r.at[m], sib).wait_recv()

        @pl.when(here & is_source)
        def _():
            text_own(m).wait()

        for d in (1, 3):
            if m == 0 or here is holds:
                start_if(here, text_x(m, d))
        start_if(here, text_sib(m, 0))

    def text_pass_on(m):
        for d in (1, 3):
            if m:
                @pl.when(holds)
                def _():
                    text_got(m, d)

                start_if(holds, text_relay(m, d // 2))
                start_if(holds, text_cross(d))
                crossed(d)
            else:
                text_got(m, d)
                start(text_relay(m, d // 2))
            start(text_sib(m, d))

    def text_far(m):
        def arrived():
            for i in range(2):
                ref = tlanes(m, lax.rem(x + 2, 4), i)
                copy(ref, ref, t4_s.at[m, i], t4_r.at[m, i], sib).wait_recv()

        if m:
            pl.when(holds)(arrived)
            start_if(holds, text_cross(2))
            crossed(2)
        else:
            arrived()
        start(text_sib(m, 2))

    def text_wait(m):
        for d in range(4):
            blk = lax.rem(x + 4 - d, 4)
            copy(tslab(m, blk, 1 - k), tslab(m, blk, 1 - k), t3_s.at[m, d], t3_r.at[m, d],
                 sib).wait_recv()

    lane = lax.broadcasted_iota(jnp.int32, (ROWS, 128), 1)

    def fold(op, t):
        return functools.reduce(op, [t[:, i * 128 : (i + 1) * 128] for i in range(COLS // 128)])

    def scores(m, v, pr, qr, scale, far=False):
        t = dot(imgs[m][v], texts[m][...], NT) * scale
        cm = jnp.max(t, axis=0, keepdims=True)
        top = jnp.max(fold(jnp.maximum, t), axis=1, keepdims=True)
        q = jnp.exp(t - cm)
        qr[v] = q
        p = jnp.exp(t - top)
        pr[v] = p
        cs = jnp.sum(q, axis=0, keepdims=True)
        if far:
            cfar[0:1, :] = cm
            cfar[1:2, :] = cs
        else:
            colst[m, pl.ds(v, 1), :] = cm
            colst[m, pl.ds(v + 4, 1), :] = cs
        total = jnp.sum(fold(jnp.add, p), axis=1, keepdims=True)
        rowst[:ROWS, :] = jnp.where(
            lane == v, top, jnp.where(lane == v + 4, total, rowst[:ROWS, :])
        )

    def row_copy(m, d):
        return copy(rowsend.at[m], rowrecv.at[m, d - 1], row_s.at[m], row_r.at[m],
                    znext(d))

    def quad_copy(m, d):
        return copy(colst.at[m], quad_in.at[m, d - 1], quad_s.at[m], quad_r.at[m],
                    (x * 4 + lax.rem(j + d, 4), a))

    def col_copy(m, d):
        return copy(colq.at[m], colx_in.at[m, d - 1], col_s.at[m], col_r.at[m],
                    (lax.rem(x + d, 4) * 4 + j, a))

    def merged(mine, others):
        top = functools.reduce(jnp.maximum, [t[:4] for t in others], mine[:4])
        total = mine[4:] * jnp.exp(mine[:4] - top)
        for t in others:
            total = total + t[4:] * jnp.exp(t[:4] - top)
        return top, total

    def far_copy(d):
        return copy(cfar, cfar_in.at[d - 1], far_s.at[0], far_r.at[0],
                    (lax.rem(b + d, 16), a))

    def far_finish():
        take_group(cfar_in, far_s.at[0], far_r.at[0])

        def arrived(d, top):
            return jnp.maximum(top, cfar_in[d - 1, 0:1, :])

        mine = cfar[0:1, :]
        top = lax.fori_loop(1, 16, arrived, mine)

        def add(d, total):
            return total + cfar_in[d, 1:2, :] * jnp.exp(cfar_in[d, 0:1, :] - top)

        total = lax.fori_loop(0, 15, add, cfar[1:2, :] * jnp.exp(mine - top))
        colfac[0, pl.ds(zp2, 1), :] = jnp.exp(mine - top - jnp.log(total))

    def cols_start(m):
        start_group([quad_copy(m, d) for d in (1, 2, 3)], quad_in.at[m], quad_s.at[m], quad_r.at[m])

    def rows_start(m):
        rowsend[m] = jnp.transpose(rowst[...])[:8]
        start_group([row_copy(m, d) for d in (1, 3, 2)], rowrecv.at[m], row_s.at[m], row_r.at[m])

    def stats_middle(m):
        take_group(quad_in.at[m], quad_s.at[m], quad_r.at[m])
        top, total = merged(colst[m], [quad_in[m, d] for d in range(3)])
        colq[m, 0:4, :] = top
        colq[m, 4:8, :] = total
        start_group([col_copy(m, d) for d in (1, 3, 2)], colx_in.at[m], col_s.at[m], col_r.at[m])

    def stats_finish(m):
        take_group(rowrecv.at[m], row_s.at[m], row_r.at[m])
        mine = rowsend[m]
        top, total = merged(mine, [rowrecv[m, d] for d in range(3)])
        row_lse = top + jnp.log(total)
        rowtmp[0:4, :] = jnp.exp(mine[:4] - row_lse)
        rowfac[m] = jnp.transpose(rowtmp[...])
        take_group(colx_in.at[m], col_s.at[m], col_r.at[m])
        top, total = merged(colq[m], [colx_in[m, d] for d in range(3)])
        col_lse = top + jnp.log(total)
        colfac[m, 0:4, :] = jnp.exp(colst[m, 0:4, :] - col_lse)
        return row_lse, col_lse

    rowst[...] = jnp.ones_like(rowst)
    rowtmp[...] = jnp.zeros_like(rowtmp)
    colst[0] = jnp.ones_like(colst[0])
    img_start(1)
    img_rest(1)
    text_start(1)
    img_start(0)
    text_start(0)
    img_own(1).start()
    img_own(0).start()
    text_spread(1, holds)
    text_spread(1, lacks)
    text_spread(0, lacks)
    img_pass_on(1)
    img_rest(0)
    text_pass_on(1)
    text_spread(0, holds)
    text_far(1)
    text_wait(1)

    img_own(1).wait()
    scores(1, z, ps, qs, student_scale)
    img_recv(1, 0, 1)
    scores(1, zm1, ps, qs, student_scale)
    img_recv(1, 1, 0)
    scores(1, zp1, ps, qs, student_scale)
    img_pass_on(0)
    text_pass_on(0)
    img_recv_far(1, 0)
    img_recv_far(1, 1)
    scores(1, zp2, ps, qs, student_scale)
    cols_start(1)
    rows_start(1)

    partner = (b, (1 - yh) * 4 + z)
    total_img = (
        is_[0].astype(F32) + is_[1].astype(F32) + is_[2].astype(F32) + is_[3].astype(F32)
    )
    for g in range(4):
        isum[0, g] = total_img[:HALF, g * 128 : (g + 1) * 128]
        isum[1, g] = total_img[HALF:, g * 128 : (g + 1) * 128]
    iy = copy(isum.at[1 - yh, z], isum_in.at[z], iy_s.at[0], iy_r.at[0], partner)
    start(iy)
    text_far(0)
    text_wait(0)

    img_own(0).wait()
    scores(0, z, pt, qt, teacher_scale)
    stats_middle(1)
    img_recv(0, 0, 1)
    scores(0, zm1, pt, qt, teacher_scale)
    img_recv(0, 1, 0)
    scores(0, zp1, pt, qt, teacher_scale)
    cols_start(0)
    stats_middle(0)
    img_recv_far(0, 0)
    img_recv_far(0, 1)
    scores(0, zp2, pt, qt, teacher_scale, far=True)
    start_all(1, 16, far_copy, cfar_in, far_s.at[0], far_r.at[0])
    rows_start(0)

    def iz_copy(d):
        slot = isum_in.at[z]
        return copy(slot, slot, iz_s.at[d - 1], iz_r.at[d - 1], znext(d))

    def iz_wait(d):
        slot = isum_in.at[lax.rem(z + 4 - d, 4)]
        copy(slot, slot, iz_s.at[d - 1], iz_r.at[d - 1], partner).wait_recv()

    iy.wait_recv()
    for d in (1, 3, 2):
        start(iz_copy(d))

    row_lse, col_lse = stats_finish(1)
    rl = lax.broadcasted_iota(jnp.int32, (4, 384), 0)
    cl = lax.broadcasted_iota(jnp.int32, (4, 384), 1)
    row_part = jnp.sum(jnp.where((rl == z) & (cl < ROWS), row_lse, 0.0), axis=0, keepdims=True)
    lse_part = (
        jnp.sum(row_part, axis=1, keepdims=True)
        + jnp.sum(jnp.sum(col_lse, axis=0, keepdims=True), axis=1, keepdims=True) * (1.0 / 16.0)
    )

    for d in (2, 1, 3, 0):
        v = lax.rem(z + d, 4)
        factor = jnp.sum(jnp.where(lane == v, rowfac[1, :ROWS, :], 0.0), axis=1, keepdims=True)
        w[v] = (ps[v] * factor + qs[v] * colfac[1, pl.ds(v, 1), :]).astype(BF16)
        gsend[d] = dot(w[v], ts[...], NN)

    def g_far(h):
        return copy(gsend.at[2, half(h)], gfar_in.at[h], g_s.at[0], g_r.at[2, h],
                    znext(1 if h == 0 else 3))

    def g_copy(i, h):
        d = 1 + 2 * i
        return copy(gsend.at[d, half(h)], grecv.at[i, half(h)], g_s.at[0], g_r.at[i, h],
                    znext(d))

    g_far(0).start()
    g_far(1).start()
    g_copy(0, 1).start()
    g_copy(1, 0).start()


    stats_finish(0)
    far_finish()


    def tgt_copy(n):
        return copy(tgt.at[n], tgt_in.at[n], tgt_s.at[n], tgt_r.at[n], partner)

    def own_targets(h, n):
        rows = pl.ds(pl.multiple_of(h * HALF + n * 48, 16), 48)
        acc = None
        for v in range(4):
            term = pt[v, rows] * rowfac[0, rows, v : v + 1] + qt[v, rows] * colfac[0, v : v + 1, :]
            acc = term if acc is None else acc + term
        return acc

    for n in range(NCH):
        tgt[n] = own_targets(1 - yh, n)
        start(tgt_copy(n))
    acc = dot(w[0], is_[0], TN)
    for v in range(1, 4):
        acc = acc + dot(w[v], is_[v], TN)
    gtp[...] = acc
    for n in range(NCH):
        tgt_mine[n] = own_targets(yh, n)

    for d in (1, 3, 2):
        iz_wait(d)
    for g in range(4):
        isum8[g] = isum_in[g] + isum[yh, g]
    for g in range(4):
        t = isum8[g]
        hi[:, g * 128 : (g + 1) * 128] = t.astype(BF16)
        lo[:, g * 128 : (g + 1) * 128] = (t - t.astype(BF16).astype(F32)).astype(BF16)
    for i in range(2):
        g_far(i).wait_recv()
        rows = slice(i * HALF, (i + 1) * HALF)
        gsend[1 + 2 * i, rows] = gsend[1 + 2 * i, rows] + gfar_in[i]
        g_copy(i, i).start()
    sent_in_all(gsend.at[1:4], g_s.at[0], g_r.at[0, 0])

    for n in range(NCH):
        tgt_copy(n).wait_recv()
        tw[n * 48 : (n + 1) * 48] = ((tgt_mine[n] + tgt_in[n]) * 0.125).astype(BF16)
    res = gtp[...] - dot(tw[...], hi[...], TN) - dot(tw[...], lo[...], TN)
    for s in range(8):
        row = s * HALF
        for g in range(4):
            gtc[s % 2, s // 2, g] = res[row : row + HALF, g * 128 : (g + 1) * 128]
    def gc_copy(i):
        rows = slice(i * 72, (i + 1) * 72)
        return copy(gtc.at[1 - k, :, :, rows, :], gt_sib.at[:, :, rows, :], gc_s.at[i],
                    gc_r.at[i], sib)

    start(gc_copy(0))
    start(gc_copy(1))

    target_text = dot(tw[...], ts[...], NN)
    for g in range(4):
        tt_part[g] = target_text[:, g * 128 : (g + 1) * 128]

    def tz_copy(d):
        return copy(tt_part.at[lax.rem(z + d, 4)], tt_in.at[d - 1], tz_s.at[0],
                    tz_r.at[0], znext(d))

    start_group([tz_copy(d) for d in (2, 1, 3)], tt_in, tz_s.at[0], tz_r.at[0])

    target_loss = isum8[0] * tt_part[0]
    for g in range(1, 4):
        target_loss = target_loss + isum8[g] * tt_part[g]
    target_loss = jnp.sum(jnp.sum(target_loss, axis=0, keepdims=True), axis=1, keepdims=True)
    part = lse_part - target_loss * student_scale
    loss_src[...] = jnp.broadcast_to(part, (8, 128))

    def lb_copy(d):
        return copy(loss_src, loss_b.at[d - 1], lb_s.at[0], lb_r.at[0],
                    (lax.rem(b + d, 16), a))

    start_all(1, 16, lb_copy, loss_b, lb_s.at[0], lb_r.at[0])

    y = yh * 2 + yl
    pieces = gtc.at[k]

    def ydev(d):
        yd = lax.rem(y + d, 4)
        return dev(x, (yd % 2) * 2 + k, yd // 2, z)

    def xdev(d):
        return dev(lax.rem(x + d, 4), j, yh, z)

    def ra_copy(d):
        return copy(pieces.at[lax.rem(x + d, 4), :, 0:72, :], ra_in.at[d - 1],
                    rs_s.at[0], rs_r.at[0], xdev(d))

    def rb_copy(d):
        return copy(pieces.at[:, lax.rem(y + d, 4), 72:144, :], rb_in.at[d - 1],
                    rs_s.at[1], rs_r.at[1], ydev(d))

    def ra2_copy(d):
        return copy(ra_sum.at[lax.rem(y + d, 4)], ra2_in.at[d - 1],
                    rs_s.at[2], rs_r.at[2], ydev(d))

    def rb2_copy(d):
        return copy(rb_sum.at[lax.rem(x + d, 4)], rb2_in.at[d - 1],
                    rs_s.at[3], rs_r.at[3], xdev(d))

    for i in range(2):
        gc_copy(i).wait_recv()
        rows = slice(i * 72, (i + 1) * 72)
        for blk in range(4):
            for g in range(4):
                gtc[k, blk, g, rows, :] = gtc[k, blk, g, rows, :] + gt_sib[blk, g, rows, :]
        if i == 0:
            start_group([ra_copy(d) for d in (1, 3, 2)], ra_in, rs_s.at[0], rs_r.at[0])
        else:
            start_group([rb_copy(d) for d in (1, 3)], rb_in, rs_s.at[1], rs_r.at[1])

    total = tt_part[z]
    take_group(tt_in, tz_s.at[0], tz_r.at[0])
    for d in (1, 3, 2):
        total = total + tt_in[d - 1]
    tt_src[...] = total

    a_in = (1 - yh) * 4 + z
    ty = copy(tt_src, tt_all.at[a], ta_s.at[0], ta_r.at[a], partner)
    ty.start()
    rb_copy(2).start()

    def ta_copy(d):
        return copy(tt_src, tt_all.at[a], ta_s.at[0], ta_r.at[a], znext(d))

    def tb_copy(d):
        return copy(tt_all.at[a_in], tt_all.at[a_in], ta_s.at[0], ta_r.at[a_in], znext(d))

    def t_wait(slot):
        copy(tt_src, tt_all.at[slot], ta_s.at[0], ta_r.at[slot], partner).wait_recv()

    for d in (1, 3, 2):
        ta_copy(d).start()
    tt_all[a] = total

    take_group(loss_b, lb_s.at[0], lb_r.at[0])

    def lb_wait(d, acc):
        return acc + loss_b[d - 1]

    loss_src2[...] = lax.fori_loop(1, 16, lb_wait, loss_src[...])

    def la_copy(d):
        return copy(loss_src2, loss_a.at[d - 1], la_s.at[0], la_r.at[0],
                    (b, lax.rem(a + d, 8)))

    start_all(1, 8, la_copy, loss_a, la_s.at[0], la_r.at[0])

    ra_sum[...] = gtc[k, x, :, 0:72, :]
    rb_sum[...] = gtc[k, :, y, 72:144, :]
    take_group(ra_in, rs_s.at[0], rs_r.at[0])
    for d in (1, 3, 2):
        ra_sum[...] = ra_sum[...] + ra_in[d - 1]
    start_group([ra2_copy(d) for d in (1, 3, 2)], ra2_in, rs_s.at[2], rs_r.at[2])
    take_group(rb_in, rs_s.at[1], rs_r.at[1])
    for d in (1, 3, 2):
        rb_sum[...] = rb_sum[...] + rb_in[d - 1]
    start_group([rb2_copy(d) for d in (1, 3, 2)], rb2_in, rs_s.at[3], rs_r.at[3])
    t_wait(a_in)
    for d in (1, 3, 2):
        tb_copy(d).start()
    sent_in_all(tt_all.at[0:7], ta_s.at[0], ta_r.at[0])
    def fz_copy(c, i, d):
        ref = fb_src.at[c, i * 72 : (i + 1) * 72]
        return copy(ref, ref, fz_s.at[0], fz_r.at[i, d - 1], znext(d))

    first = ra_sum[y]
    take_group(ra2_in, rs_s.at[2], rs_r.at[2])
    for d in (1, 3, 2):
        first = first + ra2_in[d - 1]
    fb_src[z, 0:72, :] = first
    for d in (1, 3, 2):
        fz_copy(z, 0, d).start()
    last = rb_sum[x]
    take_group(rb2_in, rs_s.at[3], rs_r.at[3])
    for d in (1, 3, 2):
        last = last + rb2_in[d - 1]
    fb_src[z, 72:144, :] = last
    for d in (1, 3, 2):
        fz_copy(z, 1, d).start()
    sent_in_all(fb_src.at[0:3], fz_s.at[0], fz_r.at[0, 0])

    def fb_copy(c, h):
        return copy(fb_src.at[c], fb_buf.at[j * 2 + yh], fb_s.at[c, h], fb_r.at[j * 2 + yh],
                    dev(x, c, h, z))

    def is_self(c, h):
        return (j == c) & (yh == h)

    def fb_send(c):
        for h in range(2):
            @pl.when(jnp.logical_not(is_self(c, h)))
            def _():
                fb_copy(c, h).start()

    def fb_gone():
        for c in range(4):
            for h in range(2):
                @pl.when(jnp.logical_not(is_self(c, h)))
                def _():
                    fb_copy(c, h).wait_send()

    sent.append(fb_gone)
    fb_send(z)
    for d in (1, 3, 2):
        c = lax.rem(z + 4 - d, 4)
        fz_copy(c, 0, d).wait_recv()
        fz_copy(c, 1, d).wait_recv()
        fb_send(c)
    fb_buf[j * 2 + yh] = fb_src[j]

    acc = gsend[0]
    for i in range(2):
        g_copy(i, 0).wait_recv()
        g_copy(i, 1).wait_recv()
        acc = acc + grecv[i]

    for d in (1, 3, 2):
        zd = lax.rem(z + d, 4)
        t_wait(yh * 4 + zd)
        t_wait((1 - yh) * 4 + zd)
    for h in range(2):
        rows = slice(h * HALF, (h + 1) * HALF)
        for g in range(4):
            lanes = slice(g * 128, (g + 1) * 128)
            grads_out[0, rows, lanes] = acc[rows, lanes] - tt_all[h * 4 + g]

    take_group(loss_a, la_s.at[0], la_r.at[0])

    def la_wait(d, acc):
        return acc + loss_a[d - 1]

    whole = lax.fori_loop(1, 8, la_wait, loss_src2[...])
    loss_out[0, 0] = jnp.sum(whole[0:1, 0:1]) * (1.0 / (2.0 * 8 * 4608))

    def fb_wait(s, _):
        @pl.when(s != j * 2 + yh)
        def _():
            copy(fb_src.at[0], fb_buf.at[s], fb_s.at[0, 0], fb_r.at[s], partner).wait_recv()

        return 0

    lax.fori_loop(0, 8, fb_wait, 0)
    for s in range(8):
        syl_, sk_, syh_ = s // 4, (s // 2) % 2, s % 2
        g = syh_ * 2 + syl_
        grads_out[1, sk_ * HALF : (sk_ + 1) * HALF, g * 128 : (g + 1) * 128] = fb_buf[s]

    for gone in sent:
        gone()


def per_device(student_image, student_text, teacher_image, teacher_text):
    vm = pl.BlockSpec(memory_space=pltpu.VMEM)
    dma = pltpu.SemaphoreType.DMA
    V = pltpu.VMEM
    sw, twd = student_image.shape[2], teacher_image.shape[2]
    loss, grads = pl.pallas_call(
        kernel,
        name="distill",
        out_shape=(
            jax.ShapeDtypeStruct((1, 1), F32),
            pltpu.VMEM((2, ROWS, sw), F32),
        ),
        in_specs=[pl.BlockSpec(memory_space=pl.ANY)] * 4,
        out_specs=(pl.BlockSpec(memory_space=pltpu.SMEM), vm),
        scratch_shapes=[
            V((4, ROWS, twd), BF16), V((4, ROWS, sw), BF16),
            V((4 * ROWS, twd), BF16), V((4 * ROWS, sw), BF16),
            V((4, ROWS, COLS), F32), V((4, ROWS, COLS), F32),
            V((4, ROWS, COLS), F32), V((4, ROWS, COLS), F32),
            V((4, ROWS, COLS), BF16),
            V((NCH, 48, COLS), F32), V((NCH, 48, COLS), F32), V((NCH, 48, COLS), F32),
            V((HALF, COLS), BF16),
            V((2, 4, HALF, 128), F32), V((4, HALF, 128), F32), V((4, HALF, 128), F32),
            V((HALF, sw), BF16), V((HALF, sw), BF16),
            V((4, HALF, 128), F32), V((3, HALF, 128), F32), V((HALF, 128), F32),
            V((8, HALF, 128), F32),
            V((4, ROWS, sw), F32), V((2, ROWS, sw), F32), V((2, HALF, sw), F32),
            V((COLS, sw), F32), V((4, 4, HALF, 128), F32),
            V((3, 4, 72, 128), F32), V((3, 4, 72, 128), F32), V((4, 72, 128), F32),
            V((4, 72, 128), F32), V((3, 72, 128), F32), V((3, 72, 128), F32),
            V((4, HALF, 128), F32), V((8, HALF, 128), F32),
            V((2, 4, 4, HALF, 128), F32),
            V((384, 128), F32), V((2, 8, 384), F32), V((2, 3, 8, 384), F32),
            V((2, 384, 128), F32), V((128, 384), F32),
            V((2, 8, COLS), F32), V((2, 3, 8, COLS), F32), V((2, 8, COLS), F32),
            V((2, 3, 8, COLS), F32), V((2, 8, COLS), F32),
            V((2, COLS), F32), V((15, 2, COLS), F32),
            V((8, 128), F32), V((15, 8, 128), F32), V((8, 128), F32), V((7, 8, 128), F32),
            dma((4,)), dma((2,)), dma((2, 3, 2)),
            dma((2, 3)), dma((2,)), dma((2, 3)), dma((2, 3)), dma((2, 4)), dma((2, 4)),
            dma((2, 2)), dma((2, 2)), dma((3,)), dma((3,)),
            dma((1,)), dma((1,)), dma((3,)), dma((3,)), dma((1,)), dma((1,)), dma((1,)), dma((8,)),
            dma((1,)), dma((1,)), dma((2,)), dma((2,)), dma((2,)), dma((2,)), dma((2,)), dma((2,)),
            dma((3,)), dma((3,)), dma((1,)), dma((3, 2)), dma((2,)), dma((2,)),
            dma((4,)), dma((4,)), dma((1,)), dma((2, 3)), dma((4, 2)), dma((8,)),
            dma((1,)), dma((1,)), dma((1,)), dma((1,)),
        ],
        compiler_params=pltpu.CompilerParams(
            collective_id=0, has_side_effects=True, vmem_limit_bytes=58 * 1024 * 1024
        ),
        cost_estimate=pl.CostEstimate(
            flops=8 * 10**9, bytes_accessed=4 * 2**20, transcendentals=6 * 10**6
        ),
    )(student_image[0], student_text, teacher_image[0], teacher_text)
    scale = 3.0 / math.sqrt(sw)
    return loss.reshape(()), (grads[0] * scale)[None], grads[1] * scale


def solution(mesh):
    return jax.shard_map(
        per_device,
        mesh=mesh,
        in_specs=(
            P("aug", "batch", None),
            P("batch", None),
            P("aug", "batch", None),
            P("batch", None),
        ),
        out_specs=(P(), P("aug", "batch", None), P("batch", None)),
        check_vma=False,
    )
```

```python
import functools
import math

import jax
import jax.numpy as jnp
from jax import lax
from jax.experimental import pallas as pl
from jax.experimental.pallas import tpu as pltpu
from jax.sharding import PartitionSpec as P

MESH = pl.DeviceIdType.MESH
F32 = jnp.float32
BF16 = jnp.bfloat16
ROWS = 288
HALF = ROWS // 2
COLS = 4 * ROWS
NCH = 3
NT = (((1,), (1,)), ((), ()))
NN = (((1,), (0,)), ((), ()))
TN = (((0,), (0,)), ((), ()))


def dot(a, b, dims):
    return lax.dot_general(a, b, dims, preferred_element_type=F32)


def kernel(
    simg, stext, timg, ttext,
    loss_out, grads_out,
    it, is_, tt, ts, pt, qt, ps, qs, w, tgt, tgt_mine, tgt_in, tw,
    isum, isum_in, isum8, hi, lo, tt_part, tt_in, tt_src, tt_all,
    gsend, grecv, gfar_in, gtp, gt_sib, ra_in, rb_in, ra_sum, rb_sum, ra2_in, rb2_in, fb_src, fb_buf, gtc,
    rowst, rowsend, rowrecv, rowfac, rowtmp, colst, quad_in, colq, colx_in, colfac, cfar, cfar_in,
    loss_src, loss_b, loss_src2, loss_a,
    own_s, zi_s, zi_r, t1_s, t1_r, t2_s, t2_r, t3_s, t3_r, t4_s, t4_r, t5_s, t5_r,
    iy_s, iy_r, iz_s, iz_r, tz_s, tz_r, ta_s, ta_r,
    far_s, far_r, quad_s, quad_r, row_s, row_r, col_s, col_r, tgt_s, tgt_r, g_s, g_r, gc_s, gc_r,
    rs_s, rs_r, fz_s, fz_r, fb_s, fb_r, lb_s, lb_r, la_s, la_r,
):
    b = lax.axis_index("batch")
    a = lax.axis_index("aug")
    x, j = b // 4, b % 4
    yl, k = j // 2, j % 2
    yh, z = a // 4, a % 4
    sib = (b + 1 - 2 * k, a)
    teacher_scale = 3.0 / math.sqrt(timg.shape[1])
    student_scale = 3.0 / math.sqrt(simg.shape[1])

    def dev(x_, j_, yh_, z_):
        return (x_ * 4 + j_, yh_ * 4 + z_)

    def znext(d):
        return (b, yh * 4 + lax.rem(z + d, 4))

    def copy(src, dst, ss, rs, to):
        return pltpu.make_async_remote_copy(
            src_ref=src, dst_ref=dst, send_sem=ss, recv_sem=rs, device_id=to, device_id_type=MESH
        )

    sent = []

    def start(c):
        c.start()
        sent.append(c.wait_send)

    def start_if(cond, c):
        @pl.when(cond)
        def _():
            c.start()

        def gone():
            @pl.when(cond)
            def _():
                c.wait_send()

        sent.append(gone)

    def start_group(copies, into, ss, rs):
        for c in copies:
            c.start()
        sent.append(copy(into, into, ss, rs, sib).wait_send)

    def sent_in_all(ref, ss, rs):
        sent.append(copy(ref, ref, ss, rs, sib).wait_send)

    def take_group(into, ss, rs):
        copy(into, into, ss, rs, sib).wait_recv()

    def start_all(lo, hi, make, into, ss, rs):
        def go(i, _):
            make(i).start()
            return 0

        lax.fori_loop(lo, hi, go, 0)
        sent.append(copy(into, into, ss, rs, sib).wait_send)

    barrier = pltpu.get_barrier_semaphore()

    near = [(b, yh * 4 + lax.rem(z + d, 4)) for d in (1, 2, 3)]
    near += [(lax.rem(x + d, 4) * 4 + j, a) for d in (1, 2, 3)]
    near += [(x * 4 + lax.rem(j + d, 4), a) for d in (1, 2, 3)]
    near += [(x * 4 + lax.rem(j + d, 4), (1 - yh) * 4 + z) for d in range(4)]
    for peer in near:
        pl.semaphore_signal(barrier, 1, device_id=peer, device_id_type=MESH)
    pl.semaphore_wait(barrier, len(near))

    zm1, zp1, zp2 = lax.rem(z + 3, 4), lax.rem(z + 1, 4), lax.rem(z + 2, 4)
    own = (timg, simg)
    imgs = (it, is_)
    texts = (tt, ts)
    own_text = (ttext, stext)

    def half(h):
        return pl.ds(h * HALF, HALF)

    def img_send(m, d, h):
        return copy(
            own[m].at[half(h)], imgs[m].at[z, half(h)], zi_s.at[m], zi_r.at[m, d, h],
            znext(1 if d == 0 else 3),
        )

    def img_relay(m, d):
        slot = zm1 if d == 0 else zp1
        ref = imgs[m].at[slot, half(d)]
        return copy(ref, ref, zi_s.at[m], zi_r.at[m, 2, d], znext(1 if d == 0 else 3))

    def img_recv(m, d, h):
        slot = zm1 if d == 0 else zp1
        ref = imgs[m].at[slot, half(h)]
        copy(ref, ref, zi_s.at[m], zi_r.at[m, d, h], znext(1)).wait_recv()

    def img_recv_far(m, d):
        ref = imgs[m].at[zp2, half(d)]
        copy(ref, ref, zi_s.at[m], zi_r.at[m, 2, d], znext(1)).wait_recv()

    def img_start(m):
        img_send(m, 0, 0).start()
        img_send(m, 1, 1).start()

    def img_rest(m):
        img_send(m, 0, 1).start()
        img_send(m, 1, 0).start()

    def img_pass_on(m):
        img_recv(m, 0, 0)
        img_relay(m, 0).start()
        img_recv(m, 1, 1)
        img_relay(m, 1).start()
        sent_in_all(imgs[m].at[0:3], zi_s.at[m], zi_r.at[m, 2, 1])

    syl, sk = z // 2, z % 2
    is_source = j == z

    def tslab(m, blk, h):
        return texts[m].at[pl.ds(blk * ROWS + h * HALF, HALF)]

    def text_first(m):
        return (
            copy(own_text[m].at[pl.ds((1 - sk) * HALF, HALF)], tslab(m, x, 1 - sk),
                 t1_s.at[m, 0], t1_r.at[m], dev(x, syl * 2 + 1 - sk, yh, z)),
            copy(own_text[m].at[half(0)], tslab(m, x, 0),
                 t1_s.at[m, 1], t1_r.at[m], dev(x, (1 - syl) * 2, yh, z)),
            copy(own_text[m].at[half(1)], tslab(m, x, 1),
                 t1_s.at[m, 2], t1_r.at[m], dev(x, (1 - syl) * 2 + 1, 1 - yh, z)),
        )

    def text_own(m):
        return pltpu.make_async_copy(
            own_text[m].at[pl.ds(k * HALF, HALF)], tslab(m, x, k), own_s.at[2 + m]
        )

    def img_own(m):
        return pltpu.make_async_copy(own[m], imgs[m].at[z], own_s.at[m])

    def text_start(m):
        @pl.when(is_source)
        def _():
            for c in text_first(m):
                c.start()
            text_own(m).start()

        def gone():
            @pl.when(is_source)
            def _():
                for c in text_first(m):
                    c.wait_send()

        sent.append(gone)

    def text_x(m, d):
        return copy(tslab(m, x, k), tslab(m, x, k), t2_s.at[m, d - 1], t2_r.at[m, d - 1],
                    (lax.rem(x + d, 4) * 4 + j, a))

    def text_got(m, d):
        slab = tslab(m, lax.rem(x + 4 - d, 4), k)
        copy(slab, slab, t2_s.at[m, d - 1], t2_r.at[m, d - 1], sib).wait_recv()

    def tlanes(m, blk, i):
        width = texts[m].shape[1] // 2
        return texts[m].at[pl.ds(blk * ROWS + k * HALF, HALF), i * width : (i + 1) * width]

    def text_relay(m, i):
        ref = tlanes(m, lax.rem(x + 3 - 2 * i, 4), i)
        return copy(ref, ref, t4_s.at[m, i], t4_r.at[m, i], (lax.rem(x + 1 + 2 * i, 4) * 4 + j, a))

    def text_sib(m, d):
        blk = lax.rem(x + 4 - d, 4)
        return copy(tslab(m, blk, k), tslab(m, blk, k), t3_s.at[m], t3_r.at[m, d], sib)

    holds = yl == syl
    lacks = yl != syl

    def text_cross(d):
        slab = tslab(1, lax.rem(x + 4 - d, 4), k)
        to = dev(x, (1 - syl) * 2 + k, yh + k * (1 - 2 * yh), z)
        return copy(slab, slab, t5_s.at[d - 1], t5_r.at[d - 1], to)

    def crossed(d):
        @pl.when(lacks)
        def _():
            slab = tslab(1, lax.rem(x + 4 - d, 4), k)
            copy(slab, slab, t5_s.at[d - 1], t5_r.at[d - 1], sib).wait_recv()

    def text_spread(m, here):
        @pl.when(here & jnp.logical_not(is_source))
        def _():
            copy(tslab(m, x, k), tslab(m, x, k), t1_s.at[m, 0], t1_r.at[m], sib).wait_recv()

        @pl.when(here & is_source)
        def _():
            text_own(m).wait()

        for d in (1, 3):
            if m == 0 or here is holds:
                start_if(here, text_x(m, d))
        @pl.when(here)
        def _():
            text_sib(m, 0).start()

    def text_pass_on(m):
        for d in (1, 3):
            if m:
                @pl.when(holds)
                def _():
                    text_got(m, d)

                start_if(holds, text_relay(m, d // 2))
                start_if(holds, text_cross(d))
                crossed(d)
            else:
                text_got(m, d)
                start(text_relay(m, d // 2))
            text_sib(m, d).start()

    def text_far(m):
        def arrived():
            for i in range(2):
                ref = tlanes(m, lax.rem(x + 2, 4), i)
                copy(ref, ref, t4_s.at[m, i], t4_r.at[m, i], sib).wait_recv()

        if m:
            pl.when(holds)(arrived)
            start_if(holds, text_cross(2))
            crossed(2)
        else:
            arrived()
        text_sib(m, 2).start()
        sent_in_all(texts[m].at[0 : 2 * ROWS], t3_s.at[m], t3_r.at[m, 0])

    def text_wait(m):
        for d in range(4):
            blk = lax.rem(x + 4 - d, 4)
            copy(tslab(m, blk, 1 - k), tslab(m, blk, 1 - k), t3_s.at[m], t3_r.at[m, d],
                 sib).wait_recv()

    lane = lax.broadcasted_iota(jnp.int32, (ROWS, 128), 1)

    def fold(op, t):
        return functools.reduce(op, [t[:, i * 128 : (i + 1) * 128] for i in range(COLS // 128)])

    def scores(m, v, pr, qr, scale, far=False):
        t = dot(imgs[m][v], texts[m][...], NT) * scale
        cm = jnp.max(t, axis=0, keepdims=True)
        top = jnp.max(fold(jnp.maximum, t), axis=1, keepdims=True)
        q = jnp.exp(t - cm)
        qr[v] = q
        p = jnp.exp(t - top)
        pr[v] = p
        cs = jnp.sum(q, axis=0, keepdims=True)
        if far:
            cfar[0:1, :] = cm
            cfar[1:2, :] = cs
        else:
            colst[m, pl.ds(v, 1), :] = cm
            colst[m, pl.ds(v + 4, 1), :] = cs
        total = jnp.sum(fold(jnp.add, p), axis=1, keepdims=True)
        rowst[:ROWS, :] = jnp.where(
            lane == v, top, jnp.where(lane == v + 4, total, rowst[:ROWS, :])
        )

    def row_copy(m, d):
        return copy(rowsend.at[m], rowrecv.at[m, d - 1], row_s.at[m], row_r.at[m],
                    znext(d))

    def quad_copy(m, d):
        return copy(colst.at[m], quad_in.at[m, d - 1], quad_s.at[m], quad_r.at[m],
                    (x * 4 + lax.rem(j + d, 4), a))

    def col_copy(m, d):
        return copy(colq.at[m], colx_in.at[m, d - 1], col_s.at[m], col_r.at[m],
                    (lax.rem(x + d, 4) * 4 + j, a))

    def merged(mine, others):
        top = functools.reduce(jnp.maximum, [t[:4] for t in others], mine[:4])
        total = mine[4:] * jnp.exp(mine[:4] - top)
        for t in others:
            total = total + t[4:] * jnp.exp(t[:4] - top)
        return top, total

    def far_copy(d):
        return copy(cfar, cfar_in.at[d - 1], far_s.at[0], far_r.at[0],
                    (lax.rem(b + d, 16), a))

    def far_finish():
        take_group(cfar_in, far_s.at[0], far_r.at[0])

        def arrived(d, top):
            return jnp.maximum(top, cfar_in[d - 1, 0:1, :])

        mine = cfar[0:1, :]
        top = lax.fori_loop(1, 16, arrived, mine)

        def add(d, total):
            return total + cfar_in[d, 1:2, :] * jnp.exp(cfar_in[d, 0:1, :] - top)

        total = lax.fori_loop(0, 15, add, cfar[1:2, :] * jnp.exp(mine - top))
        colfac[0, pl.ds(zp2, 1), :] = jnp.exp(mine - top - jnp.log(total))

    def cols_start(m):
        start_group([quad_copy(m, d) for d in (1, 2, 3)], quad_in.at[m], quad_s.at[m], quad_r.at[m])

    def rows_start(m):
        rowsend[m] = jnp.transpose(rowst[...])[:8]
        start_group([row_copy(m, d) for d in (1, 3, 2)], rowrecv.at[m], row_s.at[m], row_r.at[m])

    def stats_middle(m):
        take_group(quad_in.at[m], quad_s.at[m], quad_r.at[m])
        top, total = merged(colst[m], [quad_in[m, d] for d in range(3)])
        colq[m, 0:4, :] = top
        colq[m, 4:8, :] = total
        start_group([col_copy(m, d) for d in (1, 3, 2)], colx_in.at[m], col_s.at[m], col_r.at[m])

    def stats_finish(m):
        take_group(rowrecv.at[m], row_s.at[m], row_r.at[m])
        mine = rowsend[m]
        top, total = merged(mine, [rowrecv[m, d] for d in range(3)])
        row_lse = top + jnp.log(total)
        rowtmp[0:4, :] = jnp.exp(mine[:4] - row_lse)
        rowfac[m] = jnp.transpose(rowtmp[...])
        take_group(colx_in.at[m], col_s.at[m], col_r.at[m])
        top, total = merged(colq[m], [colx_in[m, d] for d in range(3)])
        col_lse = top + jnp.log(total)
        colfac[m, 0:4, :] = jnp.exp(colst[m, 0:4, :] - col_lse)
        return row_lse, col_lse

    rowst[...] = jnp.ones_like(rowst)
    rowtmp[...] = jnp.zeros_like(rowtmp)
    colst[0] = jnp.ones_like(colst[0])
    img_start(1)
    img_rest(1)
    text_start(1)
    img_start(0)
    text_start(0)
    img_own(1).start()
    img_own(0).start()
    text_spread(1, holds)
    text_spread(1, lacks)
    text_spread(0, lacks)
    img_pass_on(1)
    img_rest(0)
    text_pass_on(1)
    text_spread(0, holds)
    text_far(1)
    text_wait(1)

    img_own(1).wait()
    scores(1, z, ps, qs, student_scale)
    img_recv(1, 0, 1)
    scores(1, zm1, ps, qs, student_scale)
    img_recv(1, 1, 0)
    scores(1, zp1, ps, qs, student_scale)
    img_pass_on(0)
    text_pass_on(0)
    img_recv_far(1, 0)
    img_recv_far(1, 1)
    scores(1, zp2, ps, qs, student_scale)
    cols_start(1)
    rows_start(1)

    partner = (b, (1 - yh) * 4 + z)
    total_img = (
        is_[0].astype(F32) + is_[1].astype(F32) + is_[2].astype(F32) + is_[3].astype(F32)
    )
    for g in range(4):
        isum[0, g] = total_img[:HALF, g * 128 : (g + 1) * 128]
        isum[1, g] = total_img[HALF:, g * 128 : (g + 1) * 128]
    iy = copy(isum.at[1 - yh, z], isum_in.at[z], iy_s.at[0], iy_r.at[0], partner)
    start(iy)
    text_far(0)
    text_wait(0)

    img_own(0).wait()
    scores(0, z, pt, qt, teacher_scale)
    stats_middle(1)
    img_recv(0, 0, 1)
    scores(0, zm1, pt, qt, teacher_scale)
    img_recv(0, 1, 0)
    scores(0, zp1, pt, qt, teacher_scale)
    cols_start(0)
    stats_middle(0)
    img_recv_far(0, 0)
    img_recv_far(0, 1)
    scores(0, zp2, pt, qt, teacher_scale, far=True)
    rows_start(0)
    start_all(1, 16, far_copy, cfar_in, far_s.at[0], far_r.at[0])

    def iz_copy(d):
        slot = isum_in.at[z]
        return copy(slot, slot, iz_s.at[d - 1], iz_r.at[d - 1], znext(d))

    def iz_wait(d):
        slot = isum_in.at[lax.rem(z + 4 - d, 4)]
        copy(slot, slot, iz_s.at[d - 1], iz_r.at[d - 1], partner).wait_recv()

    iy.wait_recv()
    for d in (1, 3, 2):
        start(iz_copy(d))

    row_lse, col_lse = stats_finish(1)
    rl = lax.broadcasted_iota(jnp.int32, (4, 384), 0)
    cl = lax.broadcasted_iota(jnp.int32, (4, 384), 1)
    row_part = jnp.sum(jnp.where((rl == z) & (cl < ROWS), row_lse, 0.0), axis=0, keepdims=True)
    lse_part = (
        jnp.sum(row_part, axis=1, keepdims=True)
        + jnp.sum(jnp.sum(col_lse, axis=0, keepdims=True), axis=1, keepdims=True) * (1.0 / 16.0)
    )

    for d in (2, 1, 3, 0):
        v = lax.rem(z + d, 4)
        factor = jnp.sum(jnp.where(lane == v, rowfac[1, :ROWS, :], 0.0), axis=1, keepdims=True)
        w[v] = (ps[v] * factor + qs[v] * colfac[1, pl.ds(v, 1), :]).astype(BF16)
        gsend[d] = dot(w[v], ts[...], NN)

    def g_far(h):
        return copy(gsend.at[2, half(h)], gfar_in.at[h], g_s.at[0], g_r.at[2, h],
                    znext(1 if h == 0 else 3))

    def g_copy(i, h):
        d = 1 + 2 * i
        return copy(gsend.at[d, half(h)], grecv.at[i, half(h)], g_s.at[0], g_r.at[i, h],
                    znext(d))

    g_far(0).start()
    g_far(1).start()
    g_copy(0, 1).start()
    g_copy(1, 0).start()


    stats_finish(0)
    far_finish()


    def tgt_copy(n):
        return copy(tgt.at[n], tgt_in.at[n], tgt_s.at[n], tgt_r.at[n], partner)

    def own_targets(h, n):
        rows = pl.ds(pl.multiple_of(h * HALF + n * 48, 16), 48)
        acc = None
        for v in range(4):
            term = pt[v, rows] * rowfac[0, rows, v : v + 1] + qt[v, rows] * colfac[0, v : v + 1, :]
            acc = term if acc is None else acc + term
        return acc

    for n in range(NCH):
        tgt[n] = own_targets(1 - yh, n)
        start(tgt_copy(n))
    acc = dot(w[0], is_[0], TN)
    for v in range(1, 4):
        acc = acc + dot(w[v], is_[v], TN)
    gtp[...] = acc
    for n in range(NCH):
        tgt_mine[n] = own_targets(yh, n)

    for d in (1, 3, 2):
        iz_wait(d)
    for g in range(4):
        isum8[g] = isum_in[g] + isum[yh, g]
    for g in range(4):
        t = isum8[g]
        hi[:, g * 128 : (g + 1) * 128] = t.astype(BF16)
        lo[:, g * 128 : (g + 1) * 128] = (t - t.astype(BF16).astype(F32)).astype(BF16)
    for i in range(2):
        g_far(i).wait_recv()
        rows = slice(i * HALF, (i + 1) * HALF)
        gsend[1 + 2 * i, rows] = gsend[1 + 2 * i, rows] + gfar_in[i]
        g_copy(i, i).start()
    sent_in_all(gsend.at[1:4], g_s.at[0], g_r.at[0, 0])

    for n in range(NCH):
        tgt_copy(n).wait_recv()
        tw[n * 48 : (n + 1) * 48] = ((tgt_mine[n] + tgt_in[n]) * 0.125).astype(BF16)
    res = gtp[...] - dot(tw[...], hi[...], TN) - dot(tw[...], lo[...], TN)
    for s in range(8):
        row = s * HALF
        for g in range(4):
            gtc[s % 2, s // 2, g] = res[row : row + HALF, g * 128 : (g + 1) * 128]
    def gc_copy(i):
        rows = slice(i * 72, (i + 1) * 72)
        return copy(gtc.at[1 - k, :, :, rows, :], gt_sib.at[:, :, rows, :], gc_s.at[i],
                    gc_r.at[i], sib)

    start(gc_copy(0))
    start(gc_copy(1))

    target_text = dot(tw[...], ts[...], NN)
    for g in range(4):
        tt_part[g] = target_text[:, g * 128 : (g + 1) * 128]

    def tz_copy(d):
        return copy(tt_part.at[lax.rem(z + d, 4)], tt_in.at[d - 1], tz_s.at[0],
                    tz_r.at[0], znext(d))

    start_group([tz_copy(d) for d in (2, 1, 3)], tt_in, tz_s.at[0], tz_r.at[0])

    target_loss = isum8[0] * tt_part[0]
    for g in range(1, 4):
        target_loss = target_loss + isum8[g] * tt_part[g]
    target_loss = jnp.sum(jnp.sum(target_loss, axis=0, keepdims=True), axis=1, keepdims=True)
    part = lse_part - target_loss * student_scale
    loss_src[...] = jnp.broadcast_to(part, (8, 128))

    def lb_copy(d):
        return copy(loss_src, loss_b.at[d - 1], lb_s.at[0], lb_r.at[0],
                    (lax.rem(b + d, 16), a))

    start_all(1, 16, lb_copy, loss_b, lb_s.at[0], lb_r.at[0])

    y = yh * 2 + yl
    pieces = gtc.at[k]

    def ydev(d):
        yd = lax.rem(y + d, 4)
        return dev(x, (yd % 2) * 2 + k, yd // 2, z)

    def xdev(d):
        return dev(lax.rem(x + d, 4), j, yh, z)

    def ra_copy(d):
        return copy(pieces.at[lax.rem(x + d, 4), :, 0:72, :], ra_in.at[d - 1],
                    rs_s.at[0], rs_r.at[0], xdev(d))

    def rb_copy(d):
        return copy(pieces.at[:, lax.rem(y + d, 4), 72:144, :], rb_in.at[d - 1],
                    rs_s.at[1], rs_r.at[1], ydev(d))

    def ra2_copy(d):
        return copy(ra_sum.at[lax.rem(y + d, 4)], ra2_in.at[d - 1],
                    rs_s.at[2], rs_r.at[2], ydev(d))

    def rb2_copy(d):
        return copy(rb_sum.at[lax.rem(x + d, 4)], rb2_in.at[d - 1],
                    rs_s.at[3], rs_r.at[3], xdev(d))

    for i in range(2):
        gc_copy(i).wait_recv()
        rows = slice(i * 72, (i + 1) * 72)
        for blk in range(4):
            for g in range(4):
                gtc[k, blk, g, rows, :] = gtc[k, blk, g, rows, :] + gt_sib[blk, g, rows, :]
        if i == 0:
            start_group([ra_copy(d) for d in (1, 3, 2)], ra_in, rs_s.at[0], rs_r.at[0])
        else:
            start_group([rb_copy(d) for d in (1, 3)], rb_in, rs_s.at[1], rs_r.at[1])

    total = tt_part[z]
    take_group(tt_in, tz_s.at[0], tz_r.at[0])
    for d in (1, 3, 2):
        total = total + tt_in[d - 1]
    tt_src[...] = total

    a_in = (1 - yh) * 4 + z
    ty = copy(tt_src, tt_all.at[a], ta_s.at[0], ta_r.at[a], partner)
    ty.start()
    rb_copy(2).start()

    def ta_copy(d):
        return copy(tt_src, tt_all.at[a], ta_s.at[0], ta_r.at[a], znext(d))

    def tb_copy(d):
        return copy(tt_all.at[a_in], tt_all.at[a_in], ta_s.at[0], ta_r.at[a_in], znext(d))

    def t_wait(slot):
        copy(tt_src, tt_all.at[slot], ta_s.at[0], ta_r.at[slot], partner).wait_recv()

    for d in (1, 3, 2):
        ta_copy(d).start()
    tt_all[a] = total

    take_group(loss_b, lb_s.at[0], lb_r.at[0])

    def lb_wait(d, acc):
        return acc + loss_b[d - 1]

    loss_src2[...] = lax.fori_loop(1, 16, lb_wait, loss_src[...])

    def la_copy(d):
        return copy(loss_src2, loss_a.at[d - 1], la_s.at[0], la_r.at[0],
                    (b, lax.rem(a + d, 8)))

    start_all(1, 8, la_copy, loss_a, la_s.at[0], la_r.at[0])

    ra_sum[...] = gtc[k, x, :, 0:72, :]
    rb_sum[...] = gtc[k, :, y, 72:144, :]
    take_group(ra_in, rs_s.at[0], rs_r.at[0])
    for d in (1, 3, 2):
        ra_sum[...] = ra_sum[...] + ra_in[d - 1]
    start_group([ra2_copy(d) for d in (1, 3, 2)], ra2_in, rs_s.at[2], rs_r.at[2])
    take_group(rb_in, rs_s.at[1], rs_r.at[1])
    for d in (1, 3, 2):
        rb_sum[...] = rb_sum[...] + rb_in[d - 1]
    start_group([rb2_copy(d) for d in (1, 3, 2)], rb2_in, rs_s.at[3], rs_r.at[3])
    t_wait(a_in)
    for d in (1, 3, 2):
        tb_copy(d).start()
    sent_in_all(tt_all.at[0:7], ta_s.at[0], ta_r.at[0])
    def fz_copy(c, i, d):
        ref = fb_src.at[c, i * 72 : (i + 1) * 72]
        return copy(ref, ref, fz_s.at[0], fz_r.at[i, d - 1], znext(d))

    first = ra_sum[y]
    take_group(ra2_in, rs_s.at[2], rs_r.at[2])
    for d in (1, 3, 2):
        first = first + ra2_in[d - 1]
    fb_src[z, 0:72, :] = first
    for d in (1, 3, 2):
        fz_copy(z, 0, d).start()
    last = rb_sum[x]
    take_group(rb2_in, rs_s.at[3], rs_r.at[3])
    for d in (1, 3, 2):
        last = last + rb2_in[d - 1]
    fb_src[z, 72:144, :] = last
    for d in (1, 3, 2):
        fz_copy(z, 1, d).start()
    sent_in_all(fb_src.at[0:3], fz_s.at[0], fz_r.at[0, 0])

    def fb_copy(c, h):
        return copy(fb_src.at[c], fb_buf.at[j * 2 + yh], fb_s.at[0], fb_r.at[j * 2 + yh],
                    dev(x, c, h, z))

    def is_self(c, h):
        return (j == c) & (yh == h)

    def fb_send(c):
        for h in range(2):
            @pl.when(jnp.logical_not(is_self(c, h)))
            def _():
                fb_copy(c, h).start()

    sent_in_all(fb_buf.at[0:7], fb_s.at[0], fb_r.at[0])
    fb_send(z)
    for d in (1, 3, 2):
        c = lax.rem(z + 4 - d, 4)
        fz_copy(c, 0, d).wait_recv()
        fz_copy(c, 1, d).wait_recv()
        fb_send(c)
    fb_buf[j * 2 + yh] = fb_src[j]

    acc = gsend[0]
    for i in range(2):
        g_copy(i, 0).wait_recv()
        g_copy(i, 1).wait_recv()
        acc = acc + grecv[i]

    for d in (1, 3, 2):
        zd = lax.rem(z + d, 4)
        t_wait(yh * 4 + zd)
        t_wait((1 - yh) * 4 + zd)
    for h in range(2):
        rows = slice(h * HALF, (h + 1) * HALF)
        for g in range(4):
            lanes = slice(g * 128, (g + 1) * 128)
            grads_out[0, rows, lanes] = acc[rows, lanes] - tt_all[h * 4 + g]

    take_group(loss_a, la_s.at[0], la_r.at[0])

    def la_wait(d, acc):
        return acc + loss_a[d - 1]

    whole = lax.fori_loop(1, 8, la_wait, loss_src2[...])
    loss_out[0, 0] = jnp.sum(whole[0:1, 0:1]) * (1.0 / (2.0 * 8 * 4608))

    def fb_wait(s, _):
        @pl.when(s != j * 2 + yh)
        def _():
            copy(fb_src.at[0], fb_buf.at[s], fb_s.at[0], fb_r.at[s], partner).wait_recv()

        return 0

    lax.fori_loop(0, 8, fb_wait, 0)
    for s in range(8):
        syl_, sk_, syh_ = s // 4, (s // 2) % 2, s % 2
        g = syh_ * 2 + syl_
        grads_out[1, sk_ * HALF : (sk_ + 1) * HALF, g * 128 : (g + 1) * 128] = fb_buf[s]

    for gone in sent:
        gone()


def per_device(student_image, student_text, teacher_image, teacher_text):
    vm = pl.BlockSpec(memory_space=pltpu.VMEM)
    dma = pltpu.SemaphoreType.DMA
    V = pltpu.VMEM
    sw, twd = student_image.shape[2], teacher_image.shape[2]
    loss, grads = pl.pallas_call(
        kernel,
        name="distill",
        out_shape=(
            jax.ShapeDtypeStruct((1, 1), F32),
            pltpu.VMEM((2, ROWS, sw), F32),
        ),
        in_specs=[pl.BlockSpec(memory_space=pl.ANY)] * 4,
        out_specs=(pl.BlockSpec(memory_space=pltpu.SMEM), vm),
        scratch_shapes=[
            V((4, ROWS, twd), BF16), V((4, ROWS, sw), BF16),
            V((4 * ROWS, twd), BF16), V((4 * ROWS, sw), BF16),
            V((4, ROWS, COLS), F32), V((4, ROWS, COLS), F32),
            V((4, ROWS, COLS), F32), V((4, ROWS, COLS), F32),
            V((4, ROWS, COLS), BF16),
            V((NCH, 48, COLS), F32), V((NCH, 48, COLS), F32), V((NCH, 48, COLS), F32),
            V((HALF, COLS), BF16),
            V((2, 4, HALF, 128), F32), V((4, HALF, 128), F32), V((4, HALF, 128), F32),
            V((HALF, sw), BF16), V((HALF, sw), BF16),
            V((4, HALF, 128), F32), V((3, HALF, 128), F32), V((HALF, 128), F32),
            V((8, HALF, 128), F32),
            V((4, ROWS, sw), F32), V((2, ROWS, sw), F32), V((2, HALF, sw), F32),
            V((COLS, sw), F32), V((4, 4, HALF, 128), F32),
            V((3, 4, 72, 128), F32), V((3, 4, 72, 128), F32), V((4, 72, 128), F32),
            V((4, 72, 128), F32), V((3, 72, 128), F32), V((3, 72, 128), F32),
            V((4, HALF, 128), F32), V((8, HALF, 128), F32),
            V((2, 4, 4, HALF, 128), F32),
            V((384, 128), F32), V((2, 8, 384), F32), V((2, 3, 8, 384), F32),
            V((2, 384, 128), F32), V((128, 384), F32),
            V((2, 8, COLS), F32), V((2, 3, 8, COLS), F32), V((2, 8, COLS), F32),
            V((2, 3, 8, COLS), F32), V((2, 8, COLS), F32),
            V((2, COLS), F32), V((15, 2, COLS), F32),
            V((8, 128), F32), V((15, 8, 128), F32), V((8, 128), F32), V((7, 8, 128), F32),
            dma((4,)), dma((2,)), dma((2, 3, 2)),
            dma((2, 3)), dma((2,)), dma((2, 3)), dma((2, 3)), dma((2,)), dma((2, 4)),
            dma((2, 2)), dma((2, 2)), dma((3,)), dma((3,)),
            dma((1,)), dma((1,)), dma((3,)), dma((3,)), dma((1,)), dma((1,)), dma((1,)), dma((8,)),
            dma((1,)), dma((1,)), dma((2,)), dma((2,)), dma((2,)), dma((2,)), dma((2,)), dma((2,)),
            dma((3,)), dma((3,)), dma((1,)), dma((3, 2)), dma((2,)), dma((2,)),
            dma((4,)), dma((4,)), dma((1,)), dma((2, 3)), dma((1,)), dma((8,)),
            dma((1,)), dma((1,)), dma((1,)), dma((1,)),
        ],
        compiler_params=pltpu.CompilerParams(
            collective_id=0, has_side_effects=True, vmem_limit_bytes=58 * 1024 * 1024
        ),
        cost_estimate=pl.CostEstimate(
            flops=8 * 10**9, bytes_accessed=4 * 2**20, transcendentals=6 * 10**6
        ),
    )(student_image[0], student_text, teacher_image[0], teacher_text)
    scale = 3.0 / math.sqrt(sw)
    return loss.reshape(()), (grads[0] * scale)[None], grads[1] * scale


def solution(mesh):
    return jax.shard_map(
        per_device,
        mesh=mesh,
        in_specs=(
            P("aug", "batch", None),
            P("batch", None),
            P("aug", "batch", None),
            P("batch", None),
        ),
        out_specs=(P(), P("aug", "batch", None), P("batch", None)),
        check_vma=False,
    )
```
